32 devices in a mesh: dp: 8 (over z, x), tensor: 4 (over y, core).
Axes of the slice: x: 2, y: 2, z: 4, core: 2. Of those that a mesh axis runs over, the one named last changes fastest.
Arguments:
- inputs: bfloat16 [16384, 768], P(('dp', 'tensor')), may hold values from -6 to 6
- lengths: int32 [32], P('dp'), may hold values from 20 to 512, as said below
- weight_query: bfloat16 [768, 768], P(None, 'tensor'), may hold values from -0.21875 to 0.21875
- bias_query: bfloat16 [768], P('tensor'), may hold values from -3 to 3
- weight_key: bfloat16 [768, 768], P(None, 'tensor'), may hold values from -0.21875 to 0.21875
- weight_value: bfloat16 [768, 768], P(None, 'tensor'), may hold values from -0.21875 to 0.21875
- bias_value: bfloat16 [768], P('tensor'), may hold values from -3 to 3
- weight_out: bfloat16 [768, 768], P('tensor'), may hold values from -1.75 to 1.75
- bias_out: bfloat16 [768], replicated, may hold values from -2 to 2
- weight_in: bfloat16 [768, 3072], P(None, 'tensor'), may hold values from -0.21875 to 0.21875
- bias_in: bfloat16 [3072], P('tensor'), may hold values from -2 to 2
- weight_down: bfloat16 [3072, 768], P('tensor'), may hold values from -0.109375 to 0.109375
- bias_down: bfloat16 [768], replicated, may hold values from -2 to 2
- first_gain: bfloat16 [768], replicated, may hold values from 0.5 to 1.5
- first_shift: bfloat16 [768], replicated, may hold values from -2 to 2
- second_gain: bfloat16 [768], replicated, may hold values from 0.5 to 1.5
- second_shift: bfloat16 [768], replicated, may hold values from -2 to 2
- cotangent: bfloat16 [16384, 768], P(('dp', 'tensor')), may hold values from -6 to 6
Outputs:
- outputs: bfloat16 [16384, 768], P(('dp', 'tensor'))
- grad_inputs: float32 [16384, 768], P(('dp', 'tensor'))
- grad_weight_query: float32 [768, 768], P(None, 'tensor')
- grad_bias_query: float32 [768], P('tensor')
- grad_weight_key: float32 [768, 768], P(None, 'tensor')
- grad_weight_value: float32 [768, 768], P(None, 'tensor')
- grad_bias_value: float32 [768], P('tensor')
- grad_weight_out: float32 [768, 768], P('tensor')
- grad_bias_out: float32 [768], replicated
- grad_weight_in: float32 [768, 3072], P(None, 'tensor')
- grad_bias_in: float32 [3072], P('tensor')
- grad_weight_down: float32 [3072, 768], P('tensor')
- grad_bias_down: float32 [768], replicated
- grad_first_gain: float32 [768], replicated
- grad_first_shift: float32 [768], replicated
- grad_second_gain: float32 [768], replicated
- grad_second_shift: float32 [768], replicated
The draws below stay inside these ranges and needn't reach their ends.
Inputs may be any that keep to these rules, and one draw needn't show every extreme that they name: `lengths`: some passage has 512 tokens and some has 20.
All inputs are finite; a program needn't handle non-finite values.
Results may differ from the reference program's by a relative error of at most 0.017.
Values may be sent and summed in bfloat16 or wider, within the bound.
No kernel may reach another device: no remote copies, remote signals or barrier semaphores. Data moves between devices by JAX's collectives and lax.ppermute only.
A program may use at most 128 MiB of HBM per device.

```python
import math
import jax
import jax.numpy as jnp
from jax import lax

D = 768
HEADS = 12
HEAD = 64
FF = 3072
SEQ_LEN = 512
MIN_LEN = 20
SEQS = 32
TOKENS = 16384


def draw_lengths(key, part):
    key = jax.random.fold_in(key, 11)
    first_key, second_key, third_key = jax.random.split(key, 3)
    first_draw = jax.random.randint(first_key, (SEQS,), MIN_LEN, SEQ_LEN + 1)
    second_draw = jax.random.randint(second_key, (SEQS,), MIN_LEN, SEQ_LEN + 1)
    drawn = jnp.maximum(first_draw, second_draw)
    order = jax.random.permutation(third_key, SEQS)
    drawn = drawn.at[order[0]].set(SEQ_LEN)
    drawn = drawn.at[order[1]].set(MIN_LEN)
    return drawn.astype(jnp.int32)


def draw_cotangent(key, part):
    key = jax.random.fold_in(key, 23)
    first_key = jax.random.fold_in(key, 0)
    position = jnp.arange(TOKENS, dtype=jnp.float32) / TOKENS
    rising = (0.5 + position)[:, None]
    base = jnp.clip(jax.random.normal(first_key, (TOKENS, D), jnp.float32), -4.0, 4.0)
    return (base * rising).astype(jnp.bfloat16)


def levels(rng, dims, cuts, low, top_value):
    loudness = 1.0
    for dim, shards_of in cuts:
        draws = jax.random.uniform(jax.random.fold_in(jax.random.fold_in(rng, 6), dim), (shards_of,), jnp.float32, low / len(cuts), top_value / len(cuts))
        loudness = loudness * jnp.repeat(jnp.exp(draws), dims[dim] // shards_of).reshape((-1,) + (1,) * (len(dims) - 1 - dim))
    return loudness


def scatter_about(key, extent, width, limit, cuts=(), held_as=jnp.bfloat16):
    values = width * jax.random.normal(key, extent, jnp.float32)
    if cuts:
        values = values * levels(key, extent, cuts, -0.22, 0.18)
    return jnp.clip(values, -limit, limit).astype(held_as)


def setup_inputs(seed: int = 0) -> dict:
    keys = jax.random.split(jax.random.key(seed), 19)
    return {
        "inputs": scatter_about(keys[0], (TOKENS, D), 1.0, 6.0, ((0, 32),)),
        "lengths": draw_lengths(jax.random.fold_in(keys[18], 71), 0),
        "weight_query": scatter_about(keys[2], (D, D), D ** -0.5, 0.21875, ((1, 4),)),
        "bias_query": scatter_about(keys[3], (D,), 0.5, 3.0, ((0, 4),)),
        "weight_key": scatter_about(keys[4], (D, D), D ** -0.5, 0.21875, ((1, 4),)),
        "weight_value": scatter_about(keys[5], (D, D), D ** -0.5, 0.21875, ((1, 4),)),
        "bias_value": scatter_about(keys[6], (D,), 0.5, 3.0, ((0, 4),)),
        "weight_out": scatter_about(keys[7], (D, D), (max(D // 64, 4)) ** -0.5, 1.75, ((0, 4),)),
        "bias_out": scatter_about(keys[8], (D,), 0.3, 2.0),
        "weight_in": scatter_about(keys[9], (D, FF), D ** -0.5, 0.21875, ((1, 4),)),
        "bias_in": scatter_about(keys[10], (FF,), 0.3, 2.0, ((0, 4),)),
        "weight_down": scatter_about(keys[11], (FF, D), FF ** -0.5, 0.109375, ((0, 4),)),
        "bias_down": scatter_about(keys[12], (D,), 0.3, 2.0),
        "first_gain": jnp.clip(1.0 + 0.1 * jax.random.normal(keys[13], (D,), jnp.float32), 0.5, 1.5).astype(jnp.bfloat16),
        "first_shift": scatter_about(keys[14], (D,), 0.3, 2.0),
        "second_gain": jnp.clip(1.0 + 0.1 * jax.random.normal(keys[15], (D,), jnp.float32), 0.5, 1.5).astype(jnp.bfloat16),
        "second_shift": scatter_about(keys[16], (D,), 0.3, 2.0),
        "cotangent": draw_cotangent(jax.random.fold_in(keys[18], 71), 0),
    }


@jax.custom_vjp
def low(v):
    return lax.optimization_barrier(v.astype(jnp.bfloat16)).astype(jnp.float32)

@jax.custom_vjp
def low_back(v):
    return v

def low_keep(v):
    return (low(v), None)

def low_pass(kept, grad):
    return (grad,)

def back_keep(v):
    return (v, None)

def back_low(kept, grad):
    return (low(grad),)
low.defvjp(low_keep, low_pass)
low_back.defvjp(back_keep, back_low)

def product(left, right):
    return jnp.dot(left, right, precision=lax.Precision.HIGHEST)

def layer_norm(values, gain, shift):
    center = values - lax.optimization_barrier(jnp.mean(values, axis=-1, keepdims=True))
    spread = lax.optimization_barrier(jnp.mean(center * center, axis=-1, keepdims=True))
    return center * lax.rsqrt(spread + 1e-12) * gain + shift

def forward(inputs, lengths, params):
    weight_query, bias_query, weight_key, weight_value, bias_value, weight_out, bias_out, weight_in, bias_in, weight_down, bias_down, first_gain, first_shift, second_gain, second_shift = params
    sequences = lengths.shape[0]
    lowered = low(inputs)
    queries = low(low_back(product(lowered, weight_query)) + bias_query)
    keys_all = low(low_back(product(lowered, weight_key)))
    values_all = low(low_back(product(lowered, weight_value)) + bias_value)
    layout = (sequences, SEQ_LEN, HEADS, HEAD)
    scores = jnp.einsum('sqhd,skhd->shqk', queries.reshape(layout), keys_all.reshape(layout), precision=lax.Precision.HIGHEST) / math.sqrt(HEAD)
    visible = jnp.arange(SEQ_LEN, dtype=jnp.int32)[None, :] < lengths[:, None].astype(jnp.int32)
    scores = low_back(jnp.where(visible[:, None, None, :], scores, -1e+30))
    attention = jax.nn.softmax(scores, axis=-1)
    mixed = jnp.einsum('shqk,skhd->sqhd', low(attention), values_all.reshape(layout), precision=lax.Precision.HIGHEST)
    attended = low(low_back(mixed.reshape(inputs.shape)))
    branch = low_back(product(attended, weight_out)) + bias_out
    normed = layer_norm(inputs + branch, first_gain, first_shift)
    lifted = low_back(product(low(normed), weight_in)) + bias_in
    activated = low(jax.nn.gelu(lifted, approximate=False))
    feed = low_back(product(activated, weight_down)) + bias_down
    return layer_norm(normed + feed, second_gain, second_shift)

def reference(inputs, lengths, weight_query, bias_query, weight_key, weight_value, bias_value, weight_out, bias_out, weight_in, bias_in, weight_down, bias_down, first_gain, first_shift, second_gain, second_shift, cotangent):
    params = tuple((element.astype(jnp.float32) for element in (weight_query, bias_query, weight_key, weight_value, bias_value, weight_out, bias_out, weight_in, bias_in, weight_down, bias_down, first_gain, first_shift, second_gain, second_shift)))
    group_size = math.gcd(SEQS, max(1, 4096 // SEQ_LEN))
    block_count = SEQS // group_size
    row_count = group_size * SEQ_LEN
    stacked_inputs = inputs.astype(jnp.float32).reshape(block_count, row_count, D)
    stacked_lengths = lengths.reshape(block_count, group_size)
    stacked_cotangent = cotangent.astype(jnp.float32).reshape(block_count, row_count, D)

    def advance(totals, pieces):
        part_inputs, part_lengths, part_cotangent = pieces
        results, pullback = jax.vjp(lambda inputs_part, params_part: forward(inputs_part, part_lengths, params_part), part_inputs, params)
        grad_part, grad_params = pullback(part_cotangent)
        totals = jax.tree.map(lambda total_one, grad_one: total_one + grad_one, totals, grad_params)
        return (totals, (results, grad_part))
    initial = jax.tree.map(jnp.zeros_like, params)
    totals, (results, grad_rows) = lax.scan(advance, initial, (stacked_inputs, stacked_lengths, stacked_cotangent))
    return (results.reshape(TOKENS, D).astype(jnp.bfloat16), grad_rows.reshape(TOKENS, D), totals[0], totals[1], totals[2], totals[3], totals[4], totals[5], totals[6], totals[7], totals[8], totals[9], totals[10], totals[11], totals[12], totals[13], totals[14])
```

```python
import functools
import math

import jax
import jax.numpy as jnp
from jax import lax
from jax.experimental import pallas as pl
from jax.experimental.pallas import tpu as pltpu
from jax.sharding import PartitionSpec as P

HEAD = 64
SEQ_LEN = 512
EXTRA = 32
F32 = jnp.float32
BF16 = jnp.bfloat16
VMEM_LIMIT = 16 * 1024 * 1024


def dot(left, right, left_dim, right_dim):
    return lax.dot_general(
        left, right, (((left_dim,), (right_dim,)), ((), ())), preferred_element_type=F32
    )


def params(**kwargs):
    return pltpu.CompilerParams(vmem_limit_bytes=VMEM_LIMIT, **kwargs)


def cost(flops, moved, transcendentals=0):
    return pl.CostEstimate(
        flops=int(flops), bytes_accessed=int(moved), transcendentals=int(transcendentals)
    )


def whole(shape, index=None):
    place = index or (0,) * len(shape)
    return pl.BlockSpec(shape, lambda *_: place)


def parity_slice(parity, part, size, tile):
    place = lax.rem(parity + part, 2) * size
    return pl.ds(pl.multiple_of(place, tile), size)


def prepare_pack_kernel(place_ref, q_ref, k_ref, v_ref, out_ref, bq_ref, bv_ref, bin_ref, *refs):
    mine_ref, other_ref, held_ref, extra_ref = refs
    width = out_ref.shape[0]
    for i, ref in enumerate((q_ref, k_ref, v_ref)):
        held_ref[i * width : (i + 1) * width, :] = jnp.transpose(ref[...])
    held_ref[3 * width : 4 * width, :] = out_ref[...]
    extra_ref[...] = jnp.zeros_like(extra_ref)
    extra_ref[0:1, :width] = bq_ref[...].astype(F32)
    extra_ref[0:1, 2 * width : 3 * width] = bv_ref[...].astype(F32)
    extra_ref[1:2, :] = bin_ref[...].astype(F32)
    held_ref[4 * width :, :] = extra_ref[...].astype(BF16)
    half = mine_ref.shape[0]
    mine_ref[...] = held_ref[parity_slice(place_ref[1], 0, half, 16), :]
    other_ref[...] = held_ref[parity_slice(place_ref[1], 1, half, 16), :]


def prepare_pack(place, wq, wk, wv, wout, bq, bv, bin_):
    width, model = wout.shape
    rows = 4 * width + EXTRA
    vmem = pl.BlockSpec(memory_space=pltpu.VMEM)
    half = jax.ShapeDtypeStruct((rows // 2, model), BF16)
    return pl.pallas_call(
        prepare_pack_kernel,
        out_shape=(half, half),
        in_specs=[pl.BlockSpec(memory_space=pltpu.SMEM)] + [vmem] * 7,
        out_specs=(vmem, vmem),
        scratch_shapes=[pltpu.VMEM((rows, model), BF16), pltpu.VMEM((EXTRA, model), F32)],
        compiler_params=params(),
        name="prepare_pack",
    )(place, wq, wk, wv, wout, bq[None], bv[None], bin_[None])


def prepare_feed_kernel(place_ref, win_ref, wd_ref, *refs):
    outs, sems = refs[:4], refs[4]
    half = outs[2].shape[0]
    copies = []
    for part in range(2):
        window = parity_slice(place_ref[1], part, half, 128)
        copies.append(
            pltpu.make_async_copy(win_ref.at[:, window], outs[part], sems.at[part])
        )
        copies.append(
            pltpu.make_async_copy(wd_ref.at[window, :], outs[2 + part], sems.at[2 + part])
        )
    for one in copies:
        one.start()
    for one in copies:
        one.wait()


def prepare_feed(place, win, wd):
    model, hidden = win.shape
    rough = pl.BlockSpec(memory_space=pl.ANY)
    tall = jax.ShapeDtypeStruct((model, hidden // 2), BF16)
    wide = jax.ShapeDtypeStruct((hidden // 2, model), BF16)
    return pl.pallas_call(
        prepare_feed_kernel,
        out_shape=(tall, tall, wide, wide),
        in_specs=[pl.BlockSpec(memory_space=pltpu.SMEM), rough, rough],
        out_specs=(rough,) * 4,
        scratch_shapes=[pltpu.SemaphoreType.DMA((4,))],
        compiler_params=params(),
        name="prepare_feed",
    )(place, win, wd)


def attend_forward_kernel(place_ref, x_ref, mine_ref, other_ref, *refs):
    chained = len(refs) == 8
    if chained:
        acc_ref, *refs = refs
    pack_ref, bin_ref, qkv_ref, e_ref, r_ref, att_ref, branch_ref = refs
    width = att_ref.shape[0]
    heads = width // HEAD
    parity = place_ref[1]
    scale = math.log2(math.e) / math.sqrt(HEAD)
    half, model = mine_ref.shape
    pack_ref[parity_slice(parity, 0, half, 16), :] = mine_ref[...]
    pack_ref[parity_slice(parity, 1, half, 16), :] = other_ref[...]
    extra = slice(4 * width, 4 * width + 16)
    for part in range(2):
        bin_ref[:, part * model // 2 : (part + 1) * model // 2] = pack_ref[
            extra, parity_slice(parity, part, model // 2, 128)
        ]
    bias = jnp.transpose(pack_ref[extra, :].astype(F32))[: 3 * width, 0:1]
    projected = dot(pack_ref[: 3 * width, :], x_ref[...], 1, 1) + bias
    qkv_ref[...] = projected.astype(BF16)
    visible = lax.broadcasted_iota(jnp.int32, (SEQ_LEN, 1), 0) < place_ref[0]
    for h in range(heads):
        rows = slice(h * HEAD, (h + 1) * HEAD)
        q = qkv_ref[h * HEAD : (h + 1) * HEAD, :]
        k = qkv_ref[width + h * HEAD : width + (h + 1) * HEAD, :]
        v = qkv_ref[2 * width + h * HEAD : 2 * width + (h + 1) * HEAD, :]
        scores = jnp.where(visible, dot(k, q, 0, 0) * scale, -1e30)
        highest = jnp.max(scores, axis=0, keepdims=True)
        e = jnp.exp2(scores - highest)
        r = 1.0 / jnp.sum(e, axis=0, keepdims=True)
        low = e.astype(BF16)
        e_ref[h] = low
        r_ref[h : h + 1, :] = r
        att_ref[rows, :] = (dot(v, low, 1, 0) * r).astype(BF16)
    branch = dot(att_ref[...], pack_ref[3 * width : 4 * width, :], 0, 0)
    if chained:
        branch = branch + acc_ref[...]
    branch_ref[...] = branch


def attend_forward(place, x, mine, other, acc=None):
    rows, model = x.shape
    width = model // 4
    heads = width // HEAD
    more = [] if acc is None else [acc]
    vmem = pl.BlockSpec(memory_space=pltpu.VMEM)
    return pl.pallas_call(
        attend_forward_kernel,
        out_shape=(
            jax.ShapeDtypeStruct((2 * mine.shape[0], model), BF16),
            jax.ShapeDtypeStruct((16, model), BF16),
            jax.ShapeDtypeStruct((3 * width, rows), BF16),
            jax.ShapeDtypeStruct((heads, rows, rows), BF16),
            jax.ShapeDtypeStruct((8, rows), F32),
            jax.ShapeDtypeStruct((width, rows), BF16),
            jax.ShapeDtypeStruct((rows, model), F32),
        ),
        in_specs=[pl.BlockSpec(memory_space=pltpu.SMEM)] + [vmem] * (3 + len(more)),
        out_specs=(vmem,) * 7,
        compiler_params=params(),
        cost_estimate=cost(1e6, 1e4),
        name="attend_forward",
    )(place, x, mine, other, *more)


def attend_backward_kernel(place_ref, x_ref, pack_ref, qkv_ref, e_ref, r_ref, att_ref, *refs):
    bg_ref, acc_ref, db_ref, first_ref, second_ref, *refs = refs
    chained = len(refs) == 7
    if chained:
        add_ref, keep_ref, send_ref, dx_ref, g_ref, held_ref, extra_ref = refs
    else:
        both_ref, dx_ref, g_ref, held_ref, extra_ref = refs
    width = att_ref.shape[0]
    heads = width // HEAD
    parity = place_ref[1]
    factor = 1.0 / math.sqrt(HEAD)
    up = dot(pack_ref[3 * width : 4 * width, :], bg_ref[...], 1, 1).astype(BF16).astype(F32)
    for h in range(heads):
        rows = slice(h * HEAD, (h + 1) * HEAD)
        q = qkv_ref[h * HEAD : (h + 1) * HEAD, :]
        k = qkv_ref[width + h * HEAD : width + (h + 1) * HEAD, :]
        v = qkv_ref[2 * width + h * HEAD : 2 * width + (h + 1) * HEAD, :]
        scaled = up[rows, :] * r_ref[h : h + 1, :]
        inner = jnp.sum(att_ref[rows, :].astype(F32) * scaled, axis=0, keepdims=True)
        do = scaled.astype(BF16)
        e = e_ref[h]
        ds = (e.astype(F32) * (dot(v, do, 0, 0) - inner)).astype(BF16)
        g_ref[h * HEAD : (h + 1) * HEAD, :] = (dot(k, ds, 1, 0) * factor).astype(BF16)
        g_ref[width + h * HEAD : width + (h + 1) * HEAD, :] = (dot(q, ds, 1, 1) * factor).astype(
            BF16
        )
        g_ref[2 * width + h * HEAD : 2 * width + (h + 1) * HEAD, :] = dot(do, e, 1, 1).astype(BF16)
    g = g_ref[...]
    half, model = held_ref.shape[0] // 2, held_ref.shape[1]
    held_ref[: 3 * width, :] = dot(g, x_ref[...], 1, 0).astype(BF16)
    held_ref[3 * width : 4 * width, :] = dot(att_ref[...], bg_ref[...], 1, 0).astype(BF16)
    extra_ref[...] = jnp.zeros_like(extra_ref)
    extra_ref[0:1, : 3 * width] = dot(jnp.ones((8, g.shape[1]), BF16), g, 1, 1)[0:1, :]
    for part in range(2):
        extra_ref[1:2, parity_slice(parity, part, model // 2, 128)] = db_ref[
            0:1, part * model // 2 : (part + 1) * model // 2
        ]
    extra_ref[2:5, :] = first_ref[0:3, :]
    extra_ref[5:8, :] = second_ref[0:3, :]
    held_ref[4 * width :, :] = extra_ref[...].astype(BF16)
    for part in range(2):
        value = held_ref[parity_slice(parity, part, half, 16), :]
        if chained:
            value = (value.astype(F32) + add_ref[part].astype(F32)).astype(BF16)
            (keep_ref, send_ref)[part][...] = value
        else:
            both_ref[part] = value
    dx_ref[...] = acc_ref[...] + dot(g, pack_ref[: 3 * width, :], 0, 0)


def attend_backward(place, x, saved, bg, acc, db, first, second, add=None):
    rows, model = x.shape
    width = model // 4
    full = saved[0].shape[0]
    more = [] if add is None else [add]
    vmem = pl.BlockSpec(memory_space=pltpu.VMEM)
    half = jax.ShapeDtypeStruct((full // 2, model), BF16)
    grads = (half, half) if more else (jax.ShapeDtypeStruct((2, full // 2, model), BF16),)
    return pl.pallas_call(
        attend_backward_kernel,
        out_shape=grads + (jax.ShapeDtypeStruct((rows, model), F32),),
        in_specs=[pl.BlockSpec(memory_space=pltpu.SMEM)] + [vmem] * (11 + len(more)),
        out_specs=(vmem,) * (len(grads) + 1),
        scratch_shapes=[
            pltpu.VMEM((3 * width, rows), BF16),
            pltpu.VMEM((full, model), BF16),
            pltpu.VMEM((EXTRA, model), F32),
        ],
        compiler_params=params(),
        cost_estimate=cost(1e6, 1e4),
        name="attend_backward",
    )(place, x, *saved, bg, acc, db, first, second, *more)


def first_norm_kernel(x_ref, branch_ref, vec_ref, z_ref, low_ref, turned_ref, rstd_ref):
    total = x_ref[...].astype(F32) + branch_ref[...] + vec_ref[0:1, :]
    center = total - jnp.mean(total, axis=1, keepdims=True)
    rstd = lax.rsqrt(jnp.mean(center * center, axis=1, keepdims=True) + 1e-12)
    z = center * rstd
    z_ref[...] = z
    rstd_ref[...] = rstd
    normed = (z * vec_ref[1:2, :] + vec_ref[2:3, :]).astype(BF16)
    low_ref[...] = normed
    turned_ref[...] = jnp.transpose(normed)


def first_norm(x, branch, vec):
    rows, model = x.shape
    step = rows // 4
    block = pl.BlockSpec((step, model), lambda i: (i, 0))
    return pl.pallas_call(
        first_norm_kernel,
        grid=(4,),
        out_shape=(
            jax.ShapeDtypeStruct((rows, model), F32),
            jax.ShapeDtypeStruct((rows, model), BF16),
            jax.ShapeDtypeStruct((model, rows), BF16),
            jax.ShapeDtypeStruct((rows, 1), F32),
        ),
        in_specs=[block, block, whole(vec.shape)],
        out_specs=(
            block,
            block,
            pl.BlockSpec((model, step), lambda i: (0, i)),
            pl.BlockSpec((step, 1), lambda i: (i, 0)),
        ),
        compiler_params=params(),
        cost_estimate=cost(20 * rows * model, 7e6),
        name="first_norm",
    )(x, branch, vec)


def second_norm_kernel(z_ref, feed_ref, vec_ref, c_ref, out_ref, grad_ref, low_ref, sum_ref):
    normed = z_ref[...] * vec_ref[1:2, :] + vec_ref[2:3, :]
    total = normed + feed_ref[...] + vec_ref[3:4, :]
    center = total - jnp.mean(total, axis=1, keepdims=True)
    rstd = lax.rsqrt(jnp.mean(center * center, axis=1, keepdims=True) + 1e-12)
    z = center * rstd
    out_ref[...] = (z * vec_ref[4:5, :] + vec_ref[5:6, :]).astype(BF16)
    c = c_ref[...].astype(F32)
    e = c * vec_ref[4:5, :]
    grad = (
        e - jnp.mean(e, axis=1, keepdims=True) - z * jnp.mean(e * z, axis=1, keepdims=True)
    ) * rstd
    grad_ref[...] = grad
    low_ref[...] = grad.astype(BF16)

    @pl.when(pl.program_id(0) == 0)
    def _():
        sum_ref[...] = jnp.zeros_like(sum_ref)

    sum_ref[0:1, :] += jnp.sum(c, axis=0, keepdims=True)
    sum_ref[1:2, :] += jnp.sum(c * z, axis=0, keepdims=True)
    sum_ref[2:3, :] += jnp.sum(grad, axis=0, keepdims=True)


def second_norm(z, feed, vec, c):
    rows, model = z.shape
    step = rows // 4
    block = pl.BlockSpec((step, model), lambda i: (i, 0))
    return pl.pallas_call(
        second_norm_kernel,
        grid=(4,),
        out_shape=(
            jax.ShapeDtypeStruct((rows, model), BF16),
            jax.ShapeDtypeStruct((rows, model), F32),
            jax.ShapeDtypeStruct((rows, model), BF16),
            jax.ShapeDtypeStruct((8, model), F32),
        ),
        in_specs=[block, block, whole(vec.shape), block],
        out_specs=(block, block, block, whole((8, model))),
        compiler_params=params(),
        cost_estimate=cost(40 * rows * model, 8e6),
        name="second_norm",
    )(z, feed, vec, c)


def first_back_kernel(z_ref, rstd_ref, dn_ref, vec_ref, grad_ref, low_ref, sum_ref):
    z = z_ref[...]
    dn = dn_ref[...]
    f = dn * vec_ref[1:2, :]
    grad = (
        f - jnp.mean(f, axis=1, keepdims=True) - z * jnp.mean(f * z, axis=1, keepdims=True)
    ) * rstd_ref[...]
    grad_ref[...] = grad
    low_ref[...] = grad.astype(BF16)

    @pl.when(pl.program_id(0) == 0)
    def _():
        sum_ref[...] = jnp.zeros_like(sum_ref)

    sum_ref[0:1, :] += jnp.sum(dn, axis=0, keepdims=True)
    sum_ref[1:2, :] += jnp.sum(dn * z, axis=0, keepdims=True)
    sum_ref[2:3, :] += jnp.sum(grad, axis=0, keepdims=True)


def first_back(z, rstd, dn, vec):
    rows, model = z.shape
    step = rows // 4
    block = pl.BlockSpec((step, model), lambda i: (i, 0))
    return pl.pallas_call(
        first_back_kernel,
        grid=(4,),
        out_shape=(
            jax.ShapeDtypeStruct((rows, model), F32),
            jax.ShapeDtypeStruct((rows, model), BF16),
            jax.ShapeDtypeStruct((8, model), F32),
        ),
        in_specs=[block, pl.BlockSpec((step, 1), lambda i: (i, 0)), block, whole(vec.shape)],
        out_specs=(block, block, whole((8, model))),
        compiler_params=params(),
        cost_estimate=cost(30 * rows * model, 6e6),
        name="first_back",
    )(z, rstd, dn, vec)


def feed_forward_kernel(halves, low_ref, win_a, win_b, wd_a, wd_b, bin_a, bin_b, *refs):
    chained = len(refs) == 6
    if chained:
        acc_ref, *refs = refs
    feed_ref = refs[4]
    size = win_a.shape[1]
    total = acc_ref[...] if chained else None
    for i, (win_ref, wd_ref, bin_ref) in enumerate(((win_a, wd_a, bin_a), (win_b, wd_b, bin_b))):
        act_ref, slope_ref = refs[i], refs[2 + i]
        bias = bin_ref[1:2, halves[i] * size : (halves[i] + 1) * size].astype(F32)
        lifted = dot(low_ref[...], win_ref[...], 1, 0) + bias
        phi_big = 0.5 + 0.5 * lax.erf(lifted * math.sqrt(0.5))
        phi = jnp.exp(-0.5 * lifted * lifted) * (1.0 / math.sqrt(2.0 * math.pi))
        act = (lifted * phi_big).astype(BF16)
        act_ref[...] = act
        slope_ref[...] = (phi_big + lifted * phi).astype(BF16)
        part = dot(act, wd_ref[...], 1, 0)
        total = part if total is None else total + part
    feed_ref[...] = total


def feed_forward(low, units, acc=None):
    rows, model = low.shape
    (win_a, wd_a, bin_a, half_a), (win_b, wd_b, bin_b, half_b) = units
    size = win_a.shape[1]
    more = [] if acc is None else [acc]
    vmem = pl.BlockSpec(memory_space=pltpu.VMEM)
    thin = jax.ShapeDtypeStruct((rows, size), BF16)
    return pl.pallas_call(
        functools.partial(feed_forward_kernel, (half_a, half_b)),
        out_shape=(thin,) * 4 + (jax.ShapeDtypeStruct((rows, model), F32),),
        in_specs=[vmem] * (7 + len(more)),
        out_specs=(vmem,) * 5,
        compiler_params=params(),
        cost_estimate=cost(1e6, 1e4),
        name="feed_forward",
    )(low, win_a, win_b, wd_a, wd_b, bin_a, bin_b, *more)


def down_back_kernel(act_a, act_b, low_ref, *refs):
    for part, act_ref in enumerate((act_a, act_b)):
        grad = dot(act_ref[...], low_ref[...], 0, 0)
        if len(refs) == 1:
            refs[0][part] = grad.astype(BF16)
        else:
            refs[1 + part][...] = (grad + refs[0][part].astype(F32)).astype(BF16)


def down_back(acts, low, add=None):
    rows, model = low.shape
    size = acts[0].shape[1]
    more = [] if add is None else [add]
    vmem = pl.BlockSpec(memory_space=pltpu.VMEM)
    half = jax.ShapeDtypeStruct((size, model), BF16)
    grads = (half, half) if more else (jax.ShapeDtypeStruct((2, size, model), BF16),)
    return pl.pallas_call(
        down_back_kernel,
        out_shape=grads,
        in_specs=[vmem] * (3 + len(more)),
        out_specs=(vmem,) * len(grads),
        compiler_params=params(),
        cost_estimate=cost(1e6, 1e4),
        name="down_back",
    )(*acts, low, *more)


def feed_back_kernel(low_ref, turned_ref, acc_ref, *refs):
    wds, slopes, wins = refs[0:2], refs[2:4], refs[4:6]
    refs = refs[6:]
    chained = len(refs) == 5
    if chained:
        add_ref, keep_ref, send_ref, dn_ref, db_ref = refs
    else:
        both_ref, dn_ref, db_ref = refs
    size = wins[0].shape[1]
    total = acc_ref[...]
    for part in range(2):
        dl = dot(low_ref[...], wds[part][...], 1, 1) * slopes[part][...].astype(F32)
        db_ref[0:1, part * size : (part + 1) * size] = jnp.sum(dl, axis=0, keepdims=True)
        dl = dl.astype(BF16)
        dwin = dot(turned_ref[...], dl, 1, 0)
        if chained:
            (keep_ref, send_ref)[part][...] = (dwin + add_ref[part].astype(F32)).astype(BF16)
        else:
            both_ref[part] = dwin.astype(BF16)
        total = total + dot(dl, wins[part][...], 1, 1)
    dn_ref[...] = total


def feed_back(low, turned, wds, slopes, wins, acc, add=None):
    rows, model = low.shape
    size = wins[0].shape[1]
    more = [] if add is None else [add]
    vmem = pl.BlockSpec(memory_space=pltpu.VMEM)
    half = jax.ShapeDtypeStruct((model, size), BF16)
    grads = (half, half) if more else (jax.ShapeDtypeStruct((2, model, size), BF16),)
    return pl.pallas_call(
        feed_back_kernel,
        out_shape=grads
        + (
            jax.ShapeDtypeStruct((rows, model), F32),
            jax.ShapeDtypeStruct((8, 2 * size), F32),
        ),
        in_specs=[vmem] * (9 + len(more)),
        out_specs=(vmem,) * (len(grads) + 2),
        compiler_params=params(),
        cost_estimate=cost(1e6, 1e4),
        name="feed_back",
    )(low, turned, acc, *wds, *slopes, *wins, *more)


def after(value, *others):
    return lax.optimization_barrier((value, *others))[0]


def swap(value, axis, size, bit):
    return lax.ppermute(value, axis, [(i, i ^ bit) for i in range(size)])


def add(*values):
    total = values[0].astype(F32)
    for one in values[1:]:
        total = total + one.astype(F32)
    return total.astype(BF16)


class Group:
    def __init__(self, dp, tensor):
        self.dp, self.tensor = dp, tensor
        self.spot = lax.axis_index("dp")
        self.parity = lax.rem(self.spot, 2)

    def core(self, value):
        return swap(value, "tensor", self.tensor, 1)

    def across(self, value):
        return swap(value, "tensor", self.tensor, 2)

    def beside(self, value):
        return swap(value, "dp", self.dp, 1)

    def joined(self, mine, other, axis):
        even = self.parity == 0
        return jnp.concatenate(
            [jnp.where(even, mine, other), jnp.where(even, other, mine)], axis=axis
        )

    def hops(self):
        count = self.dp // 2
        half = count // 2
        steps = [[(k, k + 1), (count - 1 - k, count - 2 - k)] for k in range(half - 1)]
        steps.append([(half - 1, half), (half, half - 1)])
        back = [[(k + 1, k), (count - 2 - k, count - 1 - k)] for k in reversed(range(half - 1))]
        return steps, back

    def hop(self, held, pairs):
        return lax.ppermute(
            held, "dp", [(2 * a + b, 2 * c + b) for a, c in pairs for b in range(2)]
        )

    def ends(self, value, moved, pairs):
        place = self.spot // 2
        here = (place == pairs[0][1]) | (place == pairs[1][1])
        return jnp.where(here, moved, value)

    def line_sum(self, value):
        steps, back = self.hops()
        for pairs in steps:
            value = add(value, self.hop(value, pairs))
        for pairs in back:
            value = self.ends(value, self.hop(value, pairs), pairs)
        return value


def local(
    inputs,
    lengths,
    weight_query,
    bias_query,
    weight_key,
    weight_value,
    bias_value,
    weight_out,
    bias_out,
    weight_in,
    bias_in,
    weight_down,
    bias_down,
    first_gain,
    first_shift,
    second_gain,
    second_shift,
    cotangent,
):
    group = Group(lax.axis_size("dp"), lax.axis_size("tensor"))
    spot = lax.axis_index("tensor")
    model = inputs.shape[1]
    width = weight_query.shape[1]
    length = lax.dynamic_index_in_dim(lengths, spot, keepdims=False)
    place = jnp.stack([length, group.parity.astype(jnp.int32)])
    vec = jnp.stack(
        [bias_out, first_gain, first_shift, bias_down, second_gain, second_shift]
        + [jnp.zeros_like(bias_out)] * 2
    ).astype(F32)

    packs = [None] * 4
    wins = [None] * 4
    wds = [None] * 4
    packs[0] = prepare_pack(
        place, weight_query, weight_key, weight_value, weight_out, bias_query, bias_value, bias_in
    )
    packs[1] = [group.core(one) for one in packs[0]]
    pack_far = group.across(packs[0][0])
    win_p, win_q, wd_p, wd_q = prepare_feed(after(place, *packs[0]), weight_in, weight_down)
    wins[0], wds[0] = (win_p, win_q), (wd_p, wd_q)
    win_far = group.across(win_p)
    kept = [None] * 4
    branch = None

    *kept[0], branch = attend_forward(after(place, win_p), inputs, *packs[0], branch)
    wins[1] = [group.core(after(one, branch)) for one in wins[0]]
    *kept[1], branch = attend_forward(place, inputs, *packs[1], branch)
    wds[1] = [group.core(after(one, branch)) for one in wds[0]]
    pack_far = after(pack_far, branch)
    wd_far = group.across(after(wd_p, pack_far))
    packs[2] = (pack_far, group.beside(pack_far))
    packs[3] = [group.core(one) for one in packs[2]]
    *kept[2], branch = attend_forward(place, inputs, *packs[2], branch)
    win_far = after(win_far, packs[2][1])
    wins[2] = (win_far, group.beside(win_far))
    *kept[3], branch = attend_forward(place, inputs, *packs[3], branch)
    z, low, turned, rstd = first_norm(inputs, branch, vec)
    wins[3] = [group.core(after(wins[2][0], low)), group.core(wins[2][1])]
    wd_far = after(wd_far, low)
    wds[2] = (wd_far, group.beside(wd_far))
    wds[3] = [group.core(one) for one in wds[2]]

    acts, slopes = [None] * 4, [None] * 4
    feed = None
    for r in range(2):
        units = [(wins[r][h], wds[r][h], kept[r][1], h) for h in range(2)]
        a0, a1, s0, s1, feed = feed_forward(low, units, feed)
        acts[r], slopes[r] = [a0, a1], [s0, s1]
    acts[2], slopes[2], acts[3], slopes[3] = [[None, None] for _ in range(4)]
    for h in range(2):
        units = [(wins[r][h], wds[r][h], kept[r][1], h) for r in (2, 3)]
        acts[2][h], acts[3][h], slopes[2][h], slopes[3][h], feed = feed_forward(low, units, feed)
    results, grad_second, second_low, second_sums = second_norm(z, feed, vec, cotangent)

    (d3,) = down_back(acts[3], second_low)
    d3 = group.core(d3)
    (d1,) = down_back(acts[1], after(second_low, d3))
    d1 = group.core(d1)
    down_far = down_back(acts[2], second_low, d3)
    down_near = down_back(acts[0], after(second_low, *down_far), d1)
    down_q = group.across(down_far[1])
    down_p = group.across(after(down_far[0], down_far[1]))

    def back(r, low_in, acc, plus=None):
        return feed_back(low_in, turned, wds[r], slopes[r], wins[r], acc, plus)

    db = [None] * 4
    w3, dn, db[3] = back(3, after(second_low, *down_near), grad_second)
    w3 = group.core(w3)
    w1, dn, db[1] = back(1, second_low, dn)
    w1 = group.core(w1)
    *win_far_grad, dn, db[2] = back(2, second_low, dn, w3)
    down_q = add(down_near[1], after(down_q, dn))
    down_x = group.beside(down_q)
    win_gq = group.across(win_far_grad[1])
    win_gp = group.across(win_far_grad[0])
    *win_near, dn, db[0] = back(0, after(second_low, down_q), dn, w1)

    grad_first, first_low, first_sums = first_back(z, rstd, dn, vec)

    def attention_back(r, bg, acc, plus=None):
        return attend_backward(
            place, inputs, [kept[r][0], *kept[r][2:]], bg, acc, db[r], first_sums, second_sums, plus
        )

    p3, dx = attention_back(3, first_low, grad_first)
    p3 = group.core(p3)
    down_keep = add(after(down_near[0], dx), down_p, down_x)
    p1, dx = attention_back(1, after(first_low, down_keep), dx)
    p1 = group.core(p1)
    win_q = add(win_near[1], after(win_gq, dx))
    win_x = group.beside(win_q)
    *pack_far_grad, dx = attention_back(2, after(first_low, win_q), dx, p3)
    pack_gq = group.across(pack_far_grad[1])
    pack_gp = group.across(pack_far_grad[0])
    *pack_near, dx = attention_back(0, first_low, dx, p1)

    down_keep = group.line_sum(down_keep)
    win_keep = group.line_sum(add(win_near[0], win_gp, win_x))
    pack_q = add(pack_near[1], pack_gq)
    pack_keep = group.line_sum(add(pack_near[0], pack_gp, group.beside(pack_q)))
    grad_weight_down = group.joined(down_keep, group.beside(down_keep), 0).astype(F32)
    grad_weight_in = group.joined(win_keep, group.beside(win_keep), 1).astype(F32)
    grad_pack = group.joined(pack_keep, group.beside(pack_keep), 0).astype(F32)
    extra = grad_pack[4 * width :]
    return (
        results,
        dx,
        grad_pack[:width].T,
        extra[0, :width],
        grad_pack[width : 2 * width].T,
        grad_pack[2 * width : 3 * width].T,
        extra[0, 2 * width : 3 * width],
        grad_pack[3 * width : 4 * width],
        extra[4],
        grad_weight_in,
        extra[1],
        grad_weight_down,
        extra[7],
        extra[3],
        extra[2],
        extra[6],
        extra[5],
    )


def solution(mesh):
    in_specs = (
        P(("dp", "tensor"), None),
        P("dp"),
        P(None, "tensor"),
        P("tensor"),
        P(None, "tensor"),
        P(None, "tensor"),
        P("tensor"),
        P("tensor", None),
        P(),
        P(None, "tensor"),
        P("tensor"),
        P("tensor", None),
        P(),
        P(),
        P(),
        P(),
        P(),
        P(("dp", "tensor"), None),
    )
    out_specs = (
        P(("dp", "tensor"), None),
        P(("dp", "tensor"), None),
        P(None, "tensor"),
        P("tensor"),
        P(None, "tensor"),
        P(None, "tensor"),
        P("tensor"),
        P("tensor", None),
        P(),
        P(None, "tensor"),
        P("tensor"),
        P("tensor", None),
        P(),
        P(),
        P(),
        P(),
        P(),
    )
    return jax.shard_map(local, mesh=mesh, in_specs=in_specs, out_specs=out_specs, check_vma=False)
```

```python
import functools
import math

import jax
import jax.numpy as jnp
from jax import lax
from jax.experimental import pallas as pl
from jax.experimental.pallas import tpu as pltpu
from jax.sharding import PartitionSpec as P

HEAD = 64
SEQ_LEN = 512
UP_ROWS = 128
F32 = jnp.float32
BF16 = jnp.bfloat16
VMEM_LIMIT = 24 * 1024 * 1024
VMEM = pl.BlockSpec(memory_space=pltpu.VMEM)
COST = pl.CostEstimate(flops=10**9, bytes_accessed=10**9, transcendentals=0)
MIDDLE = pl.CostEstimate(flops=10**10, bytes_accessed=10**9, transcendentals=0)
LONG = pl.CostEstimate(flops=10**11, bytes_accessed=10**9, transcendentals=0)
SMEM = pl.BlockSpec(memory_space=pltpu.SMEM)
HBM = pl.BlockSpec(memory_space=pltpu.HBM)


def hbm(shape, dtype=BF16):
    return pltpu.HBM(shape, dtype)


def pinned(value):
    return pltpu.with_memory_space_constraint(value, pltpu.HBM)


def dot(left, right, left_dim, right_dim):
    return lax.dot_general(
        left, right, (((left_dim,), (right_dim,)), ((), ())), preferred_element_type=F32
    )


def params(**kwargs):
    return pltpu.CompilerParams(vmem_limit_bytes=VMEM_LIMIT, **kwargs)


def whole(shape, index=None):
    place = index or (0,) * len(shape)
    return pl.BlockSpec(shape, lambda *_: place)


def row(ref):
    return ref[...].astype(F32).reshape(1, ref.shape[0])


def pack_rows(width):
    return (4 * width + 16 + 63) // 64 * 64


def bit(spot_ref, number):
    return lax.rem(lax.div(spot_ref[0], 2**number), 2)


def window(choice, size, tile):
    return pl.ds(pl.multiple_of(choice * size, tile), size)


def quarter(spot_ref, r, size):
    first = lax.rem(bit(spot_ref, 0) + r // 2, 2)
    second = lax.rem(bit(spot_ref, 1) + r % 2, 2)
    return window(2 * first + second, size, 16)


def run(copies):
    for one in copies:
        one.start()
    for one in copies:
        one.wait()


def prepare_pack_kernel(spot_ref, q_ref, k_ref, v_ref, out_ref, bq_ref, bv_ref, bin_ref, *refs):
    full_ref, first_ref, last_ref, held_ref, extra_ref, bq, bv, bin_, sems = refs
    width = out_ref.shape[0]
    copies = [
        pltpu.make_async_copy(ref, held_ref.at[pl.ds(i * width, width), :], sems.at[i])
        for i, ref in enumerate((q_ref, k_ref, v_ref, out_ref))
    ]
    vectors = [
        pltpu.make_async_copy(ref, to, sems.at[4 + i])
        for i, (ref, to) in enumerate(((bq_ref, bq), (bv_ref, bv), (bin_ref, bin_)))
    ]
    for one in vectors + copies:
        one.start()
    extra_ref[...] = jnp.zeros_like(extra_ref)
    for one in vectors:
        one.wait()
    extra_ref[0, :width] = bq[...].astype(F32)
    extra_ref[0, 2 * width : 3 * width] = bv[...].astype(F32)
    extra_ref[1, :] = bin_[...].astype(F32)
    held_ref[4 * width :, :] = extra_ref[...].astype(BF16)
    for one in copies:
        one.wait()
    size = first_ref.shape[0]
    run(
        [
            pltpu.make_async_copy(held_ref.at[quarter(spot_ref, 0, size), :], first_ref, sems.at[0]),
            pltpu.make_async_copy(held_ref.at[quarter(spot_ref, 3, size), :], last_ref, sems.at[1]),
            pltpu.make_async_copy(held_ref, full_ref, sems.at[2]),
        ]
    )


def prepare_pack(spot, wq, wk, wv, wout, bq, bv, bin_):
    width, model = wout.shape
    rows = pack_rows(width)
    return pl.pallas_call(
        prepare_pack_kernel,
        out_shape=(hbm((rows, model)), hbm((rows // 4, model)), hbm((rows // 4, model))),
        in_specs=[SMEM] + [HBM] * 7,
        out_specs=(HBM,) * 3,
        scratch_shapes=[
            pltpu.VMEM((rows, model), BF16),
            pltpu.VMEM((rows - 4 * width, model), F32),
            pltpu.VMEM(bq.shape, BF16),
            pltpu.VMEM(bv.shape, BF16),
            pltpu.VMEM(bin_.shape, BF16),
            pltpu.SemaphoreType.DMA((7,)),
        ],
        compiler_params=params(),
        name="prepare_pack",
    )(spot, *(pinned(one) for one in (wq.T, wk.T, wv.T, wout, bq, bv, bin_)))


def prepare_feed_kernel(spot_ref, win_ref, wd_ref, *refs):
    outs, held, sems = refs[:4], refs[4:8], refs[8]
    size = outs[0].shape[0]
    loads = []
    for i in range(4):
        source = (win_ref, wd_ref)[i // 2].at[quarter(spot_ref, 3 * (i % 2), size), :]
        loads.append(pltpu.make_async_copy(source, held[i], sems.at[i]))
        loads[i].start()
    stores = []
    for i in range(4):
        loads[i].wait()
        stores.append(pltpu.make_async_copy(held[i], outs[i], sems.at[i]))
        stores[i].start()
    for one in stores:
        one.wait()


def prepare_feed(spot, win, wd):
    size, model = win.shape[0] // 4, win.shape[1]
    return pl.pallas_call(
        prepare_feed_kernel,
        out_shape=(hbm((size, model)),) * 4,
        in_specs=[SMEM, HBM, HBM],
        out_specs=(HBM,) * 4,
        scratch_shapes=[pltpu.VMEM((size, model), BF16)] * 4 + [pltpu.SemaphoreType.DMA((4,))],
        compiler_params=params(),
        name="prepare_feed",
    )(spot, pinned(win), pinned(wd))


def finish_pack_kernel(spot_ref, *refs):
    parts, (q_ref, k_ref, v_ref, out_ref, extra_ref, held_ref) = refs[:4], refs[4:]
    size = parts[0].shape[0]
    width = q_ref.shape[0]
    for r in range(4):
        held_ref[quarter(spot_ref, r, size), :] = parts[r][...]
    for i, ref in enumerate((q_ref, k_ref, v_ref, out_ref)):
        ref[...] = held_ref[i * width : (i + 1) * width, :].astype(F32)
    extra_ref[...] = held_ref[4 * width : 4 * width + 16, :].astype(F32)


def finish_pack(spot, parts, width):
    size, model = parts[0].shape
    one = jax.ShapeDtypeStruct((width, model), F32)
    return pl.pallas_call(
        finish_pack_kernel,
        out_shape=(one,) * 4 + (jax.ShapeDtypeStruct((16, model), F32),),
        in_specs=[SMEM] + [VMEM] * 4,
        out_specs=(VMEM,) * 5,
        scratch_shapes=[pltpu.VMEM((4 * size, model), BF16)],
        compiler_params=params(),
        cost_estimate=COST,
        name="finish_pack",
    )(spot, *parts)


def finish_block_kernel(spot_ref, *refs):
    for r in range(4):
        refs[4][quarter(spot_ref, r, refs[r].shape[0]), :] = refs[r][...].astype(F32)


def finish_block(spot, parts):
    size, model = parts[0].shape
    return pl.pallas_call(
        finish_block_kernel,
        out_shape=jax.ShapeDtypeStruct((4 * size, model), F32),
        in_specs=[SMEM] + [VMEM] * 4,
        out_specs=VMEM,
        compiler_params=params(),
        cost_estimate=COST,
        name="finish_block",
    )(spot, *parts)


def attend_forward_kernel(pieces, length_ref, seq_ref, spot_ref, x_ref, *refs):
    parts, refs = refs[:pieces], refs[pieces:]
    if pieces > 1:
        pack_out, *refs, pack_ref = refs
    else:
        pack_ref = parts[0]
    qkv_out, e_out, r_out, att_out, bias_out, qkv_ref, e_ref, r_ref, att_ref, sems = refs
    width = att_ref.shape[0]
    heads = width // HEAD
    if pieces == 1:
        bias_out[...] = pack_ref[4 * width : 4 * width + 16, :]
    scale = math.log2(math.e) / math.sqrt(HEAD)
    copies = []

    def store(source, target, sem):
        copies.append(pltpu.make_async_copy(source, target, sems.at[sem]))
        copies[-1].start()

    if pieces > 1:
        size = parts[0].shape[0]
        for r in range(4):
            pack_ref[quarter(spot_ref, r, size), :] = parts[r][...]
        store(pack_ref, pack_out, heads)
        bias_out[...] = pack_ref[4 * width : 4 * width + 16, :]
    bias = jnp.transpose(pack_ref[4 * width : 4 * width + 16, :].astype(F32))[: 3 * width, 0:1]
    projected = dot(pack_ref[: 3 * width, :], x_ref[...], 1, 1) + bias
    qkv_ref[...] = projected.astype(BF16)
    store(qkv_ref, qkv_out, heads + 1)
    visible = lax.broadcasted_iota(jnp.int32, (SEQ_LEN, 1), 0) < length_ref[seq_ref[0]]
    for h in range(heads):
        rows = slice(h * HEAD, (h + 1) * HEAD)
        q = qkv_ref[h * HEAD : (h + 1) * HEAD, :]
        k = qkv_ref[width + h * HEAD : width + (h + 1) * HEAD, :]
        v = qkv_ref[2 * width + h * HEAD : 2 * width + (h + 1) * HEAD, :]
        scores = jnp.where(visible, dot(k, q, 0, 0) * scale, -1e30)
        highest = jnp.max(scores, axis=0, keepdims=True)
        e = jnp.exp2(scores - highest)
        r = 1.0 / jnp.sum(e, axis=0, keepdims=True)
        low = e.astype(BF16)
        e_ref[h] = low
        store(e_ref.at[h], e_out.at[h], h)
        r_ref[h : h + 1, :] = r
        att_ref[rows, :] = (dot(v, low, 1, 0) * r).astype(BF16)
    store(r_ref, r_out, heads + 2)
    store(att_ref, att_out, heads + 3)
    for one in copies:
        one.wait()


def attend_forward(scalars, x, parts):
    rows, model = x.shape
    width = model // 4
    heads = width // HEAD
    pieces = len(parts)
    full = hbm((pieces * parts[0].shape[0], model))
    held = [hbm((3 * width, rows)), hbm((heads, rows, rows)), hbm((8, rows), F32), hbm((width, rows))]
    more = [full] if pieces > 1 else []
    outs = pl.pallas_call(
        functools.partial(attend_forward_kernel, pieces),
        out_shape=(*more, *held, jax.ShapeDtypeStruct((16, model), BF16)),
        in_specs=[SMEM] * 3 + [VMEM] * (1 + pieces),
        out_specs=(HBM,) * (len(more) + 4) + (VMEM,),
        scratch_shapes=[pltpu.VMEM(one.shape, one.dtype) for one in held]
        + [pltpu.SemaphoreType.DMA((heads + 4,))]
        + [pltpu.VMEM(one.shape, one.dtype) for one in more],
        compiler_params=params(),
        cost_estimate=MIDDLE,
        name="attend_forward",
    )(*scalars, x, *parts)
    return outs if more else (parts[0], *outs)


def attend_backward_kernel(count, plus, split, first, spot_ref, x_ref, bg_ref, *refs):
    dbs, (first_ref, second_ref), refs = refs[:count], refs[count : count + 2], refs[count + 2 :]
    saved, refs = refs[: 5 * count], refs[5 * count :]
    add_in, refs = refs[:plus], refs[plus:]
    outs, refs = refs[: 1 + split], refs[1 + split :]
    g_outs, refs = refs[:count], refs[count:]
    held, (extra_ref, sems) = refs[: 7 * count], refs[7 * count : 7 * count + 2]
    factor = 1.0 / math.sqrt(HEAD)

    def move(source, target, *sem):
        copy = pltpu.make_async_copy(source, target, sems.at[sem])
        copy.start()
        return copy

    loads = []
    for n in range(count):
        pack_in, qkv_in, e_in, r_in, att_in = saved[5 * n : 5 * n + 5]
        qkv_ref, e_ref, r_ref, att_ref, wout_ref = held[7 * n : 7 * n + 5]
        width = att_ref.shape[0]
        heads = width // HEAD
        one = [
            move(pack_in.at[pl.ds(3 * width, width), :], wout_ref, n, 0),
            move(qkv_in, qkv_ref, n, 1),
            move(r_in, r_ref, n, 2),
            move(att_in, att_ref, n, 3),
        ]
        loads.append(one + [move(e_in.at[h], e_ref.at[h], n, 4 + h) for h in range(heads)])
    stores = []
    for n in range(count):
        qkv_ref, e_ref, r_ref, att_ref, wout_ref, g_ref, held_ref = held[7 * n : 7 * n + 7]
        size = held_ref.shape[0] // 4
        extra_ref[...] = jnp.zeros_like(extra_ref)
        extra_ref[1:2, :] = dbs[n][0:1, :]
        extra_ref[2:5, :] = first_ref[0:3, :]
        extra_ref[5:8, :] = second_ref[0:3, :]
        loads[n][0].wait()
        up = dot(wout_ref[...], bg_ref[...], 1, 1).astype(BF16).astype(F32)
        for one in loads[n][1:4]:
            one.wait()
        for h in range(heads):
            rows = slice(h * HEAD, (h + 1) * HEAD)
            q = qkv_ref[h * HEAD : (h + 1) * HEAD, :]
            k = qkv_ref[width + h * HEAD : width + (h + 1) * HEAD, :]
            v = qkv_ref[2 * width + h * HEAD : 2 * width + (h + 1) * HEAD, :]
            scaled = up[rows, :] * r_ref[h : h + 1, :]
            inner = jnp.sum(att_ref[rows, :].astype(F32) * scaled, axis=0, keepdims=True)
            do = scaled.astype(BF16)
            loads[n][4 + h].wait()
            e = e_ref[h]
            ds = (e.astype(F32) * (dot(v, do, 0, 0) - inner)).astype(BF16)
            g_ref[h * HEAD : (h + 1) * HEAD, :] = (dot(k, ds, 1, 0) * factor).astype(BF16)
            g_ref[width + h * HEAD : width + (h + 1) * HEAD, :] = (
                dot(q, ds, 1, 1) * factor
            ).astype(BF16)
            g_ref[2 * width + h * HEAD : 2 * width + (h + 1) * HEAD, :] = dot(do, e, 1, 1).astype(
                BF16
            )
        stores.append(move(g_ref, g_outs[n], n, 0))
        g = g_ref[...]
        extra_ref[0:1, : 3 * width] = dot(jnp.ones((8, g.shape[1]), BF16), g, 1, 1)[0:1, :]
        held_ref[4 * width :, :] = extra_ref[...].astype(BF16)
        held_ref[: 3 * width, :] = dot(g, x_ref[...], 1, 0).astype(BF16)
        held_ref[3 * width : 4 * width, :] = dot(att_ref[...], bg_ref[...], 1, 0).astype(BF16)
        for r in range(4):
            if plus:
                part = quarter(spot_ref, r, size)
                value = held_ref[part, :].astype(F32) + add_in[0][first + r].astype(F32)
                held_ref[part, :] = value.astype(BF16)
            if len(outs) == 1:
                target = outs[0].at[4 * n + r]
            else:
                target = outs[1].at[(0, 2, 0, 1)[r]] if r else outs[0]
            stores.append(
                move(held_ref.at[quarter(spot_ref, r, size), :], target, n, 4 + heads + r)
            )
    for one in stores:
        one.wait()


def attend_backward(spot, x, bg, dbs, first, second, saved, split=False, adds=()):
    rows, model = x.shape
    width = model // 4
    heads = width // HEAD
    count = len(dbs)
    full = saved[0][0].shape[0]
    more = list(adds)
    if split:
        grads = (hbm((full // 4, model)), hbm((3, full // 4, model)))
    else:
        grads = (hbm((4 * count, full // 4, model)),)
    flat = [pinned(one) for block in saved for one in block]
    return pl.pallas_call(
        functools.partial(attend_backward_kernel, count, len(more), split, 0 if split else 4),
        out_shape=grads + (hbm((3 * width, rows)),) * count,
        in_specs=[SMEM] + [VMEM] * (4 + count) + [HBM] * (5 * count) + [VMEM] * len(more),
        out_specs=(HBM,) * (len(grads) + count),
        scratch_shapes=[
            pltpu.VMEM((3 * width, rows), BF16),
            pltpu.VMEM((heads, rows, rows), BF16),
            pltpu.VMEM((8, rows), F32),
            pltpu.VMEM((width, rows), BF16),
            pltpu.VMEM((width, model), BF16),
            pltpu.VMEM((3 * width, rows), BF16),
            pltpu.VMEM((full, model), BF16),
        ]
        * count
        + [
            pltpu.VMEM((full - 4 * width, model), F32),
            pltpu.SemaphoreType.DMA((count, 8 + heads)),
        ],
        compiler_params=params(),
        cost_estimate=MIDDLE,
        name="attend_backward",
    )(spot, x, bg, *dbs, first, second, *flat, *more)


def input_grad_kernel(count, acc_ref, *refs):
    gs, packs, out_ref, sems = refs[:count], refs[count : 2 * count], refs[2 * count], refs[-1]
    held_g, held_w = refs[2 * count + 1 : 3 * count + 1], refs[3 * count + 1 : 4 * count + 1]
    width = held_w[0].shape[0]
    loads = []
    for i in range(count):
        loads.append(pltpu.make_async_copy(gs[i], held_g[i], sems.at[2 * i]))
        loads.append(
            pltpu.make_async_copy(packs[i].at[pl.ds(0, width), :], held_w[i], sems.at[2 * i + 1])
        )
    for one in loads:
        one.start()
    total = acc_ref[...]
    for i in range(count):
        loads[2 * i].wait()
        loads[2 * i + 1].wait()
        total = total + dot(held_g[i][...], held_w[i][...], 0, 0)
    out_ref[...] = total


def input_grad(acc, gs, packs):
    rows, model = acc.shape
    width, count = gs[0].shape[0], len(gs)
    return pl.pallas_call(
        functools.partial(input_grad_kernel, count),
        out_shape=jax.ShapeDtypeStruct((rows, model), F32),
        in_specs=[VMEM] + [HBM] * (2 * count),
        out_specs=VMEM,
        scratch_shapes=[pltpu.VMEM((width, rows), BF16)] * count
        + [pltpu.VMEM((width, model), BF16)] * count
        + [pltpu.SemaphoreType.DMA((2 * count,))],
        compiler_params=params(),
        cost_estimate=COST,
        name="input_grad",
    )(acc, *(pinned(one) for one in gs), *(pinned(one) for one in packs))


def first_norm_kernel(x_ref, bias_ref, gain_ref, shift_ref, *refs):
    atts, packs, refs = refs[:4], refs[4:8], refs[8:]
    z_ref, low_ref, turned_ref, rstd_ref = refs[:4]
    held_a, held_w, sems = refs[4], refs[5], refs[6]
    width = atts[0].shape[0]
    loads = []
    for i in range(4):
        part = pl.ds(i * width, width)
        loads.append(pltpu.make_async_copy(atts[i], held_a.at[part, :], sems.at[2 * i]))
        loads.append(
            pltpu.make_async_copy(
                packs[i].at[pl.ds(3 * width, width), :], held_w.at[part, :], sems.at[2 * i + 1]
            )
        )
    run(loads)
    branch = dot(held_a[...], held_w[...], 0, 0)
    total = x_ref[...].astype(F32) + branch + row(bias_ref)
    center = total - jnp.mean(total, axis=1, keepdims=True)
    rstd = lax.rsqrt(jnp.mean(center * center, axis=1, keepdims=True) + 1e-12)
    z = center * rstd
    z_ref[...] = z
    rstd_ref[...] = rstd
    normed = (z * row(gain_ref) + row(shift_ref)).astype(BF16)
    low_ref[...] = normed
    turned_ref[...] = jnp.transpose(normed)


def first_norm(x, vectors, atts, packs):
    rows, model = x.shape
    return pl.pallas_call(
        first_norm_kernel,
        out_shape=(
            jax.ShapeDtypeStruct((rows, model), F32),
            jax.ShapeDtypeStruct((rows, model), BF16),
            jax.ShapeDtypeStruct((model, rows), BF16),
            jax.ShapeDtypeStruct((rows, 1), F32),
        ),
        in_specs=[VMEM] * 4 + [HBM] * 8,
        out_specs=(VMEM,) * 4,
        scratch_shapes=[
            pltpu.VMEM((model, rows), BF16),
            pltpu.VMEM((model, model), BF16),
            pltpu.SemaphoreType.DMA((8,)),
        ],
        compiler_params=params(),
        cost_estimate=MIDDLE,
        name="first_norm",
    )(x, *vectors, *(pinned(one) for one in atts), *(pinned(one) for one in packs))


def second_norm_kernel(z_ref, feed_ref, c_ref, *refs):
    gain1, shift1, bias, gain2, shift2 = (row(ref) for ref in refs[:5])
    out_ref, grad_ref, low_ref, sum_ref = refs[5:]
    total = z_ref[...] * gain1 + shift1 + feed_ref[...] + bias
    center = total - jnp.mean(total, axis=1, keepdims=True)
    rstd = lax.rsqrt(jnp.mean(center * center, axis=1, keepdims=True) + 1e-12)
    z = center * rstd
    out_ref[...] = (z * gain2 + shift2).astype(BF16)
    c = c_ref[...].astype(F32)
    e = c * gain2
    grad = (
        e - jnp.mean(e, axis=1, keepdims=True) - z * jnp.mean(e * z, axis=1, keepdims=True)
    ) * rstd
    grad_ref[...] = grad
    low_ref[...] = grad.astype(BF16)

    @pl.when(pl.program_id(0) == 0)
    def _():
        sum_ref[...] = jnp.zeros_like(sum_ref)

    sum_ref[0:1, :] += jnp.sum(c, axis=0, keepdims=True)
    sum_ref[1:2, :] += jnp.sum(c * z, axis=0, keepdims=True)
    sum_ref[2:3, :] += jnp.sum(grad, axis=0, keepdims=True)


def second_norm(z, feed, c, vectors):
    rows, model = z.shape
    step = rows // 4
    block = pl.BlockSpec((step, model), lambda i: (i, 0))
    return pl.pallas_call(
        second_norm_kernel,
        grid=(4,),
        out_shape=(
            jax.ShapeDtypeStruct((rows, model), BF16),
            jax.ShapeDtypeStruct((rows, model), F32),
            jax.ShapeDtypeStruct((rows, model), BF16),
            jax.ShapeDtypeStruct((8, model), F32),
        ),
        in_specs=[block] * 3 + [VMEM] * 5,
        out_specs=(block, block, block, whole((8, model))),
        compiler_params=params(),
        cost_estimate=COST,
        name="second_norm",
    )(z, feed, c, *vectors)


def first_back_kernel(z_ref, rstd_ref, dn_ref, gain_ref, grad_ref, low_ref, sum_ref):
    z = z_ref[...]
    dn = dn_ref[...]
    f = dn * row(gain_ref)
    grad = (
        f - jnp.mean(f, axis=1, keepdims=True) - z * jnp.mean(f * z, axis=1, keepdims=True)
    ) * rstd_ref[...]
    grad_ref[...] = grad
    low_ref[...] = grad.astype(BF16)

    @pl.when(pl.program_id(0) == 0)
    def _():
        sum_ref[...] = jnp.zeros_like(sum_ref)

    sum_ref[0:1, :] += jnp.sum(dn, axis=0, keepdims=True)
    sum_ref[1:2, :] += jnp.sum(dn * z, axis=0, keepdims=True)
    sum_ref[2:3, :] += jnp.sum(grad, axis=0, keepdims=True)


def first_back(z, rstd, dn, gain):
    rows, model = z.shape
    step = rows // 4
    block = pl.BlockSpec((step, model), lambda i: (i, 0))
    return pl.pallas_call(
        first_back_kernel,
        grid=(4,),
        out_shape=(
            jax.ShapeDtypeStruct((rows, model), F32),
            jax.ShapeDtypeStruct((rows, model), BF16),
            jax.ShapeDtypeStruct((8, model), F32),
        ),
        in_specs=[block, pl.BlockSpec((step, 1), lambda i: (i, 0)), block, VMEM],
        out_specs=(block, block, whole((8, model))),
        compiler_params=params(),
        cost_estimate=COST,
        name="first_back",
    )(z, rstd, dn, gain)


def feed_up_kernel(pieces, count, spot_ref, low_ref, *refs):
    biases, parts, refs = refs[:count], refs[count : count + pieces], refs[count + pieces :]
    if pieces > count:
        win_ref, *refs = refs
        for r in range(4):
            win_ref[quarter(spot_ref, r, parts[r].shape[0]), :] = parts[r][...]
        parts = (win_ref,)
    for n in range(count):
        win_ref, act_ref, slope_ref = parts[n], refs[2 * n], refs[2 * n + 1]
        bias = biases[n][1:2, :].astype(F32)

        @pl.loop(0, low_ref.shape[0] // UP_ROWS)
        def _(i):
            rows = pl.ds(pl.multiple_of(i * UP_ROWS, UP_ROWS), UP_ROWS)
            lifted = dot(low_ref[rows, :], win_ref[...], 1, 0) + bias
            phi_big = 0.5 + 0.5 * lax.erf(lifted * math.sqrt(0.5))
            phi = jnp.exp(-0.5 * lifted * lifted) * (1.0 / math.sqrt(2.0 * math.pi))
            act_ref[rows, :] = (lifted * phi_big).astype(BF16)
            slope_ref[rows, :] = (phi_big + lifted * phi).astype(BF16)


def feed_up(spot, low, parts, biases):
    rows, model = low.shape
    hidden = parts[0].shape[1]
    count = len(biases)
    tall = [jax.ShapeDtypeStruct((model, hidden), BF16)] if len(parts) > count else []
    thin = jax.ShapeDtypeStruct((rows, hidden), BF16)
    return pl.pallas_call(
        functools.partial(feed_up_kernel, len(parts), count),
        out_shape=(*tall, *[thin] * (2 * count)),
        in_specs=[SMEM] + [VMEM] * (1 + count + len(parts)),
        out_specs=(VMEM,) * (2 * count + len(tall)),
        compiler_params=params(),
        cost_estimate=MIDDLE,
        name="feed_up",
    )(spot, low, *biases, *parts)


def feed_down_kernel(pieces, chained, spot_ref, *refs):
    acts, parts, refs = refs[:2], refs[2 : 2 + 2 * pieces], refs[2 + 2 * pieces :]
    if chained:
        acc_ref, *refs = refs
    copies = []
    if pieces > 1:
        *outs, feed_ref, first_ref, second_ref, sems = refs
        wides = (first_ref, second_ref)
        for i in range(2):
            for r, part in enumerate(parts[4 * i : 4 * i + 4]):
                wides[i][quarter(spot_ref, r, part.shape[0]), :] = part[...]
            copies.append(pltpu.make_async_copy(wides[i], outs[i], sems.at[i]))
            copies[-1].start()
    else:
        feed_ref = refs[0]
        wides = parts
    total = dot(acts[0][...], wides[0][...], 1, 0) + dot(acts[1][...], wides[1][...], 1, 0)
    feed_ref[...] = total + acc_ref[...] if chained else total
    for one in copies:
        one.wait()


def feed_down(spot, acts, parts, acc=None):
    rows, hidden = acts[0].shape
    pieces = len(parts[0])
    model = parts[0][0].shape[1]
    more = [] if acc is None else [acc]
    wide = [hbm((hidden, model))] * 2 if pieces > 1 else []
    outs = pl.pallas_call(
        functools.partial(feed_down_kernel, pieces, bool(more)),
        out_shape=(*wide, jax.ShapeDtypeStruct((rows, model), F32)),
        in_specs=[SMEM] + [VMEM] * (2 + 2 * pieces + len(more)),
        out_specs=(HBM,) * len(wide) + (VMEM,),
        scratch_shapes=[pltpu.VMEM(one.shape, one.dtype) for one in wide]
        + ([pltpu.SemaphoreType.DMA((2,))] if wide else []),
        compiler_params=params(),
        cost_estimate=LONG,
        name="feed_down",
    )(spot, *acts, *parts[0], *parts[1], *more)
    return outs if wide else (parts[0][0], parts[1][0], outs[0])


def give_quarters(spot_ref, held_ref, add_ref, first, outs):
    size = held_ref.shape[0] // 4
    for r, (ref, part) in enumerate(outs):
        value = held_ref[quarter(spot_ref, r, size), :]
        if add_ref is not None:
            value = value + add_ref[first + r].astype(F32)
        ref[part] = value.astype(BF16)


TOGETHER = [[(0, r) for r in range(4)], [(0, 4 + r) for r in range(4)]]
DOWN = [[(0, r) for r in range(4)], [(1, r) for r in range(4)]]
INNER = [[(0, 0), (1, 0), (0, 1), (1, 1)], [(2, 0), (2, 1), (3, 0), (3, 1)]]


def grad_shapes(rows, model, plan):
    places = [place for block in plan for place in block]
    return tuple(
        jax.ShapeDtypeStruct((sum(1 for one, _ in places if one == i), rows // 4, model), BF16)
        for i in range(1 + max(one for one, _ in places))
    )


def down_back_kernel(plan, plus, spot_ref, act_a, act_b, low_ref, *refs):
    add_ref, outs, held_ref = (refs[0] if plus else None), refs[plus:-1], refs[-1]
    for n, act_ref in enumerate((act_a, act_b)):
        held_ref[...] = dot(act_ref[...], low_ref[...], 0, 0)
        give_quarters(spot_ref, held_ref, add_ref, 4 * n, [(outs[i], p) for i, p in plan[n]])


def down_back(spot, acts, low, plan, adds=()):
    rows, model = low.shape
    hidden = acts[0].shape[1]
    grads = grad_shapes(hidden, model, plan)
    return pl.pallas_call(
        functools.partial(down_back_kernel, plan, len(adds)),
        out_shape=grads,
        in_specs=[SMEM] + [VMEM] * (3 + len(adds)),
        out_specs=(VMEM,) * len(grads),
        scratch_shapes=[pltpu.VMEM((hidden, model), F32)],
        compiler_params=params(),
        cost_estimate=LONG if adds else COST,
        name="down_back",
    )(spot, *acts, low, *adds)


def feed_back_kernel(plan, plus, spot_ref, low_ref, turned_ref, acc_ref, *refs):
    blocks, add_ref = (refs[:3], refs[3:6]), (refs[6] if plus else None)
    outs, (dn_ref, db_a, db_b, held_ref, dl_ref) = refs[6 + plus : -5], refs[-5:]
    total = acc_ref[...]
    for n, (wd_ref, slope_ref, win_ref) in enumerate(blocks):
        half = win_ref.shape[1] // 2
        for i in range(2):
            part = slice(i * half, (i + 1) * half)
            dl = dot(low_ref[...], wd_ref[part, :], 1, 1) * slope_ref[:, part].astype(F32)
            (db_a, db_b)[n][0:1, part] = jnp.sum(dl, axis=0, keepdims=True)
            dl_ref[:, part] = dl.astype(BF16)
        held_ref[...] = dot(turned_ref[...], dl_ref[...], 1, 0)
        give_quarters(spot_ref, held_ref, add_ref, 4 * n, [(outs[i], p) for i, p in plan[n]])
        total = total + dot(dl_ref[...], win_ref[...], 1, 1)
    dn_ref[...] = total


def feed_back(spot, low, turned, acc, blocks, plan, adds=()):
    rows, model = low.shape
    hidden = blocks[0][2].shape[1]
    grads = grad_shapes(model, hidden, plan)
    flat = [one for block in blocks for one in block]
    return pl.pallas_call(
        functools.partial(feed_back_kernel, plan, len(adds)),
        out_shape=grads
        + (jax.ShapeDtypeStruct((rows, model), F32),)
        + (jax.ShapeDtypeStruct((8, hidden), F32),) * 2,
        in_specs=[SMEM] + [VMEM] * (9 + len(adds)),
        out_specs=(VMEM,) * (3 + len(grads)),
        scratch_shapes=[pltpu.VMEM((model, hidden), F32), pltpu.VMEM((rows, hidden), BF16)],
        compiler_params=params(),
        cost_estimate=COST if adds else LONG,
        name="feed_back",
    )(spot, low, turned, acc, *flat, *adds)


def after(value, *others):
    return lax.optimization_barrier((value, *others))[0]


def swap(value, axis, size, step):
    return lax.ppermute(value, axis, [(i, i ^ step) for i in range(size)])


def add_kernel(plan, *refs):
    outs = refs[len(refs) - len(plan) :]
    for out_ref, terms in zip(outs, plan):
        total = None
        for n, place in terms:
            value = (refs[n][...] if place is None else refs[n][place]).astype(F32)
            total = value if total is None else total + value
        out_ref[...] = total.astype(BF16)


def add(sums, long=False):
    arrays, plan, shapes = [], [], []
    for terms in sums:
        row = []
        for term in terms:
            value, place = term if isinstance(term, tuple) else (term, None)
            known = [n for n, one in enumerate(arrays) if one is value]
            if not known:
                arrays.append(value)
            row.append((known[0] if known else len(arrays) - 1, place))
        value, place = arrays[row[0][0]], row[0][1]
        shape = value.shape
        if isinstance(place, int):
            shape = shape[1:]
        elif place is not None:
            shape = (place.stop - place.start, *shape[1:])
        plan.append(row)
        shapes.append(jax.ShapeDtypeStruct(shape, BF16))
    return pl.pallas_call(
        functools.partial(add_kernel, plan),
        out_shape=tuple(shapes),
        in_specs=[VMEM] * len(arrays),
        out_specs=(VMEM,) * len(shapes),
        compiler_params=params(),
        cost_estimate=LONG if long else COST,
        name="add",
    )(*arrays)


class Line:
    def __init__(self):
        self.last = None

    def __call__(self, value):
        return value if self.last is None else after(value, self.last)

    def done(self, value):
        self.last = value
        return value

    def adds(self, *sums, long=False):
        first = sums[0][0]
        value, place = first if isinstance(first, tuple) else (first, None)
        tied = self(value)
        sums = [
            [
                (tied, term[1]) if isinstance(term, tuple) and term[0] is value
                else tied if term is value
                else term
                for term in terms
            ]
            for terms in sums
        ]
        outs = add(sums, long)
        self.done(outs[0])
        return outs

    def add(self, *terms):
        return self.adds(terms)[0]


class Group:
    def __init__(self, dp, tensor):
        if dp < 8 or dp & (dp - 1):
            raise ValueError("dp size")
        self.dp, self.tensor = dp, tensor
        self.place = lax.axis_index("dp")

    def core(self, value):
        return swap(value, "tensor", self.tensor, 1)

    def across(self, value):
        return swap(value, "tensor", self.tensor, 2)

    def over(self, number, value):
        return swap(value, "dp", self.dp, 2**number)

    def rest(self, value, line):
        number = 3
        while 2**number < self.dp:
            value = line.add(value, self.over(number, value))
            number += 1
        return value


def local(
    inputs,
    lengths,
    weight_query,
    bias_query,
    weight_key,
    weight_value,
    bias_value,
    weight_out,
    bias_out,
    weight_in,
    bias_in,
    weight_down,
    bias_down,
    first_gain,
    first_shift,
    second_gain,
    second_shift,
    cotangent,
):
    group = Group(lax.axis_size("dp"), lax.axis_size("tensor"))
    core, across, over = group.core, group.across, group.over
    width = weight_query.shape[1]
    seq = lax.axis_index("tensor").reshape(1)
    spot = group.place.reshape(1)
    scalars = (lengths, seq, spot)
    line = Line()

    pack, pack_0, pack_3 = prepare_pack(
        spot, weight_query, weight_key, weight_value, weight_out, bias_query, bias_value, bias_in
    )
    line.done(pack_0)
    far_0 = across(pack_0)
    pack_twin = core(pack)
    win_0, win_3, wd_0, wd_3 = prepare_feed(line(spot), weight_in, weight_down)
    line.done(win_0)
    kept = [None] * 4
    kept[0] = attend_forward(scalars, line(inputs), [pack])
    line.done(kept[0][4])
    far_3 = across(line(pack_3))
    kept[1] = attend_forward(scalars, line(inputs), [pack_twin])
    line.done(kept[1][4])
    far_0 = line.done(line(far_0))
    far_1, far_2 = over(1, far_0), over(0, far_0)
    win_0 = across(after(win_0, far_0))
    far_3 = line.done(line(far_3))
    far_parts = [far_0, far_1, far_2, far_3]
    pack_twin = [core(one) for one in far_parts]
    kept[2] = attend_forward(scalars, line(inputs), far_parts)
    line.done(kept[2][4])
    wd_0 = across(after(wd_0, kept[2][4]))
    win_0 = line.done(line(win_0))
    win_1, win_2 = over(1, win_0), over(0, win_0)
    win_3 = across(after(win_3, win_0))
    kept[3] = attend_forward(scalars, line(inputs), pack_twin)
    line.done(kept[3][4])
    win_twin = core(after(weight_in, kept[2][4]))
    z, low, turned, rstd = first_norm(
        line(inputs),
        (bias_out, first_gain, first_shift),
        [one[4] for one in kept],
        [one[0] for one in kept],
    )
    line.done(low)
    acts, slopes = [None] * 4, [None] * 4
    acts[0], slopes[0], acts[1], slopes[1] = feed_up(
        spot, line(low), [weight_in, win_twin], [kept[0][5], kept[1][5]]
    )
    line.done(acts[0])
    wd_0 = line.done(line(wd_0))
    wd_1, wd_2 = over(1, wd_0), over(0, wd_0)
    wd_3 = across(after(wd_3, wd_0))
    wd_twin = core(after(weight_down, kept[3][4]))
    win_far, acts[2], slopes[2] = feed_up(
        spot, line(low), [win_0, win_1, win_2, win_3], [kept[2][5]]
    )
    line.done(acts[2])
    wins = [weight_in, win_twin, win_far, core(win_far)]
    wd_parts = [wd_0, wd_1, wd_2, wd_3]
    *near, feed = feed_down(spot, [line(acts[0]), acts[1]], [[weight_down], [wd_twin]])
    line.done(feed)
    wd_twin = [core(one) for one in wd_parts]
    acts[3], slopes[3] = feed_up(spot, line(low), [wins[3]], [kept[3][5]])
    line.done(acts[3])
    *far, feed = feed_down(spot, [line(acts[2]), acts[3]], [wd_parts, wd_twin], feed)
    wds = near + far
    results, grad_second, second_low, second_sums = second_norm(
        z, feed, cotangent, (first_gain, first_shift, bias_down, second_gain, second_shift)
    )
    line.done(second_low)

    def down(pair, plan, adds=()):
        grads = down_back(spot, [acts[r] for r in pair], line(second_low), plan, adds)
        line.done(grads[0])
        return grads

    db = [None] * 4

    def back(pair, acc, plan, adds=()):
        blocks = [(wds[r], slopes[r], wins[r]) for r in pair]
        *grads, acc, db[pair[0]], db[pair[1]] = feed_back(
            spot, line(second_low), turned, acc, blocks, plan, adds
        )
        line.done(acc)
        return grads, acc

    (down_twin,) = down((3, 1), TOGETHER)
    down_twin = core(down_twin)
    (win_twin,), dn = back((3, 1), grad_second, TOGETHER)
    win_twin = core(win_twin)
    down_far, down_near = down((2, 0), DOWN, [down_twin])
    down_far = across(down_far)
    (far_keep, far_send, near_keep, near_send), dn = back((2, 0), dn, INNER, [win_twin])
    far_moved, near_moved = over(1, far_send), over(0, near_send)
    grad_first, first_low, first_sums = first_back(line(z), rstd, dn, first_gain)
    line.done(first_low)
    gs = [None] * 4

    def attention_back(blocks, split=False, adds=()):
        outs = attend_backward(
            spot,
            inputs,
            line(first_low),
            [db[r] for r in blocks],
            first_sums,
            second_sums,
            [kept[r][:5] for r in blocks],
            split,
            adds,
        )
        for r, one in zip(blocks, outs[-len(blocks) :]):
            gs[r] = one
        line.done(gs[blocks[-1]])
        return outs[: -len(blocks)]

    (pack_twin,) = attention_back((3, 1))
    pack_twin = core(pack_twin)

    def input_part(acc, pair):
        part = input_grad(line(acc), [gs[r] for r in pair], [kept[r][0] for r in pair])
        return line.done(part)

    dx = input_part(grad_first, (3, 1))
    down_s, down_1, down_0, win_f2, win_n1 = line.adds(
        [(down_near, slice(2, 4)), (down_far, slice(2, 4))],
        [(down_near, 1), (down_far, 1)],
        [(down_near, 0), (down_far, 0)],
        [(far_keep, 1), (far_moved, 1)],
        [(near_keep, 1), (near_moved, 1)],
        long=True,
    )
    win_fx, win_nz, down_x = over(0, win_f2), over(1, win_n1), over(0, down_s)
    pack_0, pack_321 = attention_back((2,), True, [pack_twin])
    pack_321 = across(pack_321)
    (pack_near,) = attention_back((0,), False, [pack_twin])
    dx = input_part(dx, (2, 0))
    win_f0, win_0, down_1, down_0 = line.adds(
        [(far_keep, 0), (far_moved, 0), win_fx],
        [(near_keep, 0), (near_moved, 0), win_nz],
        [down_1, (down_x, 1)],
        [down_0, (down_x, 0)],
    )
    down_z, win_y = over(1, down_1), across(win_f0)
    pack_0 = across(after(pack_0, win_f0))
    down_0 = line.add(down_0, down_z)
    down_far = over(2, down_0)
    pack_x = [
        over(0, one)
        for one in line.adds(
            [(pack_near, 3), (pack_321, 1)], [(pack_near, 2), (pack_321, 0)]
        )
    ]
    win_0 = line.add(win_0, win_y)
    win_far = over(2, win_0)
    down_0 = group.rest(line.add(down_0, down_far), line)
    down_1, down_2 = over(1, down_0), over(0, down_0)
    pack_1, pack_0 = line.adds(
        [(pack_near, 1), (pack_321, 2), pack_x[0]], [(pack_near, 0), pack_0, pack_x[1]]
    )
    pack_z = over(1, pack_1)
    down_1 = line.done(line(down_1))
    down_3 = over(0, down_1)
    win_0 = group.rest(line.add(win_0, win_far), line)
    win_1, win_2 = over(1, win_0), over(0, win_0)
    pack_0 = line.add(pack_0, pack_z)
    pack_far = over(2, pack_0)
    grad_weight_down = finish_block(line(spot), [down_0, down_1, down_2, down_3])
    line.done(grad_weight_down)
    win_1 = line.done(line(win_1))
    win_3 = over(0, win_1)
    win_2 = line.done(line(win_2))
    pack_0 = group.rest(line.add(pack_0, pack_far), line)
    pack_1, pack_2 = over(1, pack_0), over(0, pack_0)
    grad_weight_in = finish_block(line(spot), [win_0, win_1, win_2, win_3])
    line.done(grad_weight_in)
    parts = [pack_0, pack_1, pack_2, over(0, pack_1)]
    grad_q, grad_k, grad_v, grad_o, extra = finish_pack(line(spot), parts, width)
    return (
        results,
        dx,
        grad_q.T,
        extra[0, :width],
        grad_k.T,
        grad_v.T,
        extra[0, 2 * width : 3 * width],
        grad_o,
        extra[4],
        grad_weight_in,
        extra[1],
        grad_weight_down,
        extra[7],
        extra[3],
        extra[2],
        extra[6],
        extra[5],
    )


def solution(mesh):
    in_specs = (
        P(("dp", "tensor"), None),
        P("dp"),
        P(None, "tensor"),
        P("tensor"),
        P(None, "tensor"),
        P(None, "tensor"),
        P("tensor"),
        P("tensor", None),
        P(),
        P(None, "tensor"),
        P("tensor"),
        P("tensor", None),
        P(),
        P(),
        P(),
        P(),
        P(),
        P(("dp", "tensor"), None),
    )
    out_specs = (
        P(("dp", "tensor"), None),
        P(("dp", "tensor"), None),
        P(None, "tensor"),
        P("tensor"),
        P(None, "tensor"),
        P(None, "tensor"),
        P("tensor"),
        P("tensor", None),
        P(),
        P(None, "tensor"),
        P("tensor"),
        P("tensor", None),
        P(),
        P(),
        P(),
        P(),
        P(),
    )
    return jax.shard_map(local, mesh=mesh, in_specs=in_specs, out_specs=out_specs, check_vma=False)
```

```python
import functools
import math

import jax
import jax.numpy as jnp
from jax import lax
from jax.experimental import pallas as pl
from jax.experimental.pallas import tpu as pltpu
from jax.sharding import PartitionSpec as P

HEAD = 64
SEQ_LEN = 512
UP_ROWS = 128
F32 = jnp.float32
BF16 = jnp.bfloat16
VMEM_LIMIT = 24 * 1024 * 1024
VMEM = pl.BlockSpec(memory_space=pltpu.VMEM)
COST = pl.CostEstimate(flops=10**9, bytes_accessed=10**9, transcendentals=0)
MIDDLE = pl.CostEstimate(flops=10**10, bytes_accessed=10**9, transcendentals=0)
LONG = pl.CostEstimate(flops=10**11, bytes_accessed=10**9, transcendentals=0)
SMEM = pl.BlockSpec(memory_space=pltpu.SMEM)
HBM = pl.BlockSpec(memory_space=pltpu.HBM)


def hbm(shape, dtype=BF16):
    return pltpu.HBM(shape, dtype)


def pinned(value):
    return pltpu.with_memory_space_constraint(value, pltpu.HBM)


def dot(left, right, left_dim, right_dim):
    return lax.dot_general(
        left, right, (((left_dim,), (right_dim,)), ((), ())), preferred_element_type=F32
    )


def params(**kwargs):
    return pltpu.CompilerParams(vmem_limit_bytes=VMEM_LIMIT, **kwargs)


def whole(shape, index=None):
    place = index or (0,) * len(shape)
    return pl.BlockSpec(shape, lambda *_: place)


def row(ref):
    return ref[...].astype(F32).reshape(1, ref.shape[0])


def pack_rows(width):
    return (4 * width + 16 + 63) // 64 * 64


def bit(spot_ref, number):
    return lax.rem(lax.div(spot_ref[0], 2**number), 2)


def window(choice, size, tile):
    return pl.ds(pl.multiple_of(choice * size, tile), size)


def head_rows(start, h):
    return pl.ds(pl.multiple_of(start + h * HEAD, HEAD), HEAD)


def quarter(spot_ref, r, size):
    first = lax.rem(bit(spot_ref, 0) + r // 2, 2)
    second = lax.rem(bit(spot_ref, 1) + r % 2, 2)
    return window(2 * first + second, size, 16)


def run(copies):
    for one in copies:
        one.start()
    for one in copies:
        one.wait()


def prepare_pack_kernel(spot_ref, q_ref, k_ref, v_ref, out_ref, bq_ref, bv_ref, bin_ref, *refs):
    full_ref, first_ref, last_ref, held_ref, extra_ref, bq, bv, bin_, sems = refs
    width = out_ref.shape[0]
    copies = [
        pltpu.make_async_copy(ref, held_ref.at[pl.ds(i * width, width), :], sems.at[i])
        for i, ref in enumerate((q_ref, k_ref, v_ref, out_ref))
    ]
    vectors = [
        pltpu.make_async_copy(ref, to, sems.at[4 + i])
        for i, (ref, to) in enumerate(((bq_ref, bq), (bv_ref, bv), (bin_ref, bin_)))
    ]
    for one in vectors + copies:
        one.start()
    extra_ref[...] = jnp.zeros_like(extra_ref)
    for one in vectors:
        one.wait()
    extra_ref[0, :width] = bq[...].astype(F32)
    extra_ref[0, 2 * width : 3 * width] = bv[...].astype(F32)
    extra_ref[1, :] = bin_[...].astype(F32)
    held_ref[4 * width :, :] = extra_ref[...].astype(BF16)
    for one in copies:
        one.wait()
    size = first_ref.shape[0]
    run(
        [
            pltpu.make_async_copy(held_ref.at[quarter(spot_ref, 0, size), :], first_ref, sems.at[0]),
            pltpu.make_async_copy(held_ref.at[quarter(spot_ref, 3, size), :], last_ref, sems.at[1]),
            pltpu.make_async_copy(held_ref, full_ref, sems.at[2]),
        ]
    )


def prepare_pack(spot, wq, wk, wv, wout, bq, bv, bin_):
    width, model = wout.shape
    rows = pack_rows(width)
    return pl.pallas_call(
        prepare_pack_kernel,
        out_shape=(hbm((rows, model)), hbm((rows // 4, model)), hbm((rows // 4, model))),
        in_specs=[SMEM] + [HBM] * 7,
        out_specs=(HBM,) * 3,
        scratch_shapes=[
            pltpu.VMEM((rows, model), BF16),
            pltpu.VMEM((rows - 4 * width, model), F32),
            pltpu.VMEM(bq.shape, BF16),
            pltpu.VMEM(bv.shape, BF16),
            pltpu.VMEM(bin_.shape, BF16),
            pltpu.SemaphoreType.DMA((7,)),
        ],
        compiler_params=params(),
        name="prepare_pack",
    )(spot, *(pinned(one) for one in (wq.T, wk.T, wv.T, wout, bq, bv, bin_)))


def prepare_feed_kernel(spot_ref, win_ref, wd_ref, *refs):
    outs, held, sems = refs[:4], refs[4:8], refs[8]
    size = outs[0].shape[0]
    loads = []
    for i in range(4):
        source = (win_ref, wd_ref)[i // 2].at[quarter(spot_ref, 3 * (i % 2), size), :]
        loads.append(pltpu.make_async_copy(source, held[i], sems.at[i]))
        loads[i].start()
    stores = []
    for i in range(4):
        loads[i].wait()
        stores.append(pltpu.make_async_copy(held[i], outs[i], sems.at[i]))
        stores[i].start()
    for one in stores:
        one.wait()


def prepare_feed(spot, win, wd):
    size, model = win.shape[0] // 4, win.shape[1]
    return pl.pallas_call(
        prepare_feed_kernel,
        out_shape=(hbm((size, model)),) * 4,
        in_specs=[SMEM, HBM, HBM],
        out_specs=(HBM,) * 4,
        scratch_shapes=[pltpu.VMEM((size, model), BF16)] * 4 + [pltpu.SemaphoreType.DMA((4,))],
        compiler_params=params(),
        name="prepare_feed",
    )(spot, pinned(win), pinned(wd))


def finish_pack_kernel(spot_ref, *refs):
    parts, (q_ref, k_ref, v_ref, out_ref, extra_ref, held_ref) = refs[:4], refs[4:]
    size = parts[0].shape[0]
    width = q_ref.shape[0]
    for r in range(4):
        held_ref[quarter(spot_ref, r, size), :] = parts[r][...]
    for i, ref in enumerate((q_ref, k_ref, v_ref, out_ref)):
        ref[...] = held_ref[i * width : (i + 1) * width, :].astype(F32)
    extra_ref[...] = held_ref[4 * width : 4 * width + 16, :].astype(F32)


def finish_pack(spot, parts, width):
    size, model = parts[0].shape
    one = jax.ShapeDtypeStruct((width, model), F32)
    return pl.pallas_call(
        finish_pack_kernel,
        out_shape=(one,) * 4 + (jax.ShapeDtypeStruct((16, model), F32),),
        in_specs=[SMEM] + [VMEM] * 4,
        out_specs=(VMEM,) * 5,
        scratch_shapes=[pltpu.VMEM((4 * size, model), BF16)],
        compiler_params=params(),
        cost_estimate=COST,
        name="finish_pack",
    )(spot, *parts)


def finish_block_kernel(spot_ref, *refs):
    for r in range(4):
        refs[4][quarter(spot_ref, r, refs[r].shape[0]), :] = refs[r][...].astype(F32)


def finish_block(spot, parts):
    size, model = parts[0].shape
    return pl.pallas_call(
        finish_block_kernel,
        out_shape=jax.ShapeDtypeStruct((4 * size, model), F32),
        in_specs=[SMEM] + [VMEM] * 4,
        out_specs=VMEM,
        compiler_params=params(),
        cost_estimate=COST,
        name="finish_block",
    )(spot, *parts)


def attend_forward_kernel(pieces, length_ref, seq_ref, spot_ref, x_ref, *refs):
    parts, refs = refs[:pieces], refs[pieces:]
    if pieces > 1:
        pack_out, *refs, pack_ref = refs
    else:
        pack_ref = parts[0]
    qkv_out, e_out, r_out, att_out, bias_out, qkv_ref, e_ref, r_ref, att_ref, sems = refs
    width = att_ref.shape[0]
    heads = width // HEAD
    if pieces == 1:
        bias_out[...] = pack_ref[4 * width : 4 * width + 16, :]
    scale = math.log2(math.e) / math.sqrt(HEAD)
    copies = []

    def store(source, target, sem):
        copies.append(pltpu.make_async_copy(source, target, sems.at[sem]))
        copies[-1].start()

    if pieces > 1:
        size = parts[0].shape[0]
        for r in range(4):
            pack_ref[quarter(spot_ref, r, size), :] = parts[r][...]
        store(pack_ref, pack_out, heads)
        bias_out[...] = pack_ref[4 * width : 4 * width + 16, :]
    bias = jnp.transpose(pack_ref[4 * width : 4 * width + 16, :].astype(F32))[: 3 * width, 0:1]
    projected = dot(pack_ref[: 3 * width, :], x_ref[...], 1, 1) + bias
    qkv_ref[...] = projected.astype(BF16)
    store(qkv_ref, qkv_out, heads + 1)
    visible = lax.broadcasted_iota(jnp.int32, (SEQ_LEN, 1), 0) < length_ref[seq_ref[0]]

    @pl.loop(0, heads)
    def _(h):
        q, k, v = (qkv_ref[head_rows(i * width, h), :] for i in range(3))
        scores = jnp.where(visible, dot(k, q, 0, 0) * scale, -1e30)
        highest = jnp.max(scores, axis=0, keepdims=True)
        e = jnp.exp2(scores - highest)
        r = 1.0 / jnp.sum(e, axis=0, keepdims=True)
        low = e.astype(BF16)
        e_ref[h] = low
        pltpu.make_async_copy(e_ref.at[h], e_out.at[h], sems.at[h]).start()
        r_ref[h] = jnp.broadcast_to(r, r_ref.shape[1:])
        att_ref[head_rows(0, h), :] = (dot(v, low, 1, 0) * r).astype(BF16)

    copies.extend(
        pltpu.make_async_copy(e_ref.at[h], e_out.at[h], sems.at[h]) for h in range(heads)
    )
    store(r_ref, r_out, heads + 2)
    store(att_ref, att_out, heads + 3)
    for one in copies:
        one.wait()


def attend_forward(scalars, x, parts):
    rows, model = x.shape
    width = model // 4
    heads = width // HEAD
    pieces = len(parts)
    full = hbm((pieces * parts[0].shape[0], model))
    held = [
        hbm((3 * width, rows)),
        hbm((heads, rows, rows)),
        hbm((heads, 8, rows), F32),
        hbm((width, rows)),
    ]
    more = [full] if pieces > 1 else []
    outs = pl.pallas_call(
        functools.partial(attend_forward_kernel, pieces),
        out_shape=(*more, *held, jax.ShapeDtypeStruct((16, model), BF16)),
        in_specs=[SMEM] * 3 + [VMEM] * (1 + pieces),
        out_specs=(HBM,) * (len(more) + 4) + (VMEM,),
        scratch_shapes=[pltpu.VMEM(one.shape, one.dtype) for one in held]
        + [pltpu.SemaphoreType.DMA((heads + 4,))]
        + [pltpu.VMEM(one.shape, one.dtype) for one in more],
        compiler_params=params(),
        cost_estimate=MIDDLE,
        name="attend_forward",
    )(*scalars, x, *parts)
    return outs if more else (parts[0], *outs)


def attend_backward_kernel(count, plus, split, first, spot_ref, x_ref, bg_ref, *refs):
    dbs, (first_ref, second_ref), refs = refs[:count], refs[count : count + 2], refs[count + 2 :]
    saved, refs = refs[: 5 * count], refs[5 * count :]
    add_in, refs = refs[:plus], refs[plus:]
    outs, refs = refs[: 1 + split], refs[1 + split :]
    g_outs, refs = refs[:count], refs[count:]
    held, (extra_ref, up_ref, sems) = refs[: 7 * count], refs[7 * count : 7 * count + 3]
    factor = 1.0 / math.sqrt(HEAD)

    def move(source, target, *sem):
        copy = pltpu.make_async_copy(source, target, sems.at[sem])
        copy.start()
        return copy

    loads = []
    for n in range(count):
        pack_in, qkv_in, e_in, r_in, att_in = saved[5 * n : 5 * n + 5]
        qkv_ref, e_ref, r_ref, att_ref, wout_ref = held[7 * n : 7 * n + 5]
        width = att_ref.shape[0]
        heads = width // HEAD
        one = [
            move(pack_in.at[pl.ds(3 * width, width), :], wout_ref, n, 0),
            move(qkv_in, qkv_ref, n, 1),
            move(r_in, r_ref, n, 2),
            move(att_in, att_ref, n, 3),
        ]
        loads.append(one + [move(e_in.at[h], e_ref.at[h], n, 4 + h) for h in range(heads)])
    stores = []
    for n in range(count):
        e_in = saved[5 * n + 2]
        qkv_ref, e_ref, r_ref, att_ref, wout_ref, g_ref, held_ref = held[7 * n : 7 * n + 7]
        size = held_ref.shape[0] // 4
        extra_ref[...] = jnp.zeros_like(extra_ref)
        extra_ref[1:2, :] = dbs[n][0:1, :]
        extra_ref[2:5, :] = first_ref[0:3, :]
        extra_ref[5:8, :] = second_ref[0:3, :]
        loads[n][0].wait()
        up_ref[...] = dot(wout_ref[...], bg_ref[...], 1, 1).astype(BF16)
        for one in loads[n][1:4]:
            one.wait()

        @pl.loop(0, heads)
        def _(h):
            q, k, v = (qkv_ref[head_rows(i * width, h), :] for i in range(3))
            scaled = up_ref[head_rows(0, h), :].astype(F32) * r_ref[h, 0:1, :]
            attended = att_ref[head_rows(0, h), :].astype(F32)
            inner = jnp.sum(attended * scaled, axis=0, keepdims=True)
            do = scaled.astype(BF16)
            pltpu.make_async_copy(e_in.at[h], e_ref.at[h], sems.at[n, 4 + h]).wait()
            e = e_ref[h]
            ds = (e.astype(F32) * (dot(v, do, 0, 0) - inner)).astype(BF16)
            g_ref[head_rows(0, h), :] = (dot(k, ds, 1, 0) * factor).astype(BF16)
            g_ref[head_rows(width, h), :] = (dot(q, ds, 1, 1) * factor).astype(BF16)
            g_ref[head_rows(2 * width, h), :] = dot(do, e, 1, 1).astype(BF16)

        stores.append(move(g_ref, g_outs[n], n, 0))
        g = g_ref[...]
        extra_ref[0:1, : 3 * width] = dot(jnp.ones((8, g.shape[1]), BF16), g, 1, 1)[0:1, :]
        held_ref[4 * width :, :] = extra_ref[...].astype(BF16)
        held_ref[: 3 * width, :] = dot(g, x_ref[...], 1, 0).astype(BF16)
        held_ref[3 * width : 4 * width, :] = dot(att_ref[...], bg_ref[...], 1, 0).astype(BF16)
        for r in range(4):
            if plus:
                part = quarter(spot_ref, r, size)
                value = held_ref[part, :].astype(F32) + add_in[0][first + r].astype(F32)
                held_ref[part, :] = value.astype(BF16)
            if len(outs) == 1:
                target = outs[0].at[4 * n + r]
            else:
                target = outs[1].at[(0, 2, 0, 1)[r]] if r else outs[0]
            stores.append(
                move(held_ref.at[quarter(spot_ref, r, size), :], target, n, 4 + heads + r)
            )
    for one in stores:
        one.wait()


def attend_backward(spot, x, bg, dbs, first, second, saved, split=False, adds=()):
    rows, model = x.shape
    width = model // 4
    heads = width // HEAD
    count = len(dbs)
    full = saved[0][0].shape[0]
    more = list(adds)
    if split:
        grads = (hbm((full // 4, model)), hbm((3, full // 4, model)))
    else:
        grads = (hbm((4 * count, full // 4, model)),)
    flat = [pinned(one) for block in saved for one in block]
    return pl.pallas_call(
        functools.partial(attend_backward_kernel, count, len(more), split, 0 if split else 4),
        out_shape=grads + (hbm((3 * width, rows)),) * count,
        in_specs=[SMEM] + [VMEM] * (4 + count) + [HBM] * (5 * count) + [VMEM] * len(more),
        out_specs=(HBM,) * (len(grads) + count),
        scratch_shapes=[
            pltpu.VMEM((3 * width, rows), BF16),
            pltpu.VMEM((heads, rows, rows), BF16),
            pltpu.VMEM((heads, 8, rows), F32),
            pltpu.VMEM((width, rows), BF16),
            pltpu.VMEM((width, model), BF16),
            pltpu.VMEM((3 * width, rows), BF16),
            pltpu.VMEM((full, model), BF16),
        ]
        * count
        + [
            pltpu.VMEM((full - 4 * width, model), F32),
            pltpu.VMEM((width, rows), BF16),
            pltpu.SemaphoreType.DMA((count, 8 + heads)),
        ],
        compiler_params=params(),
        cost_estimate=COST if count > 1 else MIDDLE,
        name="attend_backward",
    )(spot, x, bg, *dbs, first, second, *flat, *more)


def input_grad_kernel(count, acc_ref, *refs):
    gs, packs, out_ref, sems = refs[:count], refs[count : 2 * count], refs[2 * count], refs[-1]
    held_g, held_w = refs[2 * count + 1 : 3 * count + 1], refs[3 * count + 1 : 4 * count + 1]
    width = held_w[0].shape[0]
    loads = []
    for i in range(count):
        loads.append(pltpu.make_async_copy(gs[i], held_g[i], sems.at[2 * i]))
        loads.append(
            pltpu.make_async_copy(packs[i].at[pl.ds(0, width), :], held_w[i], sems.at[2 * i + 1])
        )
    for one in loads:
        one.start()
    total = acc_ref[...]
    for i in range(count):
        loads[2 * i].wait()
        loads[2 * i + 1].wait()
        total = total + dot(held_g[i][...], held_w[i][...], 0, 0)
    out_ref[...] = total


def input_grad(acc, gs, packs):
    rows, model = acc.shape
    width, count = gs[0].shape[0], len(gs)
    return pl.pallas_call(
        functools.partial(input_grad_kernel, count),
        out_shape=jax.ShapeDtypeStruct((rows, model), F32),
        in_specs=[VMEM] + [HBM] * (2 * count),
        out_specs=VMEM,
        scratch_shapes=[pltpu.VMEM((width, rows), BF16)] * count
        + [pltpu.VMEM((width, model), BF16)] * count
        + [pltpu.SemaphoreType.DMA((2 * count,))],
        compiler_params=params(),
        cost_estimate=COST,
        name="input_grad",
    )(acc, *(pinned(one) for one in gs), *(pinned(one) for one in packs))


def first_norm_kernel(x_ref, bias_ref, gain_ref, shift_ref, *refs):
    atts, packs, refs = refs[:4], refs[4:8], refs[8:]
    z_ref, low_ref, turned_ref, rstd_ref = refs[:4]
    held_a, held_w, sems = refs[4], refs[5], refs[6]
    width = atts[0].shape[0]
    loads = []
    for i in range(4):
        part = pl.ds(i * width, width)
        loads.append(pltpu.make_async_copy(atts[i], held_a.at[part, :], sems.at[2 * i]))
        loads.append(
            pltpu.make_async_copy(
                packs[i].at[pl.ds(3 * width, width), :], held_w.at[part, :], sems.at[2 * i + 1]
            )
        )
    run(loads)
    branch = dot(held_a[...], held_w[...], 0, 0)
    total = x_ref[...].astype(F32) + branch + row(bias_ref)
    center = total - jnp.mean(total, axis=1, keepdims=True)
    rstd = lax.rsqrt(jnp.mean(center * center, axis=1, keepdims=True) + 1e-12)
    z = center * rstd
    z_ref[...] = z
    rstd_ref[...] = rstd
    normed = (z * row(gain_ref) + row(shift_ref)).astype(BF16)
    low_ref[...] = normed
    turned_ref[...] = jnp.transpose(normed)


def first_norm(x, vectors, atts, packs):
    rows, model = x.shape
    return pl.pallas_call(
        first_norm_kernel,
        out_shape=(
            jax.ShapeDtypeStruct((rows, model), F32),
            jax.ShapeDtypeStruct((rows, model), BF16),
            jax.ShapeDtypeStruct((model, rows), BF16),
            jax.ShapeDtypeStruct((rows, 1), F32),
        ),
        in_specs=[VMEM] * 4 + [HBM] * 8,
        out_specs=(VMEM,) * 4,
        scratch_shapes=[
            pltpu.VMEM((model, rows), BF16),
            pltpu.VMEM((model, model), BF16),
            pltpu.SemaphoreType.DMA((8,)),
        ],
        compiler_params=params(),
        cost_estimate=MIDDLE,
        name="first_norm",
    )(x, *vectors, *(pinned(one) for one in atts), *(pinned(one) for one in packs))


def second_norm_kernel(z_ref, feed_ref, c_ref, *refs):
    gain1, shift1, bias, gain2, shift2 = (row(ref) for ref in refs[:5])
    out_ref, grad_ref, low_ref, sum_ref = refs[5:]
    total = z_ref[...] * gain1 + shift1 + feed_ref[...] + bias
    center = total - jnp.mean(total, axis=1, keepdims=True)
    rstd = lax.rsqrt(jnp.mean(center * center, axis=1, keepdims=True) + 1e-12)
    z = center * rstd
    out_ref[...] = (z * gain2 + shift2).astype(BF16)
    c = c_ref[...].astype(F32)
    e = c * gain2
    grad = (
        e - jnp.mean(e, axis=1, keepdims=True) - z * jnp.mean(e * z, axis=1, keepdims=True)
    ) * rstd
    grad_ref[...] = grad
    low_ref[...] = grad.astype(BF16)

    @pl.when(pl.program_id(0) == 0)
    def _():
        sum_ref[...] = jnp.zeros_like(sum_ref)

    sum_ref[0:1, :] += jnp.sum(c, axis=0, keepdims=True)
    sum_ref[1:2, :] += jnp.sum(c * z, axis=0, keepdims=True)
    sum_ref[2:3, :] += jnp.sum(grad, axis=0, keepdims=True)


def second_norm(z, feed, c, vectors):
    rows, model = z.shape
    step = rows // 4
    block = pl.BlockSpec((step, model), lambda i: (i, 0))
    return pl.pallas_call(
        second_norm_kernel,
        grid=(4,),
        out_shape=(
            jax.ShapeDtypeStruct((rows, model), BF16),
            jax.ShapeDtypeStruct((rows, model), F32),
            jax.ShapeDtypeStruct((rows, model), BF16),
            jax.ShapeDtypeStruct((8, model), F32),
        ),
        in_specs=[block] * 3 + [VMEM] * 5,
        out_specs=(block, block, block, whole((8, model))),
        compiler_params=params(),
        cost_estimate=COST,
        name="second_norm",
    )(z, feed, c, *vectors)


def first_back_kernel(z_ref, rstd_ref, dn_ref, gain_ref, grad_ref, low_ref, sum_ref):
    z = z_ref[...]
    dn = dn_ref[...]
    f = dn * row(gain_ref)
    grad = (
        f - jnp.mean(f, axis=1, keepdims=True) - z * jnp.mean(f * z, axis=1, keepdims=True)
    ) * rstd_ref[...]
    grad_ref[...] = grad
    low_ref[...] = grad.astype(BF16)

    @pl.when(pl.program_id(0) == 0)
    def _():
        sum_ref[...] = jnp.zeros_like(sum_ref)

    sum_ref[0:1, :] += jnp.sum(dn, axis=0, keepdims=True)
    sum_ref[1:2, :] += jnp.sum(dn * z, axis=0, keepdims=True)
    sum_ref[2:3, :] += jnp.sum(grad, axis=0, keepdims=True)


def first_back(z, rstd, dn, gain):
    rows, model = z.shape
    step = rows // 4
    block = pl.BlockSpec((step, model), lambda i: (i, 0))
    return pl.pallas_call(
        first_back_kernel,
        grid=(4,),
        out_shape=(
            jax.ShapeDtypeStruct((rows, model), F32),
            jax.ShapeDtypeStruct((rows, model), BF16),
            jax.ShapeDtypeStruct((8, model), F32),
        ),
        in_specs=[block, pl.BlockSpec((step, 1), lambda i: (i, 0)), block, VMEM],
        out_specs=(block, block, whole((8, model))),
        compiler_params=params(),
        cost_estimate=COST,
        name="first_back",
    )(z, rstd, dn, gain)


def feed_up_kernel(pieces, count, spot_ref, low_ref, *refs):
    biases, parts, refs = refs[:count], refs[count : count + pieces], refs[count + pieces :]
    if pieces > count:
        win_ref, *refs = refs
        for r in range(4):
            win_ref[quarter(spot_ref, r, parts[r].shape[0]), :] = parts[r][...]
        parts = (win_ref,)
    for n in range(count):
        win_ref, act_ref, slope_ref = parts[n], refs[2 * n], refs[2 * n + 1]
        bias = biases[n][1:2, :].astype(F32)

        @pl.loop(0, low_ref.shape[0] // UP_ROWS)
        def _(i):
            rows = pl.ds(pl.multiple_of(i * UP_ROWS, UP_ROWS), UP_ROWS)
            lifted = dot(low_ref[rows, :], win_ref[...], 1, 0) + bias
            phi_big = 0.5 + 0.5 * lax.erf(lifted * math.sqrt(0.5))
            phi = jnp.exp(-0.5 * lifted * lifted) * (1.0 / math.sqrt(2.0 * math.pi))
            act_ref[rows, :] = (lifted * phi_big).astype(BF16)
            slope_ref[rows, :] = (phi_big + lifted * phi).astype(BF16)


def feed_up(spot, low, parts, biases):
    rows, model = low.shape
    hidden = parts[0].shape[1]
    count = len(biases)
    tall = [jax.ShapeDtypeStruct((model, hidden), BF16)] if len(parts) > count else []
    thin = jax.ShapeDtypeStruct((rows, hidden), BF16)
    return pl.pallas_call(
        functools.partial(feed_up_kernel, len(parts), count),
        out_shape=(*tall, *[thin] * (2 * count)),
        in_specs=[SMEM] + [VMEM] * (1 + count + len(parts)),
        out_specs=(VMEM,) * (2 * count + len(tall)),
        compiler_params=params(),
        cost_estimate=MIDDLE,
        name="feed_up",
    )(spot, low, *biases, *parts)


def feed_down_kernel(pieces, chained, spot_ref, *refs):
    acts, parts, refs = refs[:2], refs[2 : 2 + 2 * pieces], refs[2 + 2 * pieces :]
    if chained:
        acc_ref, *refs = refs
    copies = []
    if pieces > 1:
        *outs, feed_ref, first_ref, second_ref, sems = refs
        wides = (first_ref, second_ref)
        for i in range(2):
            for r, part in enumerate(parts[4 * i : 4 * i + 4]):
                wides[i][quarter(spot_ref, r, part.shape[0]), :] = part[...]
            copies.append(pltpu.make_async_copy(wides[i], outs[i], sems.at[i]))
            copies[-1].start()
    else:
        feed_ref = refs[0]
        wides = parts
    total = dot(acts[0][...], wides[0][...], 1, 0) + dot(acts[1][...], wides[1][...], 1, 0)
    feed_ref[...] = total + acc_ref[...] if chained else total
    for one in copies:
        one.wait()


def feed_down(spot, acts, parts, acc=None):
    rows, hidden = acts[0].shape
    pieces = len(parts[0])
    model = parts[0][0].shape[1]
    more = [] if acc is None else [acc]
    wide = [hbm((hidden, model))] * 2 if pieces > 1 else []
    outs = pl.pallas_call(
        functools.partial(feed_down_kernel, pieces, bool(more)),
        out_shape=(*wide, jax.ShapeDtypeStruct((rows, model), F32)),
        in_specs=[SMEM] + [VMEM] * (2 + 2 * pieces + len(more)),
        out_specs=(HBM,) * len(wide) + (VMEM,),
        scratch_shapes=[pltpu.VMEM(one.shape, one.dtype) for one in wide]
        + ([pltpu.SemaphoreType.DMA((2,))] if wide else []),
        compiler_params=params(),
        cost_estimate=LONG,
        name="feed_down",
    )(spot, *acts, *parts[0], *parts[1], *more)
    return outs if wide else (parts[0][0], parts[1][0], outs[0])


def give_quarters(spot_ref, held_ref, add_ref, first, outs):
    size = held_ref.shape[0] // 4
    for r, (ref, part) in enumerate(outs):
        value = held_ref[quarter(spot_ref, r, size), :]
        if add_ref is not None:
            value = value + add_ref[first + r].astype(F32)
        ref[part] = value.astype(BF16)


TOGETHER = [[(0, r) for r in range(4)], [(0, 4 + r) for r in range(4)]]
LATE = [[(1, 0), (0, 2), (0, 0), (0, 1)], [(2, r) for r in range(4)]]
EARLY = [[(0, 0), (1, 0), (0, 1), (1, 1)], [(2, 0), (2, 1), (3, 0), (3, 1)]]


def grad_shapes(rows, model, plan):
    places = [place for block in plan for place in block]
    return tuple(
        jax.ShapeDtypeStruct((sum(1 for one, _ in places if one == i), rows // 4, model), BF16)
        for i in range(1 + max(one for one, _ in places))
    )


def down_back_kernel(plan, plus, spot_ref, act_a, act_b, low_ref, *refs):
    add_ref, outs, held_ref = (refs[0] if plus else None), refs[plus:-1], refs[-1]
    for n, act_ref in enumerate((act_a, act_b)):
        held_ref[...] = dot(act_ref[...], low_ref[...], 0, 0)
        give_quarters(spot_ref, held_ref, add_ref, 4 * n, [(outs[i], p) for i, p in plan[n]])


def down_back(spot, acts, low, plan, adds=()):
    rows, model = low.shape
    hidden = acts[0].shape[1]
    grads = grad_shapes(hidden, model, plan)
    return pl.pallas_call(
        functools.partial(down_back_kernel, plan, len(adds)),
        out_shape=grads,
        in_specs=[SMEM] + [VMEM] * (3 + len(adds)),
        out_specs=(VMEM,) * len(grads),
        scratch_shapes=[pltpu.VMEM((hidden, model), F32)],
        compiler_params=params(),
        cost_estimate=LONG if adds else COST,
        name="down_back",
    )(spot, *acts, low, *adds)


def feed_back_kernel(plan, plus, spot_ref, low_ref, turned_ref, acc_ref, *refs):
    blocks, add_ref = (refs[:3], refs[3:6]), (refs[6] if plus else None)
    outs, (dn_ref, db_a, db_b, held_ref, dl_ref) = refs[6 + plus : -5], refs[-5:]
    total = acc_ref[...]
    for n, (wd_ref, slope_ref, win_ref) in enumerate(blocks):
        half = win_ref.shape[1] // 2
        for i in range(2):
            part = slice(i * half, (i + 1) * half)
            dl = dot(low_ref[...], wd_ref[part, :], 1, 1) * slope_ref[:, part].astype(F32)
            (db_a, db_b)[n][0:1, part] = jnp.sum(dl, axis=0, keepdims=True)
            dl_ref[:, part] = dl.astype(BF16)
        held_ref[...] = dot(turned_ref[...], dl_ref[...], 1, 0)
        give_quarters(spot_ref, held_ref, add_ref, 4 * n, [(outs[i], p) for i, p in plan[n]])
        total = total + dot(dl_ref[...], win_ref[...], 1, 1)
    dn_ref[...] = total


def feed_back(spot, low, turned, acc, blocks, plan, adds=()):
    rows, model = low.shape
    hidden = blocks[0][2].shape[1]
    grads = grad_shapes(model, hidden, plan)
    flat = [one for block in blocks for one in block]
    return pl.pallas_call(
        functools.partial(feed_back_kernel, plan, len(adds)),
        out_shape=grads
        + (jax.ShapeDtypeStruct((rows, model), F32),)
        + (jax.ShapeDtypeStruct((8, hidden), F32),) * 2,
        in_specs=[SMEM] + [VMEM] * (9 + len(adds)),
        out_specs=(VMEM,) * (3 + len(grads)),
        scratch_shapes=[pltpu.VMEM((model, hidden), F32), pltpu.VMEM((rows, hidden), BF16)],
        compiler_params=params(),
        cost_estimate=COST if adds else LONG,
        name="feed_back",
    )(spot, low, turned, acc, *flat, *adds)


def after(value, *others):
    return lax.optimization_barrier((value, *others))[0]


def swap(value, axis, size, step):
    return lax.ppermute(value, axis, [(i, i ^ step) for i in range(size)])


def add_kernel(plan, *refs):
    outs = refs[len(refs) - len(plan) :]
    for out_ref, terms in zip(outs, plan):
        total = None
        for n, place in terms:
            value = (refs[n][...] if place is None else refs[n][place]).astype(F32)
            total = value if total is None else total + value
        out_ref[...] = total.astype(BF16)


def add(sums, long=False):
    arrays, plan, shapes = [], [], []
    for terms in sums:
        row = []
        for term in terms:
            value, place = term if isinstance(term, tuple) else (term, None)
            known = [n for n, one in enumerate(arrays) if one is value]
            if not known:
                arrays.append(value)
            row.append((known[0] if known else len(arrays) - 1, place))
        value, place = arrays[row[0][0]], row[0][1]
        shape = value.shape
        if isinstance(place, int):
            shape = shape[1:]
        elif place is not None:
            shape = (place.stop - place.start, *shape[1:])
        plan.append(row)
        shapes.append(jax.ShapeDtypeStruct(shape, BF16))
    return pl.pallas_call(
        functools.partial(add_kernel, plan),
        out_shape=tuple(shapes),
        in_specs=[VMEM] * len(arrays),
        out_specs=(VMEM,) * len(shapes),
        compiler_params=params(),
        cost_estimate=LONG if long else COST,
        name="add",
    )(*arrays)


class Line:
    def __init__(self):
        self.last = None

    def __call__(self, value):
        return value if self.last is None else after(value, self.last)

    def done(self, value):
        self.last = value
        return value

    def adds(self, *sums, long=False):
        first = sums[0][0]
        value, place = first if isinstance(first, tuple) else (first, None)
        tied = self(value)
        sums = [
            [
                (tied, term[1]) if isinstance(term, tuple) and term[0] is value
                else tied if term is value
                else term
                for term in terms
            ]
            for terms in sums
        ]
        outs = add(sums, long)
        self.done(outs[0])
        return outs

    def add(self, *terms):
        return self.adds(terms)[0]


class Group:
    def __init__(self, dp, tensor):
        if dp < 8 or dp & (dp - 1):
            raise ValueError("dp size")
        self.dp, self.tensor = dp, tensor
        self.place = lax.axis_index("dp")

    def core(self, value):
        return swap(value, "tensor", self.tensor, 1)

    def across(self, value):
        return swap(value, "tensor", self.tensor, 2)

    def over(self, number, value):
        return swap(value, "dp", self.dp, 2**number)

    def rest(self, value, line):
        number = 3
        while 2**number < self.dp:
            value = line.add(value, self.over(number, value))
            number += 1
        return value


def local(
    inputs,
    lengths,
    weight_query,
    bias_query,
    weight_key,
    weight_value,
    bias_value,
    weight_out,
    bias_out,
    weight_in,
    bias_in,
    weight_down,
    bias_down,
    first_gain,
    first_shift,
    second_gain,
    second_shift,
    cotangent,
):
    group = Group(lax.axis_size("dp"), lax.axis_size("tensor"))
    core, across, over = group.core, group.across, group.over
    width = weight_query.shape[1]
    seq = lax.axis_index("tensor").reshape(1)
    spot = group.place.reshape(1)
    scalars = (lengths, seq, spot)
    line = Line()

    pack, pack_0, pack_3 = prepare_pack(
        spot, weight_query, weight_key, weight_value, weight_out, bias_query, bias_value, bias_in
    )
    line.done(pack_0)
    far_0 = across(pack_0)
    pack_twin = core(pack)
    win_0, win_3, wd_0, wd_3 = prepare_feed(line(spot), weight_in, weight_down)
    line.done(win_0)
    kept = [None] * 4
    kept[0] = attend_forward(scalars, line(inputs), [pack])
    line.done(kept[0][4])
    far_3 = across(line(pack_3))
    kept[1] = attend_forward(scalars, line(inputs), [pack_twin])
    line.done(kept[1][4])
    far_0 = line.done(line(far_0))
    far_1, far_2 = over(1, far_0), over(0, far_0)
    win_0 = across(after(win_0, far_0))
    far_3 = line.done(line(far_3))
    far_parts = [far_0, far_1, far_2, far_3]
    pack_twin = [core(one) for one in far_parts]
    kept[2] = attend_forward(scalars, line(inputs), far_parts)
    line.done(kept[2][4])
    wd_0 = across(after(wd_0, kept[2][4]))
    win_0 = line.done(line(win_0))
    win_1, win_2 = over(1, win_0), over(0, win_0)
    win_3 = across(after(win_3, win_0))
    kept[3] = attend_forward(scalars, line(inputs), pack_twin)
    line.done(kept[3][4])
    win_twin = core(after(weight_in, kept[2][4]))
    z, low, turned, rstd = first_norm(
        line(inputs),
        (bias_out, first_gain, first_shift),
        [one[4] for one in kept],
        [one[0] for one in kept],
    )
    line.done(low)
    acts, slopes = [None] * 4, [None] * 4
    acts[0], slopes[0], acts[1], slopes[1] = feed_up(
        spot, line(low), [weight_in, win_twin], [kept[0][5], kept[1][5]]
    )
    line.done(acts[0])
    wd_0 = line.done(line(wd_0))
    wd_1, wd_2 = over(1, wd_0), over(0, wd_0)
    wd_3 = across(after(wd_3, wd_0))
    wd_twin = core(after(weight_down, kept[3][4]))
    win_far, acts[2], slopes[2] = feed_up(
        spot, line(low), [win_0, win_1, win_2, win_3], [kept[2][5]]
    )
    line.done(acts[2])
    wins = [weight_in, win_twin, win_far, core(win_far)]
    wd_parts = [wd_0, wd_1, wd_2, wd_3]
    *near, feed = feed_down(spot, [line(acts[0]), acts[1]], [[weight_down], [wd_twin]])
    line.done(feed)
    wd_twin = [core(one) for one in wd_parts]
    acts[3], slopes[3] = feed_up(spot, line(low), [wins[3]], [kept[3][5]])
    line.done(acts[3])
    *far, feed = feed_down(spot, [line(acts[2]), acts[3]], [wd_parts, wd_twin], feed)
    wds = near + far
    results, grad_second, second_low, second_sums = second_norm(
        z, feed, cotangent, (first_gain, first_shift, bias_down, second_gain, second_shift)
    )
    line.done(second_low)

    def down(pair, plan, adds=()):
        grads = down_back(spot, [acts[r] for r in pair], line(second_low), plan, adds)
        line.done(grads[0])
        return grads

    db = [None] * 4

    def back(pair, acc, plan, adds=()):
        blocks = [(wds[r], slopes[r], wins[r]) for r in pair]
        *grads, acc, db[pair[0]], db[pair[1]] = feed_back(
            spot, line(second_low), turned, acc, blocks, plan, adds
        )
        line.done(acc)
        return grads, acc

    (down_twin,) = down((3, 1), TOGETHER)
    down_twin = core(down_twin)
    (win_twin,), dn = back((3, 1), grad_second, TOGETHER)
    win_twin = core(win_twin)
    far_keep, far_send, near_keep, near_send = down((2, 0), EARLY, [down_twin])
    far_moved, near_moved = over(1, far_send), over(0, near_send)
    (win_321, win_0, win_near), dn = back((2, 0), dn, LATE, [win_twin])
    win_321, win_0 = across(win_321), across(win_0)
    grad_first, first_low, first_sums = first_back(line(z), rstd, dn, first_gain)
    line.done(first_low)
    gs = [None] * 4

    def attention_back(blocks, split=False, adds=()):
        outs = attend_backward(
            spot,
            inputs,
            line(first_low),
            [db[r] for r in blocks],
            first_sums,
            second_sums,
            [kept[r][:5] for r in blocks],
            split,
            adds,
        )
        for r, one in zip(blocks, outs[-len(blocks) :]):
            gs[r] = one
        line.done(gs[blocks[-1]])
        return outs[: -len(blocks)]

    (pack_twin,) = attention_back((3, 1))
    pack_twin = core(pack_twin)

    def input_part(acc, pair):
        part = input_grad(line(acc), [gs[r] for r in pair], [kept[r][0] for r in pair])
        return line.done(part)

    down_f2, down_n1 = line.adds(
        [(far_keep, 1), (far_moved, 1)], [(near_keep, 1), (near_moved, 1)]
    )
    down_fx, down_nz = over(0, down_f2), over(1, down_n1)
    dx = input_part(grad_first, (3, 1))
    down_f0, down_0, win_s, win_1 = line.adds(
        [(far_keep, 0), (far_moved, 0), down_fx],
        [(near_keep, 0), (near_moved, 0), down_nz],
        [(win_near, slice(2, 4)), (win_321, slice(0, 2))],
        [(win_near, 1), (win_321, 2)],
        long=True,
    )
    down_y, win_x = across(down_f0), over(0, win_s)
    pack_0, pack_321 = attention_back((2,), True, [pack_twin])
    pack_321 = across(pack_321)
    (pack_near,) = attention_back((0,), False, [pack_twin])
    down_0, win_1, win_0 = line.adds(
        [down_0, down_y],
        [win_1, (win_x, 1)],
        [(win_near, 0), (win_0, 0), (win_x, 0)],
    )
    down_far, win_z = over(2, down_0), over(1, win_1)
    pack_0 = across(after(pack_0, down_0))
    dx = input_part(dx, (2, 0))
    win_0 = line.add(win_0, win_z)
    win_far = over(2, win_0)
    pack_s = line.add((pack_near, slice(2, 4)), (pack_321, slice(0, 2)))
    pack_x = over(0, pack_s)
    down_0 = group.rest(line.add(down_0, down_far), line)
    down_1, down_2 = over(1, down_0), over(0, down_0)
    down_1 = line.done(line(down_1))
    down_3 = over(0, down_1)
    pack_1, pack_0 = line.adds(
        [(pack_near, 1), (pack_321, 2), (pack_x, 1)], [(pack_near, 0), pack_0, (pack_x, 0)]
    )
    pack_z = over(1, pack_1)
    win_0 = group.rest(line.add(win_0, win_far), line)
    pack_0 = line.add(pack_0, pack_z)
    pack_far = over(2, pack_0)
    win_1, win_2 = over(1, after(win_0, pack_0)), over(0, after(win_0, pack_0))
    grad_weight_down = finish_block(line(spot), [down_0, down_1, down_2, down_3])
    line.done(grad_weight_down)
    win_2 = line.done(line(win_2))
    win_3 = over(1, win_2)
    win_1 = line.done(line(win_1))
    pack_0 = group.rest(line.add(pack_0, pack_far), line)
    pack_1, pack_2 = over(1, pack_0), over(0, pack_0)
    grad_weight_in = finish_block(line(spot), [win_0, win_1, win_2, win_3])
    line.done(grad_weight_in)
    parts = [pack_0, pack_1, pack_2, over(0, pack_1)]
    grad_q, grad_k, grad_v, grad_o, extra = finish_pack(line(spot), parts, width)
    return (
        results,
        dx,
        grad_q.T,
        extra[0, :width],
        grad_k.T,
        grad_v.T,
        extra[0, 2 * width : 3 * width],
        grad_o,
        extra[4],
        grad_weight_in,
        extra[1],
        grad_weight_down,
        extra[7],
        extra[3],
        extra[2],
        extra[6],
        extra[5],
    )


def solution(mesh):
    in_specs = (
        P(("dp", "tensor"), None),
        P("dp"),
        P(None, "tensor"),
        P("tensor"),
        P(None, "tensor"),
        P(None, "tensor"),
        P("tensor"),
        P("tensor", None),
        P(),
        P(None, "tensor"),
        P("tensor"),
        P("tensor", None),
        P(),
        P(),
        P(),
        P(),
        P(),
        P(("dp", "tensor"), None),
    )
    out_specs = (
        P(("dp", "tensor"), None),
        P(("dp", "tensor"), None),
        P(None, "tensor"),
        P("tensor"),
        P(None, "tensor"),
        P(None, "tensor"),
        P("tensor"),
        P("tensor", None),
        P(),
        P(None, "tensor"),
        P("tensor"),
        P("tensor", None),
        P(),
        P(),
        P(),
        P(),
        P(),
    )
    return jax.shard_map(local, mesh=mesh, in_specs=in_specs, out_specs=out_specs, check_vma=False)
```

```python
import functools
import math

import jax
import jax.numpy as jnp
from jax import lax
from jax.experimental import pallas as pl
from jax.experimental.pallas import tpu as pltpu
from jax.sharding import PartitionSpec as P

HEAD = 64
SEQ_LEN = 512
UP_ROWS = 128
F32 = jnp.float32
BF16 = jnp.bfloat16
VMEM_LIMIT = 24 * 1024 * 1024
VMEM = pl.BlockSpec(memory_space=pltpu.VMEM)
COST = pl.CostEstimate(flops=10**9, bytes_accessed=10**9, transcendentals=0)
MIDDLE = pl.CostEstimate(flops=10**10, bytes_accessed=10**9, transcendentals=0)
LONG = pl.CostEstimate(flops=10**11, bytes_accessed=10**9, transcendentals=0)
SMEM = pl.BlockSpec(memory_space=pltpu.SMEM)
HBM = pl.BlockSpec(memory_space=pltpu.HBM)


def hbm(shape, dtype=BF16):
    return pltpu.HBM(shape, dtype)


def pinned(value):
    return pltpu.with_memory_space_constraint(value, pltpu.HBM)


def dot(left, right, left_dim, right_dim):
    return lax.dot_general(
        left, right, (((left_dim,), (right_dim,)), ((), ())), preferred_element_type=F32
    )


def params(**kwargs):
    return pltpu.CompilerParams(vmem_limit_bytes=VMEM_LIMIT, **kwargs)


def whole(shape, index=None):
    place = index or (0,) * len(shape)
    return pl.BlockSpec(shape, lambda *_: place)


def row(ref):
    return ref[...].astype(F32).reshape(1, ref.shape[0])


def pack_rows(width):
    return (4 * width + 16 + 63) // 64 * 64


def bit(spot_ref, number):
    return lax.rem(lax.div(spot_ref[0], 2**number), 2)


def window(choice, size, tile):
    return pl.ds(pl.multiple_of(choice * size, tile), size)


def head_rows(start, h):
    return pl.ds(pl.multiple_of(start + h * HEAD, HEAD), HEAD)


def quarter(spot_ref, r, size):
    first = lax.rem(bit(spot_ref, 0) + r // 2, 2)
    second = lax.rem(bit(spot_ref, 1) + r % 2, 2)
    return window(2 * first + second, size, 16)


def run(copies):
    for one in copies:
        one.start()
    for one in copies:
        one.wait()


def prepare_pack_kernel(spot_ref, q_ref, k_ref, v_ref, out_ref, bq_ref, bv_ref, bin_ref, *refs):
    full_ref, first_ref, last_ref, held_ref, extra_ref, bq, bv, bin_, sems = refs
    width = out_ref.shape[0]
    copies = [
        pltpu.make_async_copy(ref, held_ref.at[pl.ds(i * width, width), :], sems.at[i])
        for i, ref in enumerate((q_ref, k_ref, v_ref, out_ref))
    ]
    vectors = [
        pltpu.make_async_copy(ref, to, sems.at[4 + i])
        for i, (ref, to) in enumerate(((bq_ref, bq), (bv_ref, bv), (bin_ref, bin_)))
    ]
    for one in vectors + copies:
        one.start()
    extra_ref[...] = jnp.zeros_like(extra_ref)
    for one in vectors:
        one.wait()
    extra_ref[0, :width] = bq[...].astype(F32)
    extra_ref[0, 2 * width : 3 * width] = bv[...].astype(F32)
    extra_ref[1, :] = bin_[...].astype(F32)
    held_ref[4 * width :, :] = extra_ref[...].astype(BF16)
    for one in copies:
        one.wait()
    size = first_ref.shape[0]
    run(
        [
            pltpu.make_async_copy(held_ref.at[quarter(spot_ref, 0, size), :], first_ref, sems.at[0]),
            pltpu.make_async_copy(held_ref.at[quarter(spot_ref, 3, size), :], last_ref, sems.at[1]),
            pltpu.make_async_copy(held_ref, full_ref, sems.at[2]),
        ]
    )


def prepare_pack(spot, wq, wk, wv, wout, bq, bv, bin_):
    width, model = wout.shape
    rows = pack_rows(width)
    return pl.pallas_call(
        prepare_pack_kernel,
        out_shape=(hbm((rows, model)), hbm((rows // 4, model)), hbm((rows // 4, model))),
        in_specs=[SMEM] + [HBM] * 7,
        out_specs=(HBM,) * 3,
        scratch_shapes=[
            pltpu.VMEM((rows, model), BF16),
            pltpu.VMEM((rows - 4 * width, model), F32),
            pltpu.VMEM(bq.shape, BF16),
            pltpu.VMEM(bv.shape, BF16),
            pltpu.VMEM(bin_.shape, BF16),
            pltpu.SemaphoreType.DMA((7,)),
        ],
        compiler_params=params(),
        name="prepare_pack",
    )(spot, *(pinned(one) for one in (wq.T, wk.T, wv.T, wout, bq, bv, bin_)))


def prepare_feed_kernel(spot_ref, win_ref, wd_ref, *refs):
    outs, held, sems = refs[:4], refs[4:8], refs[8]
    size = outs[0].shape[0]
    loads = []
    for i in range(4):
        source = (win_ref, wd_ref)[i // 2].at[quarter(spot_ref, 3 * (i % 2), size), :]
        loads.append(pltpu.make_async_copy(source, held[i], sems.at[i]))
        loads[i].start()
    stores = []
    for i in range(4):
        loads[i].wait()
        stores.append(pltpu.make_async_copy(held[i], outs[i], sems.at[i]))
        stores[i].start()
    for one in stores:
        one.wait()


def prepare_feed(spot, win, wd):
    size, model = win.shape[0] // 4, win.shape[1]
    return pl.pallas_call(
        prepare_feed_kernel,
        out_shape=(hbm((size, model)),) * 4,
        in_specs=[SMEM, HBM, HBM],
        out_specs=(HBM,) * 4,
        scratch_shapes=[pltpu.VMEM((size, model), BF16)] * 4 + [pltpu.SemaphoreType.DMA((4,))],
        compiler_params=params(),
        name="prepare_feed",
    )(spot, pinned(win), pinned(wd))


def finish_pack_kernel(spot_ref, *refs):
    parts, (q_ref, k_ref, v_ref, out_ref), refs = refs[:4], refs[4:8], refs[8:]
    (bq_ref, bv_ref, *vectors), (held_ref, extra_ref) = refs[:-2], refs[-2:]
    size = parts[0].shape[0]
    width = q_ref.shape[0]
    for r in range(4):
        held_ref[quarter(spot_ref, r, size), :] = parts[r][...]
    for i, ref in enumerate((q_ref, k_ref, v_ref, out_ref)):
        ref[...] = held_ref[i * width : (i + 1) * width, :].astype(F32)
    extra_ref[...] = held_ref[4 * width : 4 * width + 16, :].astype(F32)
    bq_ref[...] = extra_ref[0, :width]
    bv_ref[...] = extra_ref[0, 2 * width : 3 * width]
    for i, ref in enumerate(vectors):
        ref[...] = extra_ref[1 + i, :]


def finish_pack(spot, parts, width):
    size, model = parts[0].shape
    one = jax.ShapeDtypeStruct((width, model), F32)
    vector = jax.ShapeDtypeStruct((model,), F32)
    return pl.pallas_call(
        finish_pack_kernel,
        out_shape=(one,) * 4 + (jax.ShapeDtypeStruct((width,), F32),) * 2 + (vector,) * 7,
        in_specs=[SMEM] + [VMEM] * 4,
        out_specs=(VMEM,) * 13,
        scratch_shapes=[pltpu.VMEM((4 * size, model), BF16), pltpu.VMEM((16, model), F32)],
        compiler_params=params(),
        cost_estimate=COST,
        name="finish_pack",
    )(spot, *parts)


def finish_block_kernel(spot_ref, *refs):
    for r in range(4):
        refs[4][quarter(spot_ref, r, refs[r].shape[0]), :] = refs[r][...].astype(F32)


def finish_block(spot, parts):
    size, model = parts[0].shape
    return pl.pallas_call(
        finish_block_kernel,
        out_shape=jax.ShapeDtypeStruct((4 * size, model), F32),
        in_specs=[SMEM] + [VMEM] * 4,
        out_specs=VMEM,
        compiler_params=params(),
        cost_estimate=COST,
        name="finish_block",
    )(spot, *parts)


def attend_forward_kernel(pieces, length_ref, seq_ref, spot_ref, x_ref, *refs):
    parts, refs = refs[:pieces], refs[pieces:]
    if pieces > 1:
        pack_out, *refs, pack_ref = refs
    else:
        pack_ref = parts[0]
    qkv_out, e_out, r_out, att_out, bias_out, qkv_ref, e_ref, r_ref, att_ref, sems = refs
    width = att_ref.shape[0]
    heads = width // HEAD
    if pieces == 1:
        bias_out[...] = pack_ref[4 * width : 4 * width + 16, :]
    scale = math.log2(math.e) / math.sqrt(HEAD)
    copies = []

    def store(source, target, sem):
        copies.append(pltpu.make_async_copy(source, target, sems.at[sem]))
        copies[-1].start()

    if pieces > 1:
        size = parts[0].shape[0]
        for r in range(4):
            pack_ref[quarter(spot_ref, r, size), :] = parts[r][...]
        store(pack_ref, pack_out, heads)
        bias_out[...] = pack_ref[4 * width : 4 * width + 16, :]
    bias = jnp.transpose(pack_ref[4 * width : 4 * width + 16, :].astype(F32))[: 3 * width, 0:1]
    projected = dot(pack_ref[: 3 * width, :], x_ref[...], 1, 1) + bias
    qkv_ref[...] = projected.astype(BF16)
    store(qkv_ref, qkv_out, heads + 1)
    visible = lax.broadcasted_iota(jnp.int32, (SEQ_LEN, 1), 0) < length_ref[seq_ref[0]]

    @pl.loop(0, heads)
    def _(h):
        q, k, v = (qkv_ref[head_rows(i * width, h), :] for i in range(3))
        scores = jnp.where(visible, dot(k, q, 0, 0) * scale, -1e30)
        highest = jnp.max(scores, axis=0, keepdims=True)
        e = jnp.exp2(scores - highest)
        r = 1.0 / jnp.sum(e, axis=0, keepdims=True)
        low = e.astype(BF16)
        e_ref[h] = low
        pltpu.make_async_copy(e_ref.at[h], e_out.at[h], sems.at[h]).start()
        r_ref[h] = jnp.broadcast_to(r, r_ref.shape[1:])
        att_ref[head_rows(0, h), :] = (dot(v, low, 1, 0) * r).astype(BF16)

    copies.extend(
        pltpu.make_async_copy(e_ref.at[h], e_out.at[h], sems.at[h]) for h in range(heads)
    )
    store(r_ref, r_out, heads + 2)
    store(att_ref, att_out, heads + 3)
    for one in copies:
        one.wait()


def attend_forward(scalars, x, parts):
    rows, model = x.shape
    width = model // 4
    heads = width // HEAD
    pieces = len(parts)
    full = hbm((pieces * parts[0].shape[0], model))
    held = [
        hbm((3 * width, rows)),
        hbm((heads, rows, rows)),
        hbm((heads, 8, rows), F32),
        hbm((width, rows)),
    ]
    more = [full] if pieces > 1 else []
    outs = pl.pallas_call(
        functools.partial(attend_forward_kernel, pieces),
        out_shape=(*more, *held, jax.ShapeDtypeStruct((16, model), BF16)),
        in_specs=[SMEM] * 3 + [VMEM] * (1 + pieces),
        out_specs=(HBM,) * (len(more) + 4) + (VMEM,),
        scratch_shapes=[pltpu.VMEM(one.shape, one.dtype) for one in held]
        + [pltpu.SemaphoreType.DMA((heads + 4,))]
        + [pltpu.VMEM(one.shape, one.dtype) for one in more],
        compiler_params=params(),
        cost_estimate=MIDDLE,
        name="attend_forward",
    )(*scalars, x, *parts)
    return outs if more else (parts[0], *outs)


def attend_backward_kernel(count, plus, split, first, spot_ref, x_ref, bg_ref, *refs):
    dbs, (first_ref, second_ref), refs = refs[:count], refs[count : count + 2], refs[count + 2 :]
    saved, refs = refs[: 5 * count], refs[5 * count :]
    add_in, refs = refs[:plus], refs[plus:]
    outs, refs = refs[: 1 + split], refs[1 + split :]
    g_outs, refs = refs[:count], refs[count:]
    held, (extra_ref, up_ref, sems) = refs[: 7 * count], refs[7 * count : 7 * count + 3]
    factor = 1.0 / math.sqrt(HEAD)

    def move(source, target, *sem):
        copy = pltpu.make_async_copy(source, target, sems.at[sem])
        copy.start()
        return copy

    loads = []
    for n in range(count):
        pack_in, qkv_in, e_in, r_in, att_in = saved[5 * n : 5 * n + 5]
        qkv_ref, e_ref, r_ref, att_ref, wout_ref = held[7 * n : 7 * n + 5]
        width = att_ref.shape[0]
        heads = width // HEAD
        one = [
            move(pack_in.at[pl.ds(3 * width, width), :], wout_ref, n, 0),
            move(qkv_in, qkv_ref, n, 1),
            move(r_in, r_ref, n, 2),
            move(att_in, att_ref, n, 3),
        ]
        loads.append(one + [move(e_in.at[h], e_ref.at[h], n, 4 + h) for h in range(heads)])
    stores = []
    for n in range(count):
        e_in = saved[5 * n + 2]
        qkv_ref, e_ref, r_ref, att_ref, wout_ref, g_ref, held_ref = held[7 * n : 7 * n + 7]
        size = held_ref.shape[0] // 4
        extra_ref[...] = jnp.zeros_like(extra_ref)
        extra_ref[1:2, :] = dbs[n][0:1, :]
        extra_ref[2:5, :] = first_ref[0:3, :]
        extra_ref[5:8, :] = second_ref[0:3, :]
        loads[n][0].wait()
        up_ref[...] = dot(wout_ref[...], bg_ref[...], 1, 1).astype(BF16)
        for one in loads[n][1:4]:
            one.wait()

        @pl.loop(0, heads)
        def _(h):
            q, k, v = (qkv_ref[head_rows(i * width, h), :] for i in range(3))
            scaled = up_ref[head_rows(0, h), :].astype(F32) * r_ref[h, 0:1, :]
            attended = att_ref[head_rows(0, h), :].astype(F32)
            inner = jnp.sum(attended * scaled, axis=0, keepdims=True)
            do = scaled.astype(BF16)
            pltpu.make_async_copy(e_in.at[h], e_ref.at[h], sems.at[n, 4 + h]).wait()
            e = e_ref[h]
            ds = (e.astype(F32) * (dot(v, do, 0, 0) - inner)).astype(BF16)
            g_ref[head_rows(0, h), :] = (dot(k, ds, 1, 0) * factor).astype(BF16)
            g_ref[head_rows(width, h), :] = (dot(q, ds, 1, 1) * factor).astype(BF16)
            g_ref[head_rows(2 * width, h), :] = dot(do, e, 1, 1).astype(BF16)

        stores.append(move(g_ref, g_outs[n], n, 0))
        g = g_ref[...]
        extra_ref[0:1, : 3 * width] = dot(jnp.ones((8, g.shape[1]), BF16), g, 1, 1)[0:1, :]
        held_ref[4 * width :, :] = extra_ref[...].astype(BF16)
        held_ref[: 3 * width, :] = dot(g, x_ref[...], 1, 0).astype(BF16)
        held_ref[3 * width : 4 * width, :] = dot(att_ref[...], bg_ref[...], 1, 0).astype(BF16)
        for r in range(4):
            if plus:
                part = quarter(spot_ref, r, size)
                value = held_ref[part, :].astype(F32) + add_in[0][first + r].astype(F32)
                held_ref[part, :] = value.astype(BF16)
            if len(outs) == 1:
                target = outs[0].at[4 * n + r]
            else:
                target = outs[1].at[(0, 2, 0, 1)[r]] if r else outs[0]
            stores.append(
                move(held_ref.at[quarter(spot_ref, r, size), :], target, n, 4 + heads + r)
            )
    for one in stores:
        one.wait()


def attend_backward(spot, x, bg, dbs, first, second, saved, split=False, adds=()):
    rows, model = x.shape
    width = model // 4
    heads = width // HEAD
    count = len(dbs)
    full = saved[0][0].shape[0]
    more = list(adds)
    if split:
        grads = (hbm((full // 4, model)), hbm((3, full // 4, model)))
    else:
        grads = (hbm((4 * count, full // 4, model)),)
    flat = [pinned(one) for block in saved for one in block]
    return pl.pallas_call(
        functools.partial(attend_backward_kernel, count, len(more), split, 0 if split else 4),
        out_shape=grads + (hbm((3 * width, rows)),) * count,
        in_specs=[SMEM] + [VMEM] * (4 + count) + [HBM] * (5 * count) + [VMEM] * len(more),
        out_specs=(HBM,) * (len(grads) + count),
        scratch_shapes=[
            pltpu.VMEM((3 * width, rows), BF16),
            pltpu.VMEM((heads, rows, rows), BF16),
            pltpu.VMEM((heads, 8, rows), F32),
            pltpu.VMEM((width, rows), BF16),
            pltpu.VMEM((width, model), BF16),
            pltpu.VMEM((3 * width, rows), BF16),
            pltpu.VMEM((full, model), BF16),
        ]
        * count
        + [
            pltpu.VMEM((full - 4 * width, model), F32),
            pltpu.VMEM((width, rows), BF16),
            pltpu.SemaphoreType.DMA((count, 8 + heads)),
        ],
        compiler_params=params(),
        cost_estimate=COST if count > 1 else MIDDLE,
        name="attend_backward",
    )(spot, x, bg, *dbs, first, second, *flat, *more)


def input_grad_kernel(count, acc_ref, *refs):
    gs, packs, out_ref, sems = refs[:count], refs[count : 2 * count], refs[2 * count], refs[-1]
    held_g, held_w = refs[2 * count + 1 : 3 * count + 1], refs[3 * count + 1 : 4 * count + 1]
    width = held_w[0].shape[0]
    loads = []
    for i in range(count):
        loads.append(pltpu.make_async_copy(gs[i], held_g[i], sems.at[2 * i]))
        loads.append(
            pltpu.make_async_copy(packs[i].at[pl.ds(0, width), :], held_w[i], sems.at[2 * i + 1])
        )
    for one in loads:
        one.start()
    total = acc_ref[...]
    for i in range(count):
        loads[2 * i].wait()
        loads[2 * i + 1].wait()
        total = total + dot(held_g[i][...], held_w[i][...], 0, 0)
    out_ref[...] = total


def input_grad(acc, gs, packs):
    rows, model = acc.shape
    width, count = gs[0].shape[0], len(gs)
    return pl.pallas_call(
        functools.partial(input_grad_kernel, count),
        out_shape=jax.ShapeDtypeStruct((rows, model), F32),
        in_specs=[VMEM] + [HBM] * (2 * count),
        out_specs=VMEM,
        scratch_shapes=[pltpu.VMEM((width, rows), BF16)] * count
        + [pltpu.VMEM((width, model), BF16)] * count
        + [pltpu.SemaphoreType.DMA((2 * count,))],
        compiler_params=params(),
        cost_estimate=COST,
        name="input_grad",
    )(acc, *(pinned(one) for one in gs), *(pinned(one) for one in packs))


def first_norm_kernel(x_ref, bias_ref, gain_ref, shift_ref, *refs):
    atts, packs, refs = refs[:4], refs[4:8], refs[8:]
    z_ref, low_ref, turned_ref, rstd_ref = refs[:4]
    held_a, held_w, sems = refs[4], refs[5], refs[6]
    width = atts[0].shape[0]
    loads = []
    for i in range(4):
        part = pl.ds(i * width, width)
        loads.append(pltpu.make_async_copy(atts[i], held_a.at[part, :], sems.at[2 * i]))
        loads.append(
            pltpu.make_async_copy(
                packs[i].at[pl.ds(3 * width, width), :], held_w.at[part, :], sems.at[2 * i + 1]
            )
        )
    run(loads)
    branch = dot(held_a[...], held_w[...], 0, 0)
    total = x_ref[...].astype(F32) + branch + row(bias_ref)
    center = total - jnp.mean(total, axis=1, keepdims=True)
    rstd = lax.rsqrt(jnp.mean(center * center, axis=1, keepdims=True) + 1e-12)
    z = center * rstd
    z_ref[...] = z
    rstd_ref[...] = rstd
    normed = (z * row(gain_ref) + row(shift_ref)).astype(BF16)
    low_ref[...] = normed
    turned_ref[...] = jnp.transpose(normed)


def first_norm(x, vectors, atts, packs):
    rows, model = x.shape
    return pl.pallas_call(
        first_norm_kernel,
        out_shape=(
            jax.ShapeDtypeStruct((rows, model), F32),
            jax.ShapeDtypeStruct((rows, model), BF16),
            jax.ShapeDtypeStruct((model, rows), BF16),
            jax.ShapeDtypeStruct((rows, 1), F32),
        ),
        in_specs=[VMEM] * 4 + [HBM] * 8,
        out_specs=(VMEM,) * 4,
        scratch_shapes=[
            pltpu.VMEM((model, rows), BF16),
            pltpu.VMEM((model, model), BF16),
            pltpu.SemaphoreType.DMA((8,)),
        ],
        compiler_params=params(),
        cost_estimate=MIDDLE,
        name="first_norm",
    )(x, *vectors, *(pinned(one) for one in atts), *(pinned(one) for one in packs))


def second_norm_kernel(z_ref, feed_ref, c_ref, *refs):
    gain1, shift1, bias, gain2, shift2 = (row(ref) for ref in refs[:5])
    out_ref, grad_ref, low_ref, sum_ref = refs[5:]
    total = z_ref[...] * gain1 + shift1 + feed_ref[...] + bias
    center = total - jnp.mean(total, axis=1, keepdims=True)
    rstd = lax.rsqrt(jnp.mean(center * center, axis=1, keepdims=True) + 1e-12)
    z = center * rstd
    out_ref[...] = (z * gain2 + shift2).astype(BF16)
    c = c_ref[...].astype(F32)
    e = c * gain2
    grad = (
        e - jnp.mean(e, axis=1, keepdims=True) - z * jnp.mean(e * z, axis=1, keepdims=True)
    ) * rstd
    grad_ref[...] = grad
    low_ref[...] = grad.astype(BF16)

    @pl.when(pl.program_id(0) == 0)
    def _():
        sum_ref[...] = jnp.zeros_like(sum_ref)

    sum_ref[0:1, :] += jnp.sum(c, axis=0, keepdims=True)
    sum_ref[1:2, :] += jnp.sum(c * z, axis=0, keepdims=True)
    sum_ref[2:3, :] += jnp.sum(grad, axis=0, keepdims=True)


def second_norm(z, feed, c, vectors):
    rows, model = z.shape
    step = rows // 4
    block = pl.BlockSpec((step, model), lambda i: (i, 0))
    return pl.pallas_call(
        second_norm_kernel,
        grid=(4,),
        out_shape=(
            jax.ShapeDtypeStruct((rows, model), BF16),
            jax.ShapeDtypeStruct((rows, model), F32),
            jax.ShapeDtypeStruct((rows, model), BF16),
            jax.ShapeDtypeStruct((8, model), F32),
        ),
        in_specs=[block] * 3 + [VMEM] * 5,
        out_specs=(block, block, block, whole((8, model))),
        compiler_params=params(),
        cost_estimate=COST,
        name="second_norm",
    )(z, feed, c, *vectors)


def first_back_kernel(z_ref, rstd_ref, dn_ref, gain_ref, grad_ref, low_ref, sum_ref):
    z = z_ref[...]
    dn = dn_ref[...]
    f = dn * row(gain_ref)
    grad = (
        f - jnp.mean(f, axis=1, keepdims=True) - z * jnp.mean(f * z, axis=1, keepdims=True)
    ) * rstd_ref[...]
    grad_ref[...] = grad
    low_ref[...] = grad.astype(BF16)

    @pl.when(pl.program_id(0) == 0)
    def _():
        sum_ref[...] = jnp.zeros_like(sum_ref)

    sum_ref[0:1, :] += jnp.sum(dn, axis=0, keepdims=True)
    sum_ref[1:2, :] += jnp.sum(dn * z, axis=0, keepdims=True)
    sum_ref[2:3, :] += jnp.sum(grad, axis=0, keepdims=True)


def first_back(z, rstd, dn, gain):
    rows, model = z.shape
    step = rows // 4
    block = pl.BlockSpec((step, model), lambda i: (i, 0))
    return pl.pallas_call(
        first_back_kernel,
        grid=(4,),
        out_shape=(
            jax.ShapeDtypeStruct((rows, model), F32),
            jax.ShapeDtypeStruct((rows, model), BF16),
            jax.ShapeDtypeStruct((8, model), F32),
        ),
        in_specs=[block, pl.BlockSpec((step, 1), lambda i: (i, 0)), block, VMEM],
        out_specs=(block, block, whole((8, model))),
        compiler_params=params(),
        cost_estimate=COST,
        name="first_back",
    )(z, rstd, dn, gain)


def feed_up_kernel(pieces, count, spot_ref, low_ref, *refs):
    biases, parts, refs = refs[:count], refs[count : count + pieces], refs[count + pieces :]
    if pieces > count:
        win_ref, *refs = refs
        for r in range(4):
            win_ref[quarter(spot_ref, r, parts[r].shape[0]), :] = parts[r][...]
        parts = (win_ref,)
    for n in range(count):
        win_ref, act_ref, slope_ref = parts[n], refs[2 * n], refs[2 * n + 1]
        bias = biases[n][1:2, :].astype(F32)

        @pl.loop(0, low_ref.shape[0] // UP_ROWS)
        def _(i):
            rows = pl.ds(pl.multiple_of(i * UP_ROWS, UP_ROWS), UP_ROWS)
            lifted = dot(low_ref[rows, :], win_ref[...], 1, 0) + bias
            phi_big = 0.5 + 0.5 * lax.erf(lifted * math.sqrt(0.5))
            phi = jnp.exp(-0.5 * lifted * lifted) * (1.0 / math.sqrt(2.0 * math.pi))
            act_ref[rows, :] = (lifted * phi_big).astype(BF16)
            slope_ref[rows, :] = (phi_big + lifted * phi).astype(BF16)


def feed_up(spot, low, parts, biases):
    rows, model = low.shape
    hidden = parts[0].shape[1]
    count = len(biases)
    tall = [jax.ShapeDtypeStruct((model, hidden), BF16)] if len(parts) > count else []
    thin = jax.ShapeDtypeStruct((rows, hidden), BF16)
    return pl.pallas_call(
        functools.partial(feed_up_kernel, len(parts), count),
        out_shape=(*tall, *[thin] * (2 * count)),
        in_specs=[SMEM] + [VMEM] * (1 + count + len(parts)),
        out_specs=(VMEM,) * (2 * count + len(tall)),
        compiler_params=params(),
        cost_estimate=MIDDLE,
        name="feed_up",
    )(spot, low, *biases, *parts)


def feed_down_kernel(pieces, chained, spot_ref, *refs):
    acts, parts, refs = refs[:2], refs[2 : 2 + 2 * pieces], refs[2 + 2 * pieces :]
    if chained:
        acc_ref, *refs = refs
    copies = []
    if pieces > 1:
        *outs, feed_ref, first_ref, second_ref, sems = refs
        wides = (first_ref, second_ref)
        for i in range(2):
            for r, part in enumerate(parts[4 * i : 4 * i + 4]):
                wides[i][quarter(spot_ref, r, part.shape[0]), :] = part[...]
            copies.append(pltpu.make_async_copy(wides[i], outs[i], sems.at[i]))
            copies[-1].start()
    else:
        feed_ref = refs[0]
        wides = parts
    total = dot(acts[0][...], wides[0][...], 1, 0) + dot(acts[1][...], wides[1][...], 1, 0)
    feed_ref[...] = total + acc_ref[...] if chained else total
    for one in copies:
        one.wait()


def feed_down(spot, acts, parts, acc=None):
    rows, hidden = acts[0].shape
    pieces = len(parts[0])
    model = parts[0][0].shape[1]
    more = [] if acc is None else [acc]
    wide = [hbm((hidden, model))] * 2 if pieces > 1 else []
    outs = pl.pallas_call(
        functools.partial(feed_down_kernel, pieces, bool(more)),
        out_shape=(*wide, jax.ShapeDtypeStruct((rows, model), F32)),
        in_specs=[SMEM] + [VMEM] * (2 + 2 * pieces + len(more)),
        out_specs=(HBM,) * len(wide) + (VMEM,),
        scratch_shapes=[pltpu.VMEM(one.shape, one.dtype) for one in wide]
        + ([pltpu.SemaphoreType.DMA((2,))] if wide else []),
        compiler_params=params(),
        cost_estimate=LONG,
        name="feed_down",
    )(spot, *acts, *parts[0], *parts[1], *more)
    return outs if wide else (parts[0][0], parts[1][0], outs[0])


def give_quarters(spot_ref, held_ref, add_ref, first, outs):
    size = held_ref.shape[0] // 4
    for r, (ref, part) in enumerate(outs):
        value = held_ref[quarter(spot_ref, r, size), :]
        if add_ref is not None:
            value = value + add_ref[first + r].astype(F32)
        ref[part] = value.astype(BF16)


TOGETHER = [[(0, r) for r in range(4)], [(0, 4 + r) for r in range(4)]]
LATE = [[(1, 0), (0, 2), (0, 0), (0, 1)], [(2, r) for r in range(4)]]
EARLY = [[(0, 0), (1, 0), (0, 1), (1, 1)], [(2, 0), (2, 1), (3, 0), (3, 1)]]


def grad_shapes(rows, model, plan):
    places = [place for block in plan for place in block]
    return tuple(
        jax.ShapeDtypeStruct((sum(1 for one, _ in places if one == i), rows // 4, model), BF16)
        for i in range(1 + max(one for one, _ in places))
    )


def down_back_kernel(plan, plus, spot_ref, act_a, act_b, low_ref, *refs):
    add_ref, outs, held_ref = (refs[0] if plus else None), refs[plus:-1], refs[-1]
    for n, act_ref in enumerate((act_a, act_b)):
        held_ref[...] = dot(act_ref[...], low_ref[...], 0, 0)
        give_quarters(spot_ref, held_ref, add_ref, 4 * n, [(outs[i], p) for i, p in plan[n]])


def down_back(spot, acts, low, plan, adds=()):
    rows, model = low.shape
    hidden = acts[0].shape[1]
    grads = grad_shapes(hidden, model, plan)
    return pl.pallas_call(
        functools.partial(down_back_kernel, plan, len(adds)),
        out_shape=grads,
        in_specs=[SMEM] + [VMEM] * (3 + len(adds)),
        out_specs=(VMEM,) * len(grads),
        scratch_shapes=[pltpu.VMEM((hidden, model), F32)],
        compiler_params=params(),
        cost_estimate=LONG if adds else COST,
        name="down_back",
    )(spot, *acts, low, *adds)


def feed_back_kernel(plan, plus, first, spot_ref, low_ref, turned_ref, acc_ref, *refs):
    count = len(plan)
    blocks, refs = [refs[3 * n : 3 * n + 3] for n in range(count)], refs[3 * count :]
    add_ref, refs = (refs[0] if plus else None), refs[plus:]
    *outs, held_ref, dl_ref = refs
    *outs, dn_ref = outs[: len(outs) - count] + []
    dbs = refs[len(outs) + 1 : len(outs) + 1 + count]
    total = acc_ref[...]
    for n, (wd_ref, slope_ref, win_ref) in enumerate(blocks):
        half = win_ref.shape[1] // 2
        for i in range(2):
            part = slice(i * half, (i + 1) * half)
            dl = dot(low_ref[...], wd_ref[part, :], 1, 1) * slope_ref[:, part].astype(F32)
            dbs[n][0:1, part] = jnp.sum(dl, axis=0, keepdims=True)
            dl_ref[:, part] = dl.astype(BF16)
        held_ref[...] = dot(turned_ref[...], dl_ref[...], 1, 0)
        give_quarters(spot_ref, held_ref, add_ref, first + 4 * n, [(outs[i], p) for i, p in plan[n]])
        total = total + dot(dl_ref[...], win_ref[...], 1, 1)
    dn_ref[...] = total


def feed_back(spot, low, turned, acc, blocks, plan, adds=(), first=0):
    rows, model = low.shape
    hidden = blocks[0][2].shape[1]
    grads = grad_shapes(model, hidden, plan)
    flat = [one for block in blocks for one in block]
    return pl.pallas_call(
        functools.partial(feed_back_kernel, plan, len(adds), first),
        out_shape=grads
        + (jax.ShapeDtypeStruct((rows, model), F32),)
        + (jax.ShapeDtypeStruct((8, hidden), F32),) * len(blocks),
        in_specs=[SMEM] + [VMEM] * (3 + len(flat) + len(adds)),
        out_specs=(VMEM,) * (1 + len(blocks) + len(grads)),
        scratch_shapes=[pltpu.VMEM((model, hidden), F32), pltpu.VMEM((rows, hidden), BF16)],
        compiler_params=params(),
        cost_estimate=COST if adds else LONG,
        name="feed_back",
    )(spot, low, turned, acc, *flat, *adds)


def after(value, *others):
    return lax.optimization_barrier((value, *others))[0]


def swap(value, axis, size, step):
    return lax.ppermute(value, axis, [(i, i ^ step) for i in range(size)])


def add_kernel(plan, *refs):
    outs = refs[len(refs) - len(plan) :]
    for out_ref, terms in zip(outs, plan):
        total = None
        for n, place in terms:
            value = (refs[n][...] if place is None else refs[n][place]).astype(F32)
            total = value if total is None else total + value
        out_ref[...] = total.astype(BF16)


def add(sums, long=False):
    arrays, plan, shapes = [], [], []
    for terms in sums:
        row = []
        for term in terms:
            value, place = term if isinstance(term, tuple) else (term, None)
            known = [n for n, one in enumerate(arrays) if one is value]
            if not known:
                arrays.append(value)
            row.append((known[0] if known else len(arrays) - 1, place))
        value, place = arrays[row[0][0]], row[0][1]
        shape = value.shape
        if isinstance(place, int):
            shape = shape[1:]
        elif place is not None:
            shape = (place.stop - place.start, *shape[1:])
        plan.append(row)
        shapes.append(jax.ShapeDtypeStruct(shape, BF16))
    return pl.pallas_call(
        functools.partial(add_kernel, plan),
        out_shape=tuple(shapes),
        in_specs=[VMEM] * len(arrays),
        out_specs=(VMEM,) * len(shapes),
        compiler_params=params(),
        cost_estimate=LONG if long else COST,
        name="add",
    )(*arrays)


class Line:
    def __init__(self):
        self.last = None

    def __call__(self, value):
        return value if self.last is None else after(value, self.last)

    def done(self, value):
        self.last = value
        return value

    def adds(self, *sums, long=False):
        first = sums[0][0]
        value, place = first if isinstance(first, tuple) else (first, None)
        tied = self(value)
        sums = [
            [
                (tied, term[1]) if isinstance(term, tuple) and term[0] is value
                else tied if term is value
                else term
                for term in terms
            ]
            for terms in sums
        ]
        outs = add(sums, long)
        self.done(outs[0])
        return outs

    def add(self, *terms):
        return self.adds(terms)[0]


class Group:
    def __init__(self, dp, tensor):
        if dp < 8 or dp & (dp - 1):
            raise ValueError("dp size")
        self.dp, self.tensor = dp, tensor
        self.place = lax.axis_index("dp")

    def core(self, value):
        return swap(value, "tensor", self.tensor, 1)

    def across(self, value):
        return swap(value, "tensor", self.tensor, 2)

    def over(self, number, value):
        return swap(value, "dp", self.dp, 2**number)

    def rest(self, value, line):
        number = 3
        while 2**number < self.dp:
            value = line.add(value, self.over(number, value))
            number += 1
        return value


def local(
    inputs,
    lengths,
    weight_query,
    bias_query,
    weight_key,
    weight_value,
    bias_value,
    weight_out,
    bias_out,
    weight_in,
    bias_in,
    weight_down,
    bias_down,
    first_gain,
    first_shift,
    second_gain,
    second_shift,
    cotangent,
):
    group = Group(lax.axis_size("dp"), lax.axis_size("tensor"))
    core, across, over = group.core, group.across, group.over
    width = weight_query.shape[1]
    seq = lax.axis_index("tensor").reshape(1)
    spot = group.place.reshape(1)
    scalars = (lengths, seq, spot)
    line = Line()

    pack, pack_0, pack_3 = prepare_pack(
        spot, weight_query, weight_key, weight_value, weight_out, bias_query, bias_value, bias_in
    )
    line.done(pack_0)
    far_0 = across(pack_0)
    pack_twin = core(pack)
    win_0, win_3, wd_0, wd_3 = prepare_feed(line(spot), weight_in, weight_down)
    line.done(win_0)
    kept = [None] * 4
    kept[0] = attend_forward(scalars, line(inputs), [pack])
    line.done(kept[0][4])
    far_3 = across(line(pack_3))
    kept[1] = attend_forward(scalars, line(inputs), [pack_twin])
    line.done(kept[1][4])
    far_0 = line.done(line(far_0))
    far_1, far_2 = over(1, far_0), over(0, far_0)
    win_0 = across(after(win_0, far_0))
    far_3 = line.done(line(far_3))
    far_parts = [far_0, far_1, far_2, far_3]
    pack_twin = [core(one) for one in far_parts]
    kept[2] = attend_forward(scalars, line(inputs), far_parts)
    line.done(kept[2][4])
    wd_0 = across(after(wd_0, kept[2][4]))
    win_0 = line.done(line(win_0))
    win_1, win_2 = over(1, win_0), over(0, win_0)
    win_3 = across(after(win_3, win_0))
    kept[3] = attend_forward(scalars, line(inputs), pack_twin)
    line.done(kept[3][4])
    win_twin = core(after(weight_in, kept[2][4]))
    z, low, turned, rstd = first_norm(
        line(inputs),
        (bias_out, first_gain, first_shift),
        [one[4] for one in kept],
        [one[0] for one in kept],
    )
    line.done(low)
    acts, slopes = [None] * 4, [None] * 4
    acts[0], slopes[0], acts[1], slopes[1] = feed_up(
        spot, line(low), [weight_in, win_twin], [kept[0][5], kept[1][5]]
    )
    line.done(acts[0])
    wd_0 = line.done(line(wd_0))
    wd_1, wd_2 = over(1, wd_0), over(0, wd_0)
    wd_3 = across(after(wd_3, low))
    wd_twin = core(after(weight_down, kept[3][4]))
    win_far, acts[2], slopes[2] = feed_up(
        spot, line(low), [win_0, win_1, win_2, win_3], [kept[2][5]]
    )
    line.done(acts[2])
    wd_3 = line.done(line(wd_3))
    wins = [weight_in, win_twin, win_far, core(win_far)]
    wd_parts = [wd_0, wd_1, wd_2, wd_3]
    *near, feed = feed_down(spot, [line(acts[0]), acts[1]], [[weight_down], [wd_twin]])
    line.done(feed)
    wd_twin = [core(one) for one in wd_parts]
    acts[3], slopes[3] = feed_up(spot, line(low), [wins[3]], [kept[3][5]])
    line.done(acts[3])
    *far, feed = feed_down(spot, [line(acts[2]), acts[3]], [wd_parts, wd_twin], feed)
    wds = near + far
    results, grad_second, second_low, second_sums = second_norm(
        z, feed, cotangent, (first_gain, first_shift, bias_down, second_gain, second_shift)
    )
    line.done(second_low)

    def down(pair, plan, adds=()):
        grads = down_back(spot, [acts[r] for r in pair], line(second_low), plan, adds)
        line.done(grads[0])
        return grads

    db = [None] * 4

    def back(these, acc, plan, adds=(), first=0):
        blocks = [(wds[r], slopes[r], wins[r]) for r in these]
        outs = feed_back(spot, line(second_low), turned, acc, blocks, plan, adds, first)
        *grads, acc = outs[: -len(these)]
        for r, one in zip(these, outs[-len(these) :]):
            db[r] = one
        line.done(acc)
        return grads, acc

    (down_twin,) = down((3, 1), TOGETHER)
    down_twin = core(down_twin)
    (win_twin,), dn = back((3, 1), grad_second, TOGETHER)
    win_twin = core(win_twin)
    far_keep, far_send, near_keep, near_send = down((2, 0), EARLY, [down_twin])
    far_moved, near_moved = over(1, far_send), over(0, near_send)
    (win_321, win_0), dn = back((2,), dn, LATE[:1], [win_twin])
    win_321, win_0 = across(win_321), across(win_0)
    (win_near,), dn = back((0,), dn, TOGETHER[:1], [win_twin], 4)
    grad_first, first_low, first_sums = first_back(line(z), rstd, dn, first_gain)
    line.done(first_low)
    gs = [None] * 4

    def attention_back(blocks, split=False, adds=()):
        outs = attend_backward(
            spot,
            inputs,
            line(first_low),
            [db[r] for r in blocks],
            first_sums,
            second_sums,
            [kept[r][:5] for r in blocks],
            split,
            adds,
        )
        for r, one in zip(blocks, outs[-len(blocks) :]):
            gs[r] = one
        line.done(gs[blocks[-1]])
        return outs[: -len(blocks)]

    (pack_twin,) = attention_back((3, 1))
    pack_twin = core(pack_twin)

    def input_part(acc, pair):
        part = input_grad(line(acc), [gs[r] for r in pair], [kept[r][0] for r in pair])
        return line.done(part)

    down_f2, down_n1 = line.adds(
        [(far_keep, 1), (far_moved, 1)], [(near_keep, 1), (near_moved, 1)]
    )
    down_fx, down_nz = over(0, down_f2), over(1, down_n1)
    dx = input_part(grad_first, (3, 1))
    down_f0, down_0, win_s, win_1 = line.adds(
        [(far_keep, 0), (far_moved, 0), down_fx],
        [(near_keep, 0), (near_moved, 0), down_nz],
        [(win_near, slice(2, 4)), (win_321, slice(0, 2))],
        [(win_near, 1), (win_321, 2)],
        long=True,
    )
    down_y, win_x = across(down_f0), over(0, win_s)
    pack_0, pack_321 = attention_back((2,), True, [pack_twin])
    pack_321 = across(pack_321)
    (pack_near,) = attention_back((0,), False, [pack_twin])
    down_0, win_1, win_0 = line.adds(
        [down_0, down_y],
        [win_1, (win_x, 1)],
        [(win_near, 0), (win_0, 0), (win_x, 0)],
    )
    down_far, win_z = over(2, down_0), over(1, win_1)
    pack_0 = across(after(pack_0, down_0))
    dx = input_part(dx, (2, 0))
    win_0 = line.add(win_0, win_z)
    win_far = over(2, win_0)
    pack_s = line.add((pack_near, slice(2, 4)), (pack_321, slice(0, 2)))
    pack_x = over(0, pack_s)
    down_0 = group.rest(line.add(down_0, down_far), line)
    down_1, down_2 = over(1, down_0), over(0, down_0)
    down_1 = line.done(line(down_1))
    down_3 = over(0, down_1)
    pack_1, pack_0 = line.adds(
        [(pack_near, 1), (pack_321, 2), (pack_x, 1)], [(pack_near, 0), pack_0, (pack_x, 0)]
    )
    pack_z = over(1, pack_1)
    win_0 = group.rest(line.add(win_0, win_far), line)
    pack_0 = line.add(pack_0, pack_z)
    pack_far = over(2, pack_0)
    win_1, win_2 = over(1, after(win_0, pack_0)), over(0, after(win_0, pack_0))
    grad_weight_down = finish_block(line(spot), [down_0, down_1, down_2, down_3])
    line.done(grad_weight_down)
    win_2 = line.done(line(win_2))
    win_3 = over(1, win_2)
    win_1 = line.done(line(win_1))
    pack_0 = group.rest(line.add(pack_0, pack_far), line)
    pack_1, pack_2 = over(1, pack_0), over(0, pack_0)
    grad_weight_in = finish_block(line(spot), [win_0, win_1, win_2, win_3])
    line.done(grad_weight_in)
    parts = [pack_0, pack_1, pack_2, over(0, pack_1)]
    grad_q, grad_k, grad_v, grad_o, grad_bq, grad_bv, *rest = finish_pack(line(spot), parts, width)
    grad_bin, shift1, gain1, grad_bout, shift2, gain2, grad_bdown = rest
    return (
        results,
        dx,
        grad_q.T,
        grad_bq,
        grad_k.T,
        grad_v.T,
        grad_bv,
        grad_o,
        grad_bout,
        grad_weight_in,
        grad_bin,
        grad_weight_down,
        grad_bdown,
        gain1,
        shift1,
        gain2,
        shift2,
    )


def solution(mesh):
    in_specs = (
        P(("dp", "tensor"), None),
        P("dp"),
        P(None, "tensor"),
        P("tensor"),
        P(None, "tensor"),
        P(None, "tensor"),
        P("tensor"),
        P("tensor", None),
        P(),
        P(None, "tensor"),
        P("tensor"),
        P("tensor", None),
        P(),
        P(),
        P(),
        P(),
        P(),
        P(("dp", "tensor"), None),
    )
    out_specs = (
        P(("dp", "tensor"), None),
        P(("dp", "tensor"), None),
        P(None, "tensor"),
        P("tensor"),
        P(None, "tensor"),
        P(None, "tensor"),
        P("tensor"),
        P("tensor", None),
        P(),
        P(None, "tensor"),
        P("tensor"),
        P("tensor", None),
        P(),
        P(),
        P(),
        P(),
        P(),
    )
    return jax.shard_map(local, mesh=mesh, in_specs=in_specs, out_specs=out_specs, check_vma=False)
```

```python
import functools
import math

import jax
import jax.numpy as jnp
from jax import lax
from jax.experimental import pallas as pl
from jax.experimental.pallas import tpu as pltpu
from jax.sharding import PartitionSpec as P

HEAD = 64
SEQ_LEN = 512
UP_ROWS = 128
F32 = jnp.float32
BF16 = jnp.bfloat16
VMEM_LIMIT = 24 * 1024 * 1024
VMEM = pl.BlockSpec(memory_space=pltpu.VMEM)
COST = pl.CostEstimate(flops=10**9, bytes_accessed=10**9, transcendentals=0)
MIDDLE = pl.CostEstimate(flops=10**10, bytes_accessed=10**9, transcendentals=0)
LONG = pl.CostEstimate(flops=10**11, bytes_accessed=10**9, transcendentals=0)
SMEM = pl.BlockSpec(memory_space=pltpu.SMEM)
HBM = pl.BlockSpec(memory_space=pltpu.HBM)


def hbm(shape, dtype=BF16):
    return pltpu.HBM(shape, dtype)


def pinned(value):
    return pltpu.with_memory_space_constraint(value, pltpu.HBM)


def dot(left, right, left_dim, right_dim):
    return lax.dot_general(
        left, right, (((left_dim,), (right_dim,)), ((), ())), preferred_element_type=F32
    )


def params(**kwargs):
    return pltpu.CompilerParams(vmem_limit_bytes=VMEM_LIMIT, **kwargs)


def whole(shape, index=None):
    place = index or (0,) * len(shape)
    return pl.BlockSpec(shape, lambda *_: place)


def row(ref):
    return ref[...].astype(F32).reshape(1, ref.shape[0])


def pack_rows(width):
    return (4 * width + 16 + 63) // 64 * 64


def bit(spot_ref, number):
    return lax.rem(lax.div(spot_ref[0], 2**number), 2)


def window(choice, size, tile):
    return pl.ds(pl.multiple_of(choice * size, tile), size)


def head_rows(start, h):
    return pl.ds(pl.multiple_of(start + h * HEAD, HEAD), HEAD)


def quarter(spot_ref, r, size):
    first = lax.rem(bit(spot_ref, 0) + r // 2, 2)
    second = lax.rem(bit(spot_ref, 1) + r % 2, 2)
    return window(2 * first + second, size, 16)


def run(copies):
    for one in copies:
        one.start()
    for one in copies:
        one.wait()


def prepare_pack_kernel(spot_ref, q_ref, k_ref, v_ref, out_ref, bq_ref, bv_ref, bin_ref, *refs):
    full_ref, first_ref, last_ref, held_ref, extra_ref, bq, bv, bin_, sems = refs
    width = out_ref.shape[0]
    copies = [
        pltpu.make_async_copy(ref, held_ref.at[pl.ds(i * width, width), :], sems.at[i])
        for i, ref in enumerate((q_ref, k_ref, v_ref, out_ref))
    ]
    vectors = [
        pltpu.make_async_copy(ref, to, sems.at[4 + i])
        for i, (ref, to) in enumerate(((bq_ref, bq), (bv_ref, bv), (bin_ref, bin_)))
    ]
    for one in vectors + copies:
        one.start()
    extra_ref[...] = jnp.zeros_like(extra_ref)
    for one in vectors:
        one.wait()
    extra_ref[0, :width] = bq[...].astype(F32)
    extra_ref[0, 2 * width : 3 * width] = bv[...].astype(F32)
    extra_ref[1, :] = bin_[...].astype(F32)
    held_ref[4 * width :, :] = extra_ref[...].astype(BF16)
    for one in copies:
        one.wait()
    size = first_ref.shape[0]
    run(
        [
            pltpu.make_async_copy(held_ref.at[quarter(spot_ref, 0, size), :], first_ref, sems.at[0]),
            pltpu.make_async_copy(held_ref.at[quarter(spot_ref, 3, size), :], last_ref, sems.at[1]),
            pltpu.make_async_copy(held_ref, full_ref, sems.at[2]),
        ]
    )


def prepare_pack(spot, wq, wk, wv, wout, bq, bv, bin_):
    width, model = wout.shape
    rows = pack_rows(width)
    return pl.pallas_call(
        prepare_pack_kernel,
        out_shape=(hbm((rows, model)), hbm((rows // 4, model)), hbm((rows // 4, model))),
        in_specs=[SMEM] + [HBM] * 7,
        out_specs=(HBM,) * 3,
        scratch_shapes=[
            pltpu.VMEM((rows, model), BF16),
            pltpu.VMEM((rows - 4 * width, model), F32),
            pltpu.VMEM(bq.shape, BF16),
            pltpu.VMEM(bv.shape, BF16),
            pltpu.VMEM(bin_.shape, BF16),
            pltpu.SemaphoreType.DMA((7,)),
        ],
        compiler_params=params(),
        name="prepare_pack",
    )(spot, *(pinned(one) for one in (wq.T, wk.T, wv.T, wout, bq, bv, bin_)))


def prepare_feed_kernel(spot_ref, win_ref, wd_ref, *refs):
    outs, held, sems = refs[:4], refs[4:8], refs[8]
    size = outs[0].shape[0]
    loads = []
    for i in range(4):
        source = (win_ref, wd_ref)[i // 2].at[quarter(spot_ref, 3 * (i % 2), size), :]
        loads.append(pltpu.make_async_copy(source, held[i], sems.at[i]))
        loads[i].start()
    stores = []
    for i in range(4):
        loads[i].wait()
        stores.append(pltpu.make_async_copy(held[i], outs[i], sems.at[i]))
        stores[i].start()
    for one in stores:
        one.wait()


def prepare_feed(spot, win, wd):
    size, model = win.shape[0] // 4, win.shape[1]
    return pl.pallas_call(
        prepare_feed_kernel,
        out_shape=(hbm((size, model)),) * 4,
        in_specs=[SMEM, HBM, HBM],
        out_specs=(HBM,) * 4,
        scratch_shapes=[pltpu.VMEM((size, model), BF16)] * 4 + [pltpu.SemaphoreType.DMA((4,))],
        compiler_params=params(),
        name="prepare_feed",
    )(spot, pinned(win), pinned(wd))


def finish_pack_kernel(spot_ref, *refs):
    parts, (q_ref, k_ref, v_ref, out_ref), refs = refs[:4], refs[4:8], refs[8:]
    (bq_ref, bv_ref, *vectors), (held_ref, extra_ref) = refs[:-2], refs[-2:]
    size = parts[0].shape[0]
    width = q_ref.shape[0]
    for r in range(4):
        held_ref[quarter(spot_ref, r, size), :] = parts[r][...]
    for i, ref in enumerate((q_ref, k_ref, v_ref, out_ref)):
        ref[...] = held_ref[i * width : (i + 1) * width, :].astype(F32)
    extra_ref[...] = held_ref[4 * width : 4 * width + 16, :].astype(F32)
    bq_ref[...] = extra_ref[0, :width]
    bv_ref[...] = extra_ref[0, 2 * width : 3 * width]
    for i, ref in enumerate(vectors):
        ref[...] = extra_ref[1 + i, :]


def finish_pack(spot, parts, width):
    size, model = parts[0].shape
    one = jax.ShapeDtypeStruct((width, model), F32)
    vector = jax.ShapeDtypeStruct((model,), F32)
    return pl.pallas_call(
        finish_pack_kernel,
        out_shape=(one,) * 4 + (jax.ShapeDtypeStruct((width,), F32),) * 2 + (vector,) * 7,
        in_specs=[SMEM] + [VMEM] * 4,
        out_specs=(VMEM,) * 13,
        scratch_shapes=[pltpu.VMEM((4 * size, model), BF16), pltpu.VMEM((16, model), F32)],
        compiler_params=params(),
        cost_estimate=COST,
        name="finish_pack",
    )(spot, *parts)


def finish_block_kernel(spot_ref, *refs):
    for r in range(4):
        refs[4][quarter(spot_ref, r, refs[r].shape[0]), :] = refs[r][...].astype(F32)


def finish_block(spot, parts):
    size, model = parts[0].shape
    return pl.pallas_call(
        finish_block_kernel,
        out_shape=jax.ShapeDtypeStruct((4 * size, model), F32),
        in_specs=[SMEM] + [VMEM] * 4,
        out_specs=VMEM,
        compiler_params=params(),
        cost_estimate=COST,
        name="finish_block",
    )(spot, *parts)


def attend_forward_kernel(pieces, length_ref, seq_ref, spot_ref, x_ref, *refs):
    parts, refs = refs[:pieces], refs[pieces:]
    if pieces > 1:
        pack_out, *refs, pack_ref = refs
    else:
        pack_ref = parts[0]
    qkv_out, e_out, r_out, att_out, bias_out, qkv_ref, e_ref, r_ref, att_ref, sems = refs
    width = att_ref.shape[0]
    heads = width // HEAD
    if pieces == 1:
        bias_out[...] = pack_ref[4 * width : 4 * width + 16, :]
    scale = math.log2(math.e) / math.sqrt(HEAD)
    copies = []

    def store(source, target, sem):
        copies.append(pltpu.make_async_copy(source, target, sems.at[sem]))
        copies[-1].start()

    if pieces > 1:
        size = parts[0].shape[0]
        for r in range(4):
            pack_ref[quarter(spot_ref, r, size), :] = parts[r][...]
        store(pack_ref, pack_out, heads)
        bias_out[...] = pack_ref[4 * width : 4 * width + 16, :]
    bias = jnp.transpose(pack_ref[4 * width : 4 * width + 16, :].astype(F32))[: 3 * width, 0:1]
    projected = dot(pack_ref[: 3 * width, :], x_ref[...], 1, 1) + bias
    qkv_ref[...] = projected.astype(BF16)
    store(qkv_ref, qkv_out, heads + 1)
    visible = lax.broadcasted_iota(jnp.int32, (SEQ_LEN, 1), 0) < length_ref[seq_ref[0]]

    @pl.loop(0, heads, unroll=pieces > 1)
    def _(h):
        q, k, v = (qkv_ref[head_rows(i * width, h), :] for i in range(3))
        scores = jnp.where(visible, dot(k, q, 0, 0) * scale, -1e30)
        highest = jnp.max(scores, axis=0, keepdims=True)
        e = jnp.exp2(scores - highest)
        r = 1.0 / jnp.sum(e, axis=0, keepdims=True)
        low = e.astype(BF16)
        e_ref[h] = low
        pltpu.make_async_copy(e_ref.at[h], e_out.at[h], sems.at[h]).start()
        r_ref[h] = jnp.broadcast_to(r, r_ref.shape[1:])
        att_ref[head_rows(0, h), :] = (dot(v, low, 1, 0) * r).astype(BF16)

    copies.extend(
        pltpu.make_async_copy(e_ref.at[h], e_out.at[h], sems.at[h]) for h in range(heads)
    )
    store(r_ref, r_out, heads + 2)
    store(att_ref, att_out, heads + 3)
    for one in copies:
        one.wait()


def attend_forward(scalars, x, parts):
    rows, model = x.shape
    width = model // 4
    heads = width // HEAD
    pieces = len(parts)
    full = hbm((pieces * parts[0].shape[0], model))
    held = [
        hbm((3 * width, rows)),
        hbm((heads, rows, rows)),
        hbm((heads, 8, rows), F32),
        hbm((width, rows)),
    ]
    more = [full] if pieces > 1 else []
    outs = pl.pallas_call(
        functools.partial(attend_forward_kernel, pieces),
        out_shape=(*more, *held, jax.ShapeDtypeStruct((16, model), BF16)),
        in_specs=[SMEM] * 3 + [VMEM] * (1 + pieces),
        out_specs=(HBM,) * (len(more) + 4) + (VMEM,),
        scratch_shapes=[pltpu.VMEM(one.shape, one.dtype) for one in held]
        + [pltpu.SemaphoreType.DMA((heads + 4,))]
        + [pltpu.VMEM(one.shape, one.dtype) for one in more],
        compiler_params=params(),
        cost_estimate=MIDDLE,
        name="attend_forward",
    )(*scalars, x, *parts)
    return outs if more else (parts[0], *outs)


def attend_backward_kernel(count, plus, split, first, spot_ref, x_ref, bg_ref, *refs):
    dbs, (first_ref, second_ref), refs = refs[:count], refs[count : count + 2], refs[count + 2 :]
    saved, refs = refs[: 5 * count], refs[5 * count :]
    add_in, refs = refs[:plus], refs[plus:]
    outs, refs = refs[: 1 + split], refs[1 + split :]
    g_outs, refs = refs[:count], refs[count:]
    held, (extra_ref, up_ref, sems) = refs[: 7 * count], refs[7 * count : 7 * count + 3]
    factor = 1.0 / math.sqrt(HEAD)

    def move(source, target, *sem):
        copy = pltpu.make_async_copy(source, target, sems.at[sem])
        copy.start()
        return copy

    loads = []
    for n in range(count):
        pack_in, qkv_in, e_in, r_in, att_in = saved[5 * n : 5 * n + 5]
        qkv_ref, e_ref, r_ref, att_ref, wout_ref = held[7 * n : 7 * n + 5]
        width = att_ref.shape[0]
        heads = width // HEAD
        one = [
            move(pack_in.at[pl.ds(3 * width, width), :], wout_ref, n, 0),
            move(qkv_in, qkv_ref, n, 1),
            move(r_in, r_ref, n, 2),
            move(att_in, att_ref, n, 3),
        ]
        loads.append(one + [move(e_in.at[h], e_ref.at[h], n, 4 + h) for h in range(heads)])
    stores = []
    for n in range(count):
        e_in = saved[5 * n + 2]
        qkv_ref, e_ref, r_ref, att_ref, wout_ref, g_ref, held_ref = held[7 * n : 7 * n + 7]
        size = held_ref.shape[0] // 4
        extra_ref[...] = jnp.zeros_like(extra_ref)
        extra_ref[1:2, :] = dbs[n][0:1, :]
        extra_ref[2:5, :] = first_ref[0:3, :]
        extra_ref[5:8, :] = second_ref[0:3, :]
        loads[n][0].wait()
        up_ref[...] = dot(wout_ref[...], bg_ref[...], 1, 1).astype(BF16)
        for one in loads[n][1:4]:
            one.wait()

        @pl.loop(0, heads)
        def _(h):
            q, k, v = (qkv_ref[head_rows(i * width, h), :] for i in range(3))
            scaled = up_ref[head_rows(0, h), :].astype(F32) * r_ref[h, 0:1, :]
            attended = att_ref[head_rows(0, h), :].astype(F32)
            inner = jnp.sum(attended * scaled, axis=0, keepdims=True)
            do = scaled.astype(BF16)
            pltpu.make_async_copy(e_in.at[h], e_ref.at[h], sems.at[n, 4 + h]).wait()
            e = e_ref[h]
            ds = (e.astype(F32) * (dot(v, do, 0, 0) - inner)).astype(BF16)
            g_ref[head_rows(0, h), :] = (dot(k, ds, 1, 0) * factor).astype(BF16)
            g_ref[head_rows(width, h), :] = (dot(q, ds, 1, 1) * factor).astype(BF16)
            g_ref[head_rows(2 * width, h), :] = dot(do, e, 1, 1).astype(BF16)

        stores.append(move(g_ref, g_outs[n], n, 0))
        g = g_ref[...]
        extra_ref[0:1, : 3 * width] = dot(jnp.ones((8, g.shape[1]), BF16), g, 1, 1)[0:1, :]
        held_ref[4 * width :, :] = extra_ref[...].astype(BF16)
        held_ref[: 3 * width, :] = dot(g, x_ref[...], 1, 0).astype(BF16)
        held_ref[3 * width : 4 * width, :] = dot(att_ref[...], bg_ref[...], 1, 0).astype(BF16)
        for r in range(4):
            if plus:
                part = quarter(spot_ref, r, size)
                value = held_ref[part, :].astype(F32) + add_in[0][first + r].astype(F32)
                held_ref[part, :] = value.astype(BF16)
            if len(outs) == 1:
                target = outs[0].at[4 * n + r]
            else:
                target = outs[1].at[(0, 2, 0, 1)[r]] if r else outs[0]
            stores.append(
                move(held_ref.at[quarter(spot_ref, r, size), :], target, n, 4 + heads + r)
            )
    for one in stores:
        one.wait()


def attend_backward(spot, x, bg, dbs, first, second, saved, split=False, adds=()):
    rows, model = x.shape
    width = model // 4
    heads = width // HEAD
    count = len(dbs)
    full = saved[0][0].shape[0]
    more = list(adds)
    if split:
        grads = (hbm((full // 4, model)), hbm((3, full // 4, model)))
    else:
        grads = (hbm((4 * count, full // 4, model)),)
    flat = [pinned(one) for block in saved for one in block]
    return pl.pallas_call(
        functools.partial(attend_backward_kernel, count, len(more), split, 0 if split else 4),
        out_shape=grads + (hbm((3 * width, rows)),) * count,
        in_specs=[SMEM] + [VMEM] * (4 + count) + [HBM] * (5 * count) + [VMEM] * len(more),
        out_specs=(HBM,) * (len(grads) + count),
        scratch_shapes=[
            pltpu.VMEM((3 * width, rows), BF16),
            pltpu.VMEM((heads, rows, rows), BF16),
            pltpu.VMEM((heads, 8, rows), F32),
            pltpu.VMEM((width, rows), BF16),
            pltpu.VMEM((width, model), BF16),
            pltpu.VMEM((3 * width, rows), BF16),
            pltpu.VMEM((full, model), BF16),
        ]
        * count
        + [
            pltpu.VMEM((full - 4 * width, model), F32),
            pltpu.VMEM((width, rows), BF16),
            pltpu.SemaphoreType.DMA((count, 8 + heads)),
        ],
        compiler_params=params(),
        cost_estimate=COST if count > 1 else MIDDLE,
        name="attend_backward",
    )(spot, x, bg, *dbs, first, second, *flat, *more)


def input_grad_kernel(count, acc_ref, *refs):
    gs, packs, out_ref, sems = refs[:count], refs[count : 2 * count], refs[2 * count], refs[-1]
    held_g, held_w = refs[2 * count + 1 : 3 * count + 1], refs[3 * count + 1 : 4 * count + 1]
    width = held_w[0].shape[0]
    loads = []
    for i in range(count):
        loads.append(pltpu.make_async_copy(gs[i], held_g[i], sems.at[2 * i]))
        loads.append(
            pltpu.make_async_copy(packs[i].at[pl.ds(0, width), :], held_w[i], sems.at[2 * i + 1])
        )
    for one in loads:
        one.start()
    total = acc_ref[...]
    for i in range(count):
        loads[2 * i].wait()
        loads[2 * i + 1].wait()
        total = total + dot(held_g[i][...], held_w[i][...], 0, 0)
    out_ref[...] = total


def input_grad(acc, gs, packs):
    rows, model = acc.shape
    width, count = gs[0].shape[0], len(gs)
    return pl.pallas_call(
        functools.partial(input_grad_kernel, count),
        out_shape=jax.ShapeDtypeStruct((rows, model), F32),
        in_specs=[VMEM] + [HBM] * (2 * count),
        out_specs=VMEM,
        scratch_shapes=[pltpu.VMEM((width, rows), BF16)] * count
        + [pltpu.VMEM((width, model), BF16)] * count
        + [pltpu.SemaphoreType.DMA((2 * count,))],
        compiler_params=params(),
        cost_estimate=COST,
        name="input_grad",
    )(acc, *(pinned(one) for one in gs), *(pinned(one) for one in packs))


def first_norm_kernel(x_ref, bias_ref, gain_ref, shift_ref, *refs):
    atts, packs, refs = refs[:4], refs[4:8], refs[8:]
    z_ref, low_ref, turned_ref, rstd_ref = refs[:4]
    held_a, held_w, sems = refs[4], refs[5], refs[6]
    width = atts[0].shape[0]
    loads = []
    for i in range(4):
        part = pl.ds(i * width, width)
        loads.append(pltpu.make_async_copy(atts[i], held_a.at[part, :], sems.at[2 * i]))
        loads.append(
            pltpu.make_async_copy(
                packs[i].at[pl.ds(3 * width, width), :], held_w.at[part, :], sems.at[2 * i + 1]
            )
        )
    run(loads)
    branch = dot(held_a[...], held_w[...], 0, 0)
    total = x_ref[...].astype(F32) + branch + row(bias_ref)
    center = total - jnp.mean(total, axis=1, keepdims=True)
    rstd = lax.rsqrt(jnp.mean(center * center, axis=1, keepdims=True) + 1e-12)
    z = center * rstd
    z_ref[...] = z
    rstd_ref[...] = rstd
    normed = (z * row(gain_ref) + row(shift_ref)).astype(BF16)
    low_ref[...] = normed
    turned_ref[...] = jnp.transpose(normed)


def first_norm(x, vectors, atts, packs):
    rows, model = x.shape
    return pl.pallas_call(
        first_norm_kernel,
        out_shape=(
            jax.ShapeDtypeStruct((rows, model), F32),
            jax.ShapeDtypeStruct((rows, model), BF16),
            jax.ShapeDtypeStruct((model, rows), BF16),
            jax.ShapeDtypeStruct((rows, 1), F32),
        ),
        in_specs=[VMEM] * 4 + [HBM] * 8,
        out_specs=(VMEM,) * 4,
        scratch_shapes=[
            pltpu.VMEM((model, rows), BF16),
            pltpu.VMEM((model, model), BF16),
            pltpu.SemaphoreType.DMA((8,)),
        ],
        compiler_params=params(),
        cost_estimate=MIDDLE,
        name="first_norm",
    )(x, *vectors, *(pinned(one) for one in atts), *(pinned(one) for one in packs))


def second_norm_kernel(z_ref, feed_ref, c_ref, *refs):
    gain1, shift1, bias, gain2, shift2 = (row(ref) for ref in refs[:5])
    out_ref, grad_ref, low_ref, sum_ref = refs[5:]
    total = z_ref[...] * gain1 + shift1 + feed_ref[...] + bias
    center = total - jnp.mean(total, axis=1, keepdims=True)
    rstd = lax.rsqrt(jnp.mean(center * center, axis=1, keepdims=True) + 1e-12)
    z = center * rstd
    out_ref[...] = (z * gain2 + shift2).astype(BF16)
    c = c_ref[...].astype(F32)
    e = c * gain2
    grad = (
        e - jnp.mean(e, axis=1, keepdims=True) - z * jnp.mean(e * z, axis=1, keepdims=True)
    ) * rstd
    grad_ref[...] = grad
    low_ref[...] = grad.astype(BF16)

    @pl.when(pl.program_id(0) == 0)
    def _():
        sum_ref[...] = jnp.zeros_like(sum_ref)

    sum_ref[0:1, :] += jnp.sum(c, axis=0, keepdims=True)
    sum_ref[1:2, :] += jnp.sum(c * z, axis=0, keepdims=True)
    sum_ref[2:3, :] += jnp.sum(grad, axis=0, keepdims=True)


def second_norm(z, feed, c, vectors):
    rows, model = z.shape
    step = rows // 4
    block = pl.BlockSpec((step, model), lambda i: (i, 0))
    return pl.pallas_call(
        second_norm_kernel,
        grid=(4,),
        out_shape=(
            jax.ShapeDtypeStruct((rows, model), BF16),
            jax.ShapeDtypeStruct((rows, model), F32),
            jax.ShapeDtypeStruct((rows, model), BF16),
            jax.ShapeDtypeStruct((8, model), F32),
        ),
        in_specs=[block] * 3 + [VMEM] * 5,
        out_specs=(block, block, block, whole((8, model))),
        compiler_params=params(),
        cost_estimate=COST,
        name="second_norm",
    )(z, feed, c, *vectors)


def first_back_kernel(z_ref, rstd_ref, dn_ref, gain_ref, grad_ref, low_ref, sum_ref):
    z = z_ref[...]
    dn = dn_ref[...]
    f = dn * row(gain_ref)
    grad = (
        f - jnp.mean(f, axis=1, keepdims=True) - z * jnp.mean(f * z, axis=1, keepdims=True)
    ) * rstd_ref[...]
    grad_ref[...] = grad
    low_ref[...] = grad.astype(BF16)

    @pl.when(pl.program_id(0) == 0)
    def _():
        sum_ref[...] = jnp.zeros_like(sum_ref)

    sum_ref[0:1, :] += jnp.sum(dn, axis=0, keepdims=True)
    sum_ref[1:2, :] += jnp.sum(dn * z, axis=0, keepdims=True)
    sum_ref[2:3, :] += jnp.sum(grad, axis=0, keepdims=True)


def first_back(z, rstd, dn, gain):
    rows, model = z.shape
    step = rows // 4
    block = pl.BlockSpec((step, model), lambda i: (i, 0))
    return pl.pallas_call(
        first_back_kernel,
        grid=(4,),
        out_shape=(
            jax.ShapeDtypeStruct((rows, model), F32),
            jax.ShapeDtypeStruct((rows, model), BF16),
            jax.ShapeDtypeStruct((8, model), F32),
        ),
        in_specs=[block, pl.BlockSpec((step, 1), lambda i: (i, 0)), block, VMEM],
        out_specs=(block, block, whole((8, model))),
        compiler_params=params(),
        cost_estimate=COST,
        name="first_back",
    )(z, rstd, dn, gain)


def feed_up_kernel(pieces, count, spot_ref, low_ref, *refs):
    biases, parts, refs = refs[:count], refs[count : count + pieces], refs[count + pieces :]
    if pieces > count:
        win_ref, *refs = refs
        for r in range(4):
            win_ref[quarter(spot_ref, r, parts[r].shape[0]), :] = parts[r][...]
        parts = (win_ref,)
    for n in range(count):
        win_ref, act_ref, slope_ref = parts[n], refs[2 * n], refs[2 * n + 1]
        bias = biases[n][1:2, :].astype(F32)

        @pl.loop(0, low_ref.shape[0] // UP_ROWS)
        def _(i):
            rows = pl.ds(pl.multiple_of(i * UP_ROWS, UP_ROWS), UP_ROWS)
            lifted = dot(low_ref[rows, :], win_ref[...], 1, 0) + bias
            phi_big = 0.5 + 0.5 * lax.erf(lifted * math.sqrt(0.5))
            phi = jnp.exp(-0.5 * lifted * lifted) * (1.0 / math.sqrt(2.0 * math.pi))
            act_ref[rows, :] = (lifted * phi_big).astype(BF16)
            slope_ref[rows, :] = (phi_big + lifted * phi).astype(BF16)


def feed_up(spot, low, parts, biases):
    rows, model = low.shape
    hidden = parts[0].shape[1]
    count = len(biases)
    tall = [jax.ShapeDtypeStruct((model, hidden), BF16)] if len(parts) > count else []
    thin = jax.ShapeDtypeStruct((rows, hidden), BF16)
    return pl.pallas_call(
        functools.partial(feed_up_kernel, len(parts), count),
        out_shape=(*tall, *[thin] * (2 * count)),
        in_specs=[SMEM] + [VMEM] * (1 + count + len(parts)),
        out_specs=(VMEM,) * (2 * count + len(tall)),
        compiler_params=params(),
        cost_estimate=MIDDLE,
        name="feed_up",
    )(spot, low, *biases, *parts)


def feed_down_kernel(pieces, chained, spot_ref, *refs):
    acts, parts, refs = refs[:2], refs[2 : 2 + 2 * pieces], refs[2 + 2 * pieces :]
    if chained:
        acc_ref, *refs = refs
    copies = []
    if pieces > 1:
        *outs, feed_ref, first_ref, second_ref, sems = refs
        wides = (first_ref, second_ref)
        for i in range(2):
            for r, part in enumerate(parts[4 * i : 4 * i + 4]):
                wides[i][quarter(spot_ref, r, part.shape[0]), :] = part[...]
            copies.append(pltpu.make_async_copy(wides[i], outs[i], sems.at[i]))
            copies[-1].start()
    else:
        feed_ref = refs[0]
        wides = parts
    total = dot(acts[0][...], wides[0][...], 1, 0) + dot(acts[1][...], wides[1][...], 1, 0)
    feed_ref[...] = total + acc_ref[...] if chained else total
    for one in copies:
        one.wait()


def feed_down(spot, acts, parts, acc=None):
    rows, hidden = acts[0].shape
    pieces = len(parts[0])
    model = parts[0][0].shape[1]
    more = [] if acc is None else [acc]
    wide = [hbm((hidden, model))] * 2 if pieces > 1 else []
    outs = pl.pallas_call(
        functools.partial(feed_down_kernel, pieces, bool(more)),
        out_shape=(*wide, jax.ShapeDtypeStruct((rows, model), F32)),
        in_specs=[SMEM] + [VMEM] * (2 + 2 * pieces + len(more)),
        out_specs=(HBM,) * len(wide) + (VMEM,),
        scratch_shapes=[pltpu.VMEM(one.shape, one.dtype) for one in wide]
        + ([pltpu.SemaphoreType.DMA((2,))] if wide else []),
        compiler_params=params(),
        cost_estimate=LONG,
        name="feed_down",
    )(spot, *acts, *parts[0], *parts[1], *more)
    return outs if wide else (parts[0][0], parts[1][0], outs[0])


def give_quarters(spot_ref, held_ref, add_ref, first, outs):
    size = held_ref.shape[0] // 4
    for r, (ref, part) in enumerate(outs):
        value = held_ref[quarter(spot_ref, r, size), :]
        if add_ref is not None:
            value = value + add_ref[first + r].astype(F32)
        ref[part] = value.astype(BF16)


TOGETHER = [[(0, r) for r in range(4)], [(0, 4 + r) for r in range(4)]]
LATE = [[(1, 0), (0, 2), (0, 0), (0, 1)], [(2, r) for r in range(4)]]
EARLY = [[(0, 0), (1, 0), (0, 1), (1, 1)], [(2, 0), (2, 1), (3, 0), (3, 1)]]


def grad_shapes(rows, model, plan):
    places = [place for block in plan for place in block]
    return tuple(
        jax.ShapeDtypeStruct((sum(1 for one, _ in places if one == i), rows // 4, model), BF16)
        for i in range(1 + max(one for one, _ in places))
    )


def down_back_kernel(plan, plus, spot_ref, act_a, act_b, low_ref, *refs):
    add_ref, outs, held_ref = (refs[0] if plus else None), refs[plus:-1], refs[-1]
    for n, act_ref in enumerate((act_a, act_b)):
        held_ref[...] = dot(act_ref[...], low_ref[...], 0, 0)
        give_quarters(spot_ref, held_ref, add_ref, 4 * n, [(outs[i], p) for i, p in plan[n]])


def down_back(spot, acts, low, plan, adds=()):
    rows, model = low.shape
    hidden = acts[0].shape[1]
    grads = grad_shapes(hidden, model, plan)
    return pl.pallas_call(
        functools.partial(down_back_kernel, plan, len(adds)),
        out_shape=grads,
        in_specs=[SMEM] + [VMEM] * (3 + len(adds)),
        out_specs=(VMEM,) * len(grads),
        scratch_shapes=[pltpu.VMEM((hidden, model), F32)],
        compiler_params=params(),
        cost_estimate=LONG if adds else COST,
        name="down_back",
    )(spot, *acts, low, *adds)


def feed_back_kernel(plan, plus, first, spot_ref, low_ref, turned_ref, acc_ref, *refs):
    count = len(plan)
    blocks, refs = [refs[3 * n : 3 * n + 3] for n in range(count)], refs[3 * count :]
    add_ref, refs = (refs[0] if plus else None), refs[plus:]
    *outs, held_ref, dl_ref = refs
    *outs, dn_ref = outs[: len(outs) - count] + []
    dbs = refs[len(outs) + 1 : len(outs) + 1 + count]
    total = acc_ref[...]
    for n, (wd_ref, slope_ref, win_ref) in enumerate(blocks):
        half = win_ref.shape[1] // 2
        for i in range(2):
            part = slice(i * half, (i + 1) * half)
            dl = dot(low_ref[...], wd_ref[part, :], 1, 1) * slope_ref[:, part].astype(F32)
            dbs[n][0:1, part] = jnp.sum(dl, axis=0, keepdims=True)
            dl_ref[:, part] = dl.astype(BF16)
        held_ref[...] = dot(turned_ref[...], dl_ref[...], 1, 0)
        give_quarters(spot_ref, held_ref, add_ref, first + 4 * n, [(outs[i], p) for i, p in plan[n]])
        total = total + dot(dl_ref[...], win_ref[...], 1, 1)
    dn_ref[...] = total


def feed_back(spot, low, turned, acc, blocks, plan, adds=(), first=0):
    rows, model = low.shape
    hidden = blocks[0][2].shape[1]
    grads = grad_shapes(model, hidden, plan)
    flat = [one for block in blocks for one in block]
    return pl.pallas_call(
        functools.partial(feed_back_kernel, plan, len(adds), first),
        out_shape=grads
        + (jax.ShapeDtypeStruct((rows, model), F32),)
        + (jax.ShapeDtypeStruct((8, hidden), F32),) * len(blocks),
        in_specs=[SMEM] + [VMEM] * (3 + len(flat) + len(adds)),
        out_specs=(VMEM,) * (1 + len(blocks) + len(grads)),
        scratch_shapes=[pltpu.VMEM((model, hidden), F32), pltpu.VMEM((rows, hidden), BF16)],
        compiler_params=params(),
        cost_estimate=COST if adds else LONG,
        name="feed_back",
    )(spot, low, turned, acc, *flat, *adds)


def after(value, *others):
    return lax.optimization_barrier((value, *others))[0]


def swap(value, axis, size, step):
    return lax.ppermute(value, axis, [(i, i ^ step) for i in range(size)])


def add_kernel(plan, *refs):
    outs = refs[len(refs) - len(plan) :]
    for out_ref, terms in zip(outs, plan):
        total = None
        for n, place in terms:
            value = (refs[n][...] if place is None else refs[n][place]).astype(F32)
            total = value if total is None else total + value
        out_ref[...] = total.astype(BF16)


def add(sums, long=False):
    arrays, plan, shapes = [], [], []
    for terms in sums:
        row = []
        for term in terms:
            value, place = term if isinstance(term, tuple) else (term, None)
            known = [n for n, one in enumerate(arrays) if one is value]
            if not known:
                arrays.append(value)
            row.append((known[0] if known else len(arrays) - 1, place))
        value, place = arrays[row[0][0]], row[0][1]
        shape = value.shape
        if isinstance(place, int):
            shape = shape[1:]
        elif place is not None:
            shape = (place.stop - place.start, *shape[1:])
        plan.append(row)
        shapes.append(jax.ShapeDtypeStruct(shape, BF16))
    return pl.pallas_call(
        functools.partial(add_kernel, plan),
        out_shape=tuple(shapes),
        in_specs=[VMEM] * len(arrays),
        out_specs=(VMEM,) * len(shapes),
        compiler_params=params(),
        cost_estimate=LONG if long else COST,
        name="add",
    )(*arrays)


class Line:
    def __init__(self):
        self.last = None

    def __call__(self, value):
        return value if self.last is None else after(value, self.last)

    def done(self, value):
        self.last = value
        return value

    def adds(self, *sums, long=False):
        first = sums[0][0]
        value, place = first if isinstance(first, tuple) else (first, None)
        tied = self(value)
        sums = [
            [
                (tied, term[1]) if isinstance(term, tuple) and term[0] is value
                else tied if term is value
                else term
                for term in terms
            ]
            for terms in sums
        ]
        outs = add(sums, long)
        self.done(outs[0])
        return outs

    def add(self, *terms):
        return self.adds(terms)[0]


class Group:
    def __init__(self, dp, tensor):
        if dp < 8 or dp & (dp - 1):
            raise ValueError("dp size")
        self.dp, self.tensor = dp, tensor
        self.place = lax.axis_index("dp")

    def core(self, value):
        return swap(value, "tensor", self.tensor, 1)

    def across(self, value):
        return swap(value, "tensor", self.tensor, 2)

    def over(self, number, value):
        return swap(value, "dp", self.dp, 2**number)

    def rest(self, value, line):
        number = 3
        while 2**number < self.dp:
            value = line.add(value, self.over(number, value))
            number += 1
        return value


def local(
    inputs,
    lengths,
    weight_query,
    bias_query,
    weight_key,
    weight_value,
    bias_value,
    weight_out,
    bias_out,
    weight_in,
    bias_in,
    weight_down,
    bias_down,
    first_gain,
    first_shift,
    second_gain,
    second_shift,
    cotangent,
):
    group = Group(lax.axis_size("dp"), lax.axis_size("tensor"))
    core, across, over = group.core, group.across, group.over
    width = weight_query.shape[1]
    seq = lax.axis_index("tensor").reshape(1)
    spot = group.place.reshape(1)
    scalars = (lengths, seq, spot)
    line = Line()

    pack, pack_0, pack_3 = prepare_pack(
        spot, weight_query, weight_key, weight_value, weight_out, bias_query, bias_value, bias_in
    )
    line.done(pack_0)
    far_0 = across(pack_0)
    pack_twin = core(pack)
    win_0, win_3, wd_0, wd_3 = prepare_feed(line(spot), weight_in, weight_down)
    line.done(win_0)
    kept = [None] * 4
    kept[0] = attend_forward(scalars, line(inputs), [pack])
    line.done(kept[0][4])
    far_3 = across(line(pack_3))
    kept[1] = attend_forward(scalars, line(inputs), [pack_twin])
    line.done(kept[1][4])
    far_0 = line.done(line(far_0))
    far_1, far_2 = over(1, far_0), over(0, far_0)
    win_0 = across(after(win_0, far_0))
    far_3 = line.done(line(far_3))
    far_parts = [far_0, far_1, far_2, far_3]
    pack_twin = [core(one) for one in far_parts]
    kept[2] = attend_forward(scalars, line(inputs), far_parts)
    line.done(kept[2][4])
    wd_0 = across(after(wd_0, kept[2][4]))
    win_0 = line.done(line(win_0))
    win_1, win_2 = over(1, win_0), over(0, win_0)
    win_3 = across(after(win_3, win_0))
    kept[3] = attend_forward(scalars, line(inputs), pack_twin)
    line.done(kept[3][4])
    win_twin = core(after(weight_in, kept[2][4]))
    z, low, turned, rstd = first_norm(
        line(inputs),
        (bias_out, first_gain, first_shift),
        [one[4] for one in kept],
        [one[0] for one in kept],
    )
    line.done(low)
    acts, slopes = [None] * 4, [None] * 4
    acts[0], slopes[0], acts[1], slopes[1] = feed_up(
        spot, line(low), [weight_in, win_twin], [kept[0][5], kept[1][5]]
    )
    line.done(acts[0])
    wd_0 = line.done(line(wd_0))
    wd_1, wd_2 = over(1, wd_0), over(0, wd_0)
    wd_3 = across(after(wd_3, low))
    wd_twin = core(after(weight_down, kept[3][4]))
    win_far, acts[2], slopes[2] = feed_up(
        spot, line(low), [win_0, win_1, win_2, win_3], [kept[2][5]]
    )
    line.done(acts[2])
    wd_3 = line.done(line(wd_3))
    wins = [weight_in, win_twin, win_far, core(win_far)]
    wd_parts = [wd_0, wd_1, wd_2, wd_3]
    *near, feed = feed_down(spot, [line(acts[0]), acts[1]], [[weight_down], [wd_twin]])
    line.done(feed)
    wd_twin = [core(one) for one in wd_parts]
    acts[3], slopes[3] = feed_up(spot, line(low), [wins[3]], [kept[3][5]])
    line.done(acts[3])
    *far, feed = feed_down(spot, [line(acts[2]), acts[3]], [wd_parts, wd_twin], feed)
    wds = near + far
    results, grad_second, second_low, second_sums = second_norm(
        z, feed, cotangent, (first_gain, first_shift, bias_down, second_gain, second_shift)
    )
    line.done(second_low)

    def down(pair, plan, adds=()):
        grads = down_back(spot, [acts[r] for r in pair], line(second_low), plan, adds)
        line.done(grads[0])
        return grads

    db = [None] * 4

    def back(these, acc, plan, adds=(), first=0):
        blocks = [(wds[r], slopes[r], wins[r]) for r in these]
        outs = feed_back(spot, line(second_low), turned, acc, blocks, plan, adds, first)
        *grads, acc = outs[: -len(these)]
        for r, one in zip(these, outs[-len(these) :]):
            db[r] = one
        line.done(acc)
        return grads, acc

    (down_twin,) = down((3, 1), TOGETHER)
    down_twin = core(down_twin)
    (win_twin,), dn = back((3, 1), grad_second, TOGETHER)
    win_twin = core(win_twin)
    far_keep, far_send, near_keep, near_send = down((2, 0), EARLY, [down_twin])
    far_moved, near_moved = over(1, far_send), over(0, near_send)
    (win_321, win_0), dn = back((2,), dn, LATE[:1], [win_twin])
    win_321, win_0 = across(win_321), across(win_0)
    (win_near,), dn = back((0,), dn, TOGETHER[:1], [win_twin], 4)
    grad_first, first_low, first_sums = first_back(line(z), rstd, dn, first_gain)
    line.done(first_low)
    gs = [None] * 4

    def attention_back(blocks, split=False, adds=()):
        outs = attend_backward(
            spot,
            inputs,
            line(first_low),
            [db[r] for r in blocks],
            first_sums,
            second_sums,
            [kept[r][:5] for r in blocks],
            split,
            adds,
        )
        for r, one in zip(blocks, outs[-len(blocks) :]):
            gs[r] = one
        line.done(gs[blocks[-1]])
        return outs[: -len(blocks)]

    (pack_twin,) = attention_back((3, 1))
    pack_twin = core(pack_twin)

    def input_part(acc, pair):
        part = input_grad(line(acc), [gs[r] for r in pair], [kept[r][0] for r in pair])
        return line.done(part)

    down_f2, down_n1 = line.adds(
        [(far_keep, 1), (far_moved, 1)], [(near_keep, 1), (near_moved, 1)]
    )
    down_fx, down_nz = over(0, down_f2), over(1, down_n1)
    dx = input_part(grad_first, (3, 1))
    down_f0, down_0, win_s, win_1 = line.adds(
        [(far_keep, 0), (far_moved, 0), down_fx],
        [(near_keep, 0), (near_moved, 0), down_nz],
        [(win_near, slice(2, 4)), (win_321, slice(0, 2))],
        [(win_near, 1), (win_321, 2)],
        long=True,
    )
    down_y, win_x = across(down_f0), over(0, win_s)
    pack_0, pack_321 = attention_back((2,), True, [pack_twin])
    pack_321 = across(pack_321)
    (pack_near,) = attention_back((0,), False, [pack_twin])
    down_0, win_1, win_0 = line.adds(
        [down_0, down_y],
        [win_1, (win_x, 1)],
        [(win_near, 0), (win_0, 0), (win_x, 0)],
    )
    down_far, win_z = over(2, down_0), over(1, win_1)
    pack_0 = across(after(pack_0, down_0))
    dx = input_part(dx, (2, 0))
    win_0 = line.add(win_0, win_z)
    win_far = over(2, win_0)
    pack_s = line.add((pack_near, slice(2, 4)), (pack_321, slice(0, 2)))
    pack_x = over(0, pack_s)
    down_0 = group.rest(line.add(down_0, down_far), line)
    down_1, down_2 = over(1, down_0), over(0, down_0)
    down_1 = line.done(line(down_1))
    down_3 = over(0, down_1)
    pack_1, pack_0 = line.adds(
        [(pack_near, 1), (pack_321, 2), (pack_x, 1)], [(pack_near, 0), pack_0, (pack_x, 0)]
    )
    pack_z = over(1, pack_1)
    win_0 = group.rest(line.add(win_0, win_far), line)
    pack_0 = line.add(pack_0, pack_z)
    pack_far = over(2, pack_0)
    win_1, win_2 = over(1, after(win_0, pack_0)), over(0, after(win_0, pack_0))
    grad_weight_down = finish_block(line(spot), [down_0, down_1, down_2, down_3])
    line.done(grad_weight_down)
    win_2 = line.done(line(win_2))
    win_3 = over(1, win_2)
    win_1 = line.done(line(win_1))
    pack_0 = group.rest(line.add(pack_0, pack_far), line)
    pack_1, pack_2 = over(1, pack_0), over(0, pack_0)
    grad_weight_in = finish_block(line(spot), [win_0, win_1, win_2, win_3])
    line.done(grad_weight_in)
    parts = [pack_0, pack_1, pack_2, over(0, pack_1)]
    grad_q, grad_k, grad_v, grad_o, grad_bq, grad_bv, *rest = finish_pack(line(spot), parts, width)
    grad_bin, shift1, gain1, grad_bout, shift2, gain2, grad_bdown = rest
    return (
        results,
        dx,
        grad_q.T,
        grad_bq,
        grad_k.T,
        grad_v.T,
        grad_bv,
        grad_o,
        grad_bout,
        grad_weight_in,
        grad_bin,
        grad_weight_down,
        grad_bdown,
        gain1,
        shift1,
        gain2,
        shift2,
    )


def solution(mesh):
    in_specs = (
        P(("dp", "tensor"), None),
        P("dp"),
        P(None, "tensor"),
        P("tensor"),
        P(None, "tensor"),
        P(None, "tensor"),
        P("tensor"),
        P("tensor", None),
        P(),
        P(None, "tensor"),
        P("tensor"),
        P("tensor", None),
        P(),
        P(),
        P(),
        P(),
        P(),
        P(("dp", "tensor"), None),
    )
    out_specs = (
        P(("dp", "tensor"), None),
        P(("dp", "tensor"), None),
        P(None, "tensor"),
        P("tensor"),
        P(None, "tensor"),
        P(None, "tensor"),
        P("tensor"),
        P("tensor", None),
        P(),
        P(None, "tensor"),
        P("tensor"),
        P("tensor", None),
        P(),
        P(),
        P(),
        P(),
        P(),
    )
    return jax.shard_map(local, mesh=mesh, in_specs=in_specs, out_specs=out_specs, check_vma=False)
```
